32 devices in a mesh: seq: 8 (over y, x, core), fsdp: 4 (over z).
Axes of the slice: x: 2, y: 2, z: 4, core: 2. Of those that a mesh axis runs over, the one named last changes fastest.
Arguments:
- inputs: bfloat16 [4, 1024, 1536], P('fsdp', 'seq'), may hold values from -6 to 6
- cotangent: bfloat16 [4, 1024, 1536], P('fsdp', 'seq'), may hold values from -6 to 6
- mix_weight: float32 [2, 1536, 6144], P(None, ('seq', 'fsdp')), may hold values from -0.15625 to 0.15625
- mix_first: float32 [2, 1536, 6144], P(None, ('seq', 'fsdp')), may hold values from -40 to 40
- mix_second: float32 [2, 1536, 6144], P(None, ('seq', 'fsdp')), may hold values from 215.57895 to 862.3158
- feed_weight: float32 [2, 1536, 13824], P(None, ('seq', 'fsdp')), may hold values from -0.15625 to 0.15625
- feed_first: float32 [2, 1536, 13824], P(None, ('seq', 'fsdp')), may hold values from -20 to 20
- feed_second: float32 [2, 1536, 13824], P(None, ('seq', 'fsdp')), may hold values from 53.894737 to 215.57895
- down_weight: float32 [2, 6912, 1536], P(None, ('seq', 'fsdp')), may hold values from -0.078125 to 0.078125
- down_first: float32 [2, 6912, 1536], P(None, ('seq', 'fsdp')), may hold values from -20 to 20
- down_second: float32 [2, 6912, 1536], P(None, ('seq', 'fsdp')), may hold values from 53.894737 to 215.57895
- gain_weight: float32 [2, 2, 1536], P(None, None, ('seq', 'fsdp')), may hold values from 0.5 to 1.5
- gain_first: float32 [2, 2, 1536], P(None, None, ('seq', 'fsdp')), may hold values from -64 to 64
- gain_second: float32 [2, 2, 1536], P(None, None, ('seq', 'fsdp')), may hold values from 485.05264 to 1940.2106
- tap_weight: float32 [2, 3, 1536], P(None, None, ('seq', 'fsdp')), may hold values from -3.5 to 3.5
- tap_first: float32 [2, 3, 1536], P(None, None, ('seq', 'fsdp')), may hold values from -40 to 40
- tap_second: float32 [2, 3, 1536], P(None, None, ('seq', 'fsdp')), may hold values from 215.57895 to 862.3158
Outputs:
- outputs: bfloat16 [4, 1024, 1536], P('fsdp', 'seq')
- input_grad: float32 [4, 1024, 1536], P('fsdp', 'seq')
- mix_first_new: float32 [2, 1536, 6144], P(None, ('seq', 'fsdp'))
- mix_second_new: float32 [2, 1536, 6144], P(None, ('seq', 'fsdp'))
- mix_weight_new: float32 [2, 1536, 6144], P(None, ('seq', 'fsdp'))
- feed_first_new: float32 [2, 1536, 13824], P(None, ('seq', 'fsdp'))
- feed_second_new: float32 [2, 1536, 13824], P(None, ('seq', 'fsdp'))
- feed_weight_new: float32 [2, 1536, 13824], P(None, ('seq', 'fsdp'))
- down_first_new: float32 [2, 6912, 1536], P(None, ('seq', 'fsdp'))
- down_second_new: float32 [2, 6912, 1536], P(None, ('seq', 'fsdp'))
- down_weight_new: float32 [2, 6912, 1536], P(None, ('seq', 'fsdp'))
- gain_first_new: float32 [2, 2, 1536], P(None, None, ('seq', 'fsdp'))
- gain_second_new: float32 [2, 2, 1536], P(None, None, ('seq', 'fsdp'))
- gain_weight_new: float32 [2, 2, 1536], P(None, None, ('seq', 'fsdp'))
- tap_first_new: float32 [2, 3, 1536], P(None, None, ('seq', 'fsdp'))
- tap_second_new: float32 [2, 3, 1536], P(None, None, ('seq', 'fsdp'))
- tap_weight_new: float32 [2, 3, 1536], P(None, None, ('seq', 'fsdp'))
The draws below stay inside these ranges and needn't reach their ends.
All inputs are finite; a program needn't handle non-finite values.
Results may differ from the reference program's by a relative error of at most 0.019.
The reference program's roundings to bfloat16 on the way count: a program that leaves them out, or rounds other values in their place, can miss the bound.
Values may be sent and summed in bfloat16 or wider, within the bound.
No kernel may reach another device: no remote copies, remote signals or barrier semaphores. Data moves between devices by JAX's collectives and lax.ppermute only.
A program may use at most 640 MiB of HBM per device.

```python
import math
import jax
import jax.numpy as jnp
from jax import lax

D = 1536
FF = 6912
LAYERS = 2
STEP = 10
LENGTH = 1024
SEQS = 4
TOKENS = 4096


def spiked(drawn, own_key, source, target, blocks, factor):
    owner, partner = [(jnp.arange(drawn.shape[dim]) // (drawn.shape[dim] // blocks)).reshape([-1 if axis == dim else 1 for axis in range(drawn.ndim)]) for dim in (source, target)]
    chosen = jax.random.permutation(own_key, blocks)[partner]
    strong = (owner == chosen) | (owner == (partner + blocks // 2) % blocks)
    return jnp.where(strong, factor * drawn, drawn)


def steps_of(own_key, shape, pieces, smallest, largest):
    gain = 1.0
    for position, shards_of in pieces:
        draws = jax.random.uniform(jax.random.fold_in(jax.random.fold_in(own_key, 6), position), (shards_of,), jnp.float32, smallest / len(pieces), largest / len(pieces))
        gain = gain * jnp.repeat(jnp.exp(draws), shape[position] // shards_of).reshape((-1,) + (1,) * (len(shape) - 1 - position))
    return gain


def bell_draw(own_key, extent, scale, most, pieces=(), held_as=jnp.bfloat16):
    array = jax.random.normal(own_key, extent, jnp.float32) * scale
    if len(pieces) > 0:
        array = steps_of(own_key, extent, pieces, -0.22, 0.18) * array
    return jnp.clip(array, min=-most, max=most).astype(held_as)


def heavy_noise(own_key, dims, scale, limit, split, heavy, dtype=jnp.bfloat16):
    drawn = scale * jax.random.normal(own_key, dims, jnp.float32)
    if split:
        drawn = drawn * steps_of(own_key, dims, split, -0.22, 0.18)
    return jnp.clip(spiked(drawn, jax.random.fold_in(own_key, 3), *heavy), -limit, limit).astype(dtype)


def setup_inputs(seed: int = 0) -> dict:
    arg_keys = jax.random.split(jax.random.key(seed), 18)
    return {
        "inputs": bell_draw(arg_keys[0], (SEQS, LENGTH, D), 1.0, 6.0, ((0, 4), (1, 8))),
        "cotangent": heavy_noise(arg_keys[1], (SEQS, LENGTH, D), 1.0, 6.0, ((0, 4), (1, 8)), (1, 2, 8, 2.0)),
        "mix_weight": bell_draw(arg_keys[2], (LAYERS, D, 4 * D), D ** -0.5, 0.15625, ((1, 32),), jnp.float32),
        "mix_first": bell_draw(arg_keys[3], (LAYERS, D, 4 * D), (TOKENS ** 0.5 / 9), 40.0, ((1, 32),), jnp.float32),
        "mix_second": jnp.clip(jnp.exp(math.log(862.3158) - 1.3862944 * jax.random.uniform(arg_keys[4], (LAYERS, D, 4 * D), jnp.float32) ** steps_of(arg_keys[4], (LAYERS, D, 4 * D), ((1, 32),), -0.2, 0.2)), 215.57895, 862.3158),
        "feed_weight": bell_draw(arg_keys[5], (LAYERS, D, 2 * FF), D ** -0.5, 0.15625, ((1, 32),), jnp.float32),
        "feed_first": bell_draw(arg_keys[6], (LAYERS, D, 2 * FF), (TOKENS ** 0.5 / 18), 20.0, ((1, 32),), jnp.float32),
        "feed_second": jnp.clip(jnp.exp(math.log(215.57895) - 1.3862944 * jax.random.uniform(arg_keys[7], (LAYERS, D, 2 * FF), jnp.float32) ** steps_of(arg_keys[7], (LAYERS, D, 2 * FF), ((1, 32),), -0.2, 0.2)), 53.894737, 215.57895),
        "down_weight": bell_draw(arg_keys[8], (LAYERS, FF, D), FF ** -0.5, 0.078125, ((1, 32),), jnp.float32),
        "down_first": bell_draw(arg_keys[9], (LAYERS, FF, D), (TOKENS ** 0.5 / 18), 20.0, ((1, 32),), jnp.float32),
        "down_second": jnp.clip(jnp.exp(math.log(215.57895) - 1.3862944 * jax.random.uniform(arg_keys[10], (LAYERS, FF, D), jnp.float32) ** steps_of(arg_keys[10], (LAYERS, FF, D), ((1, 32),), -0.2, 0.2)), 53.894737, 215.57895),
        "gain_weight": jnp.clip(1.0 + 0.1 * jax.random.normal(arg_keys[11], (LAYERS, 2, D), jnp.float32), 0.5, 1.5),
        "gain_first": bell_draw(arg_keys[12], (LAYERS, 2, D), (TOKENS ** 0.5 / 6), 64.0, ((2, 32),), jnp.float32),
        "gain_second": jnp.clip(jnp.exp(math.log(1940.2106) - 1.3862944 * jax.random.uniform(arg_keys[13], (LAYERS, 2, D), jnp.float32) ** steps_of(arg_keys[13], (LAYERS, 2, D), ((2, 32),), -0.2, 0.2)), 485.05264, 1940.2106),
        "tap_weight": bell_draw(arg_keys[14], (LAYERS, 3, D), 3 ** -0.5, 3.5, ((2, 32),), jnp.float32),
        "tap_first": bell_draw(arg_keys[15], (LAYERS, 3, D), (TOKENS ** 0.5 / 9), 40.0, ((2, 32),), jnp.float32),
        "tap_second": jnp.clip(jnp.exp(math.log(862.3158) - 1.3862944 * jax.random.uniform(arg_keys[16], (LAYERS, 3, D), jnp.float32) ** steps_of(arg_keys[16], (LAYERS, 3, D), ((2, 32),), -0.2, 0.2)), 215.57895, 862.3158),
    }


@jax.custom_vjp
def low(v):
    return lax.optimization_barrier(v.astype(jnp.bfloat16)).astype(jnp.float32)

@jax.custom_vjp
def low_back(v):
    return v

def low_keep(v):
    return (low(v), None)

def low_pass(kept, grad):
    return (grad,)

def back_keep(v):
    return (v, None)

def back_low(kept, grad):
    return (low(grad),)
low.defvjp(low_keep, low_pass)
low_back.defvjp(back_keep, back_low)
eps_norm = 1e-05
eps_adam = 1e-08
beta_one = 0.9
beta_two = 0.95
rate_matrix = 0.05
rate_vector = 0.6
decay_matrix = 0.1

def matmul(left, right):
    return jnp.dot(left, right, precision=lax.Precision.HIGHEST, preferred_element_type=jnp.float32)

def rms_norm(values, gain_row):
    row_scale = lax.rsqrt(lax.optimization_barrier(jnp.mean(values * values, axis=-1, keepdims=True)) + eps_norm)
    return values * row_scale * gain_row

def block(stream, mix_matrix, feed_matrix, down_matrix, gain_rows, tap_rows):
    features = stream.shape[-1]
    tokens_here = stream.shape[0]
    normed = low(rms_norm(stream, gain_rows[0]))
    projected = low_back(matmul(normed, mix_matrix[:, :3 * features]))
    b_part = projected[:, :features]
    c_part = projected[:, features:2 * features]
    x_part = projected[:, 2 * features:]
    gated = low(b_part * x_part)
    padded = jnp.concatenate([jnp.zeros((2, features), jnp.float32), gated], axis=0)
    conv_out = tap_rows[0] * padded[:tokens_here] + tap_rows[1] * padded[1:tokens_here + 1] + tap_rows[2] * padded[2:]
    mixed = low(c_part * conv_out)
    branch = low_back(matmul(mixed, mix_matrix[:, 3 * features:]))
    middle = stream + branch
    normed_two = low(rms_norm(middle, gain_rows[1]))
    gate_up = low_back(matmul(normed_two, feed_matrix))
    half_width = feed_matrix.shape[1] // 2
    hidden = low(jax.nn.silu(gate_up[:, :half_width]) * gate_up[:, half_width:])
    down_out = low_back(matmul(hidden, down_matrix))
    return middle + down_out

def forward(sequence, params):
    mix_all, feed_all, down_all, gain_all, tap_all = params
    stream = sequence
    for layer_index in range(LAYERS):
        stream = block(stream, low(mix_all[layer_index]), low(feed_all[layer_index]), low(down_all[layer_index]), low(gain_all[layer_index]), low(tap_all[layer_index]))
    return stream

def adam_update(weight, first, second, gradient, rate, decay):
    first_new = beta_one * first + (1.0 - beta_one) * gradient
    second_new = beta_two * second + (1.0 - beta_two) * gradient * gradient
    first_hat = first_new / (1.0 - beta_one ** STEP)
    second_hat = second_new / (1.0 - beta_two ** STEP)
    weight_new = weight - rate * (first_hat / (jnp.sqrt(second_hat) + eps_adam) + decay * weight)
    return (first_new, second_new, weight_new)

def add_arrays(first_tree, second_tree):
    return jax.tree.map(jnp.add, first_tree, second_tree)

def reference(inputs, cotangent, mix_weight, mix_first, mix_second, feed_weight, feed_first, feed_second, down_weight, down_first, down_second, gain_weight, gain_first, gain_second, tap_weight, tap_first, tap_second):
    params = (mix_weight, feed_weight, down_weight, gain_weight, tap_weight)
    start = jax.tree.map(jnp.zeros_like, params)

    def one_sequence(running, seq_pair):
        sequence, back_flow = seq_pair
        result, pull = jax.vjp(forward, sequence.astype(jnp.float32), params)
        seq_grad, param_grads = pull(back_flow.astype(jnp.float32))
        return (add_arrays(running, param_grads), (result.astype(jnp.bfloat16), seq_grad))
    grads, (outputs, input_grad) = lax.scan(one_sequence, start, (inputs, cotangent))
    mix_new = adam_update(mix_weight, mix_first, mix_second, grads[0], rate_matrix, decay_matrix)
    feed_new = adam_update(feed_weight, feed_first, feed_second, grads[1], rate_matrix, decay_matrix)
    down_new = adam_update(down_weight, down_first, down_second, grads[2], rate_matrix, decay_matrix)
    gain_new = adam_update(gain_weight, gain_first, gain_second, grads[3], rate_vector, 0.0)
    tap_new = adam_update(tap_weight, tap_first, tap_second, grads[4], rate_vector, 0.0)
    return (outputs, input_grad, mix_new[0], mix_new[1], mix_new[2], feed_new[0], feed_new[1], feed_new[2], down_new[0], down_new[1], down_new[2], gain_new[0], gain_new[1], gain_new[2], tap_new[0], tap_new[1], tap_new[2])
```

```python
import jax
import jax.numpy as jnp
from jax import lax
from jax.experimental import pallas as pl
from jax.experimental.pallas import tpu as pltpu
from jax.sharding import PartitionSpec as P

LAYERS = 2
STEP = 10

eps_norm = 1e-05
eps_adam = 1e-08
beta_one = 0.9
beta_two = 0.95
rate_matrix = 0.05
rate_vector = 0.6
decay_matrix = 0.1

low = jnp.bfloat16


def dot(left, right, sides=((1,), (0,))):
    return lax.dot_general(left, right, (sides, ((), ())), preferred_element_type=jnp.float32)


nt = ((1,), (1,))
tn = ((0,), (0,))


def seq_order():
    count = lax.axis_size("seq")
    return list(range(0, count, 2)) + list(range(1, count, 2))


def seq_swap(array, by):
    count = lax.axis_size("seq")
    return lax.ppermute(array, "seq", [(i, i ^ by) for i in range(count)])


def send_seq(array):
    return [array] + [seq_swap(array, by) for by in range(2, lax.axis_size("seq"), 2)]


def fsdp_shift(array, by):
    count = lax.axis_size("fsdp")
    return lax.ppermute(array, "fsdp", [(i, (i + by) % count) for i in range(count)])


def gather_fsdp(array):
    count = lax.axis_size("fsdp")
    return [array] + [fsdp_shift(array, -by) for by in range(1, count)]


def small_scatter_seq(parts):
    half = parts.shape[0] // 2
    total = parts[:half] + seq_swap(parts[half:], 1)
    for i in range(1, half):
        total = total.at[0].add(seq_swap(total[i], 2 * i))
    return total[0]


def small_scatter_fsdp(parts):
    total = parts[0]
    for by in range(1, parts.shape[0]):
        total = total + fsdp_shift(parts[by], by)
    return total


def stack_pairs(blocks, earlier=(), carried=()):
    def body(*refs):
        for i in range(len(blocks)):
            refs[-1][i] = refs[i][...]

    shape = (len(blocks),) + blocks[0].shape
    even, *rest = plain_call(
        body, [shaped(shape, blocks[0].dtype)], earlier=earlier, carried=carried
    )(*blocks)
    return even, seq_swap(even, 1), *rest


def pad_last(array, width):
    return jnp.pad(array, [(0, 0)] * (array.ndim - 1) + [(0, width - array.shape[-1])])


def place_of(axis):
    return lax.axis_index(axis).astype(jnp.int32).reshape(1)


scalar = pl.BlockSpec(memory_space=pltpu.SMEM)
held = pl.BlockSpec(memory_space=pltpu.VMEM)


def shaped(shape, kind=jnp.float32):
    return jax.ShapeDtypeStruct(shape, kind)


class Order:
    mark = None


mark_shape = jax.ShapeDtypeStruct((8, 128), jnp.float32)
anywhere = pl.BlockSpec(memory_space=pl.ANY)


def ordered_call(body, operands, in_specs, out_specs, out_shape, aliases, scratch, grid, cost):
    given, made = len(operands), len(out_shape)

    def marked(*refs):
        body(*refs[:given], *refs[given + 1 : given + 1 + made], *refs[given + 2 + made :])

    outs = pl.pallas_call(
        marked,
        in_specs=list(in_specs) + [anywhere],
        out_specs=list(out_specs) + [anywhere],
        out_shape=list(out_shape) + [mark_shape],
        scratch_shapes=list(scratch),
        input_output_aliases=aliases,
        compiler_params=pltpu.CompilerParams(vmem_limit_bytes=56 * 1024 * 1024),
        cost_estimate=pl.CostEstimate(
            flops=cost[0], bytes_accessed=cost[1], transcendentals=0
        ),
        **grid,
    )(*operands, Order.mark)
    Order.mark = outs[-1]
    return outs[:-1]


def kernel_call(
    body, grid, in_specs, out_specs, out_shape, aliases=None, scratch=(), cost=(0, 0)
):
    single = not isinstance(out_shape, list)

    def run(*operands):
        outs = ordered_call(
            body,
            operands,
            in_specs,
            [out_specs] if single else out_specs,
            [out_shape] if single else out_shape,
            aliases or {},
            scratch,
            dict(grid=grid),
            cost,
        )
        return outs[0] if single else outs

    return run


def plain_call(
    body, out_shape, scalars=0, scratch=(), earlier=(), carried=(), cost=(0, 0)
):
    def run(*operands):
        given, made, more = len(operands), len(out_shape), len(earlier) + len(carried)

        def rest(*refs):
            outs = refs[given + more :]
            body(*refs[:given], *outs[:made], *outs[made + len(carried) :])

        first = given + len(earlier)
        return ordered_call(
            rest,
            (*operands, *earlier, *carried),
            [scalar] * scalars + [held] * (given - scalars) + [anywhere] * more,
            [held] * made + [anywhere] * len(carried),
            [*out_shape, *(jax.ShapeDtypeStruct(x.shape, x.dtype) for x in carried)],
            {first + i: made + i for i in range(len(carried))},
            scratch,
            {},
            cost,
        )

    return run


def whole(shape):
    return pl.BlockSpec(shape, lambda i: (0,) * len(shape))


def pack_mix(mix_weight, layer, wide):
    seqs = lax.axis_size("seq")
    rows, columns = mix_weight.shape[1:]
    features = columns // 4
    chunk = features // seqs
    outer = features // (3 * wide)

    def body(place, weight, out):
        for s in range(seqs):
            slot = lax.bitwise_xor(place[0], jnp.int32(s))
            for g in range(3):
                start = g * features + s * chunk
                piece = weight[0, :, start : start + chunk].astype(low)
                if wide > chunk:
                    piece = jnp.concatenate([piece, jnp.zeros((rows, wide - chunk), low)], axis=1)
                out[slot, :, g * wide : (g + 1) * wide] = piece
        for i in range(outer):
            start = 3 * features + i * 3 * wide
            out[seqs + i] = weight[0, :, start : start + 3 * wide].astype(low)

    shape = (seqs + outer, rows, 3 * wide)
    return kernel_call(
        body,
        (1,),
        [scalar, pl.BlockSpec((1, rows, columns), lambda i: (layer, 0, 0))],
        whole(shape),
        jax.ShapeDtypeStruct(shape, low),
    )(place_of("seq"), mix_weight)


def assemble_mix(pieces, wide, features):
    seqs, rings = lax.axis_size("seq"), lax.axis_size("fsdp")
    outer, rows, _ = pieces[0].shape
    outer = outer - seqs
    rotated = isinstance(pieces, list)
    pieces = pieces if rotated else [pieces]

    def body(place_seq, place_fsdp, *refs):
        inner_out, outer_out = refs[-2:]
        refs = refs if rotated else [refs[0].at[j] for j in range(rings)]
        for j in range(rings):
            f = lax.rem(place_fsdp[0] + j, rings) if rotated else j
            for s in range(seqs):
                inner_out[lax.bitwise_xor(place_seq[0], jnp.int32(s)), f] = refs[j][s]
            for i in range(outer):
                outer_out[f, :, i * 3 * wide : (i + 1) * 3 * wide] = refs[j][seqs + i]

    inner_shape = (seqs, rings, rows, 3 * wide)
    outer_shape = (rings, rows, features)
    inner, out = plain_call(
        body, [shaped(inner_shape, low), shaped(outer_shape, low)], scalars=2
    )(place_of("seq"), place_of("fsdp"), *pieces)
    return inner.reshape(features, 3 * wide), out.reshape(rings * rows, features)


def swap_mix(packed):
    seqs = lax.axis_size("seq")
    return [packed[:1]] + [seq_swap(packed[by : by + 1], by) for by in range(1, seqs)]


def join_mix(parts, packed):
    seqs = len(parts)

    def body(*refs):
        out = refs[-1]
        for s in range(seqs):
            out[s] = refs[s][0]
        out[seqs:] = refs[seqs][seqs:]

    return plain_call(body, [shaped(packed.shape, low)])(*parts, packed)[0]


def tall_of(block):
    step = 128 // min(lax.axis_size("seq"), 128)
    return -(-block // step) * step


def pack_feed(feed_weight, layer):
    seqs, rings = lax.axis_size("seq"), lax.axis_size("fsdp")
    rows, columns = feed_weight.shape[1:]
    half = columns // 2
    block = half // (seqs * rings)
    tall = tall_of(block)

    def body(place, weight, out):
        for f in range(rings):
            slot = lax.rem(f - place[0] + rings, rings)
            for g in range(2):
                for s in range(seqs):
                    start = g * half + (s * rings + f) * block
                    piece = weight[0, :, start : start + block].astype(low)
                    if tall > block:
                        piece = jnp.concatenate(
                            [piece, jnp.zeros((rows, tall - block), low)], axis=1
                        )
                    to = (g * seqs + s) * tall
                    out[slot, :, to : to + tall] = piece

    shape = (rings, rows, 2 * seqs * tall)
    return kernel_call(
        body,
        (1,),
        [scalar, pl.BlockSpec((1, rows, columns), lambda i: (layer, 0, 0))],
        whole(shape),
        jax.ShapeDtypeStruct(shape, low),
    )(place_of("fsdp"), feed_weight)


def assemble_feed(pieces):
    rings = len(pieces)

    def body(place, *refs):
        out = refs[rings]
        for j in range(rings):
            out[lax.rem(place[0] - j + rings, rings)] = refs[j][0]

    shape = (rings,) + pieces[0].shape[1:]
    return kernel_call(
        body,
        (1,),
        [scalar] + [whole(piece.shape) for piece in pieces],
        whole(shape),
        jax.ShapeDtypeStruct(shape, low),
    )(place_of("fsdp"), *pieces)


def swap_feed(packed):
    rings = lax.axis_size("fsdp")
    return [packed[:1]] + [fsdp_shift(packed[by : by + 1], by) for by in range(1, rings)]


def gather_rows(part):
    return lax.all_gather(part.reshape(-1, part.shape[-1]), "seq", axis=0, tiled=True)


def pack_down(down_weight, layer):
    block = down_weight.shape[1]
    return jnp.pad(down_weight[layer].astype(low), ((0, tall_of(block) - block), (0, 0)))


def adam_kernel(load, scalars, grads, state, layer, previous, scratch=()):
    weight = state[0]
    rows, columns = weight.shape[1:]
    tile = 16 if rows % 16 == 0 else rows
    width = 768
    specs = [pl.BlockSpec((tile, grad.shape[-1]), lambda i: (i, 0)) for grad in grads]
    part = pl.BlockSpec((1, tile, columns), lambda i: (layer, i, 0))
    kept = 0 if previous is None else 3
    before = len(scalars) + len(grads)

    def body(*refs):
        weight, first, second = refs[before : before + 3]
        weight_out, first_out, second_out, total = refs[before + 3 + kept : before + 7 + kept]
        load(refs[: len(scalars)], refs[len(scalars) : before], refs[before + 7 + kept :], total)
        for start in range(0, columns, width):
            at = slice(start, start + width)
            gradient = total[:, at]
            old = weight[0, :, at]
            first_new = beta_one * first[0, :, at] + (1.0 - beta_one) * gradient
            second_new = beta_two * second[0, :, at] + (1.0 - beta_two) * gradient * gradient
            first_hat = first_new / (1.0 - beta_one**STEP)
            second_hat = second_new / (1.0 - beta_two**STEP)
            step = first_hat / (jnp.sqrt(second_hat) + eps_adam) + decay_matrix * old
            first_out[0, :, at] = first_new
            second_out[0, :, at] = second_new
            weight_out[0, :, at] = old - rate_matrix * step

    return kernel_call(
        body,
        (rows // tile,),
        [scalar] * len(scalars)
        + specs
        + [part] * 3
        + [anywhere] * kept,
        [part] * 3,
        [shaped(weight.shape)] * 3,
        aliases={before + 3 + i: i for i in range(kept)},
        scratch=[pltpu.VMEM((tile, columns), jnp.float32), *(make(tile) for make in scratch)],
        cost=(0, 26 * rows * columns),
    )(*scalars, *grads, *state, *(previous or ()))


def mix_reduce(pieces):
    seqs, rings = lax.axis_size("seq"), lax.axis_size("fsdp")
    count, rows, width = pieces[0].shape
    outer = count - seqs

    def body(place, *refs):
        inner_out, outer_out = refs[rings:]
        for s in range(seqs):
            total = refs[0][s].astype(jnp.float32)
            for j in range(1, rings):
                total = total + refs[j][s].astype(jnp.float32)
            inner_out[lax.bitwise_xor(place[0], jnp.int32(s))] = total.astype(low)
        for i in range(outer):
            total = refs[0][seqs + i].astype(jnp.float32)
            for j in range(1, rings):
                total = total + refs[j][seqs + i].astype(jnp.float32)
            outer_out[:, i * width : (i + 1) * width] = total

    inner, last = plain_call(
        body,
        [shaped((seqs, rows, width), low), shaped((rows, outer * width))],
        scalars=1,
    )(place_of("seq"), *pieces)
    return [inner[0]] + [seq_swap(inner[j], j) for j in range(1, seqs)] + [last]


def mix_adam(grads, state, layer, previous, wide):
    seqs = lax.axis_size("seq")
    features = state[0].shape[2] // 4
    chunk = features // seqs

    def load(scalars, grads, scratch, total):
        for s in range(seqs):
            scratch[0][lax.bitwise_xor(scalars[0][0], jnp.int32(s))] = grads[s][...]
        for s in range(seqs):
            for g in range(3):
                start = g * features + s * chunk
                piece = scratch[0][s, :, g * wide : g * wide + chunk]
                total[:, start : start + chunk] = piece.astype(jnp.float32)
        total[:, 3 * features :] = grads[seqs][...]

    return adam_kernel(
        load,
        [place_of("seq")],
        grads,
        state,
        layer,
        previous,
        [lambda tile: pltpu.VMEM((seqs, tile, 3 * wide), low)],
    )


def scatter_rows(grad):
    return lax.psum_scatter(grad, "seq", scatter_dimension=0, tiled=True)


def split_feed(part, rows):
    rings = lax.axis_size("fsdp")
    part = part.reshape(rings, rows, -1)

    def body(place, part, *outs):
        for j in range(rings):
            outs[j][...] = part[lax.rem(place[0] + j, rings)]

    pieces = plain_call(body, [shaped(part.shape[1:], low)] * rings, scalars=1)(
        place_of("fsdp"), part
    )
    return return_sums(pieces)


def feed_adam(grads, state, layer, previous):
    seqs, rings = lax.axis_size("seq"), lax.axis_size("fsdp")
    half = state[0].shape[2] // 2
    block = half // (seqs * rings)
    tall = tall_of(block)

    def load(scalars, grads, scratch, total):
        for j in range(rings):
            scratch[0][lax.rem(scalars[0][0] - j + rings, rings)] = grads[j][...]
        for f in range(rings):
            for g in range(2):
                for s in range(seqs):
                    start = g * half + (s * rings + f) * block
                    at = (g * seqs + s) * tall
                    piece = scratch[0][f, :, at : at + block]
                    total[:, start : start + block] = piece.astype(jnp.float32)

    return adam_kernel(
        load,
        [place_of("fsdp")],
        grads,
        state,
        layer,
        previous,
        [lambda tile: pltpu.VMEM((rings, tile, 2 * seqs * tall), low)],
    )


def down_adam(part, state, layer, previous):
    part = part[: state[0].shape[1]]

    def load(scalars, grads, scratch, total):
        total[...] = grads[0][...].astype(jnp.float32)

    return adam_kernel(load, [], [part], state, layer, previous)


def place_blocks(blocks, owners, place, earlier=()):
    def body(place, *refs):
        if len(blocks[0].shape) == len(refs[-1].shape):
            refs = [ref.at[i] for ref in refs[:-1] for i in range(ref.shape[0])] + [refs[-1]]
        for block, owner in zip(refs, owners(place[0])):
            refs[-1][owner] = block[...]

    shape = blocks[0].shape
    if len(blocks) == 2:
        shape = (2 * shape[0],) + shape[1:]
    else:
        shape = (len(blocks),) + shape
    return plain_call(body, [shaped(shape, blocks[0].dtype)], scalars=1, earlier=earlier)(
        place, *blocks
    )[0]


def vectors_start(gain_weight, tap_weight):
    gains = gain_weight.reshape(2 * LAYERS, -1)
    taps = tap_weight.reshape(3 * LAYERS, -1)
    return gather_fsdp(jnp.concatenate([gains, taps], axis=0).astype(low))


def vectors_middle(blocks, earlier):
    rings = lax.axis_size("fsdp")
    both = place_blocks(
        blocks,
        lambda place: [lax.rem(place + j, rings) for j in range(rings)],
        place_of("fsdp"),
        earlier,
    )
    return both, send_seq(both)


def vectors_end(both, blocks):
    spread = place_blocks(
        stack_pairs(blocks),
        lambda place: [lax.bitwise_xor(place, jnp.int32(i)) for i in seq_order()],
        place_of("seq"),
    )
    gains = jnp.transpose(spread[:, :, : 2 * LAYERS], (2, 0, 1, 3)).astype(jnp.float32)
    taps = jnp.transpose(both[:, 2 * LAYERS :], (1, 0, 2)).astype(jnp.float32)
    return gains.reshape(LAYERS, 2, 1, -1), taps.reshape(LAYERS, 3, -1)


def vector_gradients(gain_grads, tap_grads, short):
    seqs, rings = lax.axis_size("seq"), lax.axis_size("fsdp")
    place_seq, place_fsdp = lax.axis_index("seq"), lax.axis_index("fsdp")
    gains = gain_grads.reshape(2 * LAYERS, seqs, -1)
    owner = place_seq ^ jnp.array(seq_order())
    pick = (owner[:, None] == jnp.arange(seqs)[None, :]).astype(jnp.float32)
    gains = jnp.einsum("jo,koc->jkc", pick, gains, precision=lax.Precision.HIGHEST)
    gains = small_scatter_seq(gains)
    taps = tap_grads.reshape(3 * LAYERS, -1)[:, : rings * short]
    both = jnp.concatenate([gains, taps], axis=0).reshape(5 * LAYERS, rings, short)
    owner = (place_fsdp + jnp.arange(rings)) % rings
    pick = (owner[:, None] == jnp.arange(rings)[None, :]).astype(jnp.float32)
    both = jnp.einsum("jo,koc->jkc", pick, both, precision=lax.Precision.HIGHEST)
    both = small_scatter_fsdp(both)
    return (
        both[: 2 * LAYERS].reshape(LAYERS, 2, short),
        both[2 * LAYERS :].reshape(LAYERS, 3, short),
    )


def unit_rows(values):
    row_scale = lax.rsqrt(jnp.mean(values * values, axis=-1, keepdims=True) + eps_norm)
    return values * row_scale, row_scale


def first_norm(inputs, gain, earlier):
    def body(inputs, gain, stream_out, normed_out):
        stream = inputs[...].astype(jnp.float32)
        stream_out[...] = stream
        normed_out[...] = (unit_rows(stream)[0] * gain[...]).astype(low)

    return plain_call(
        body, [shaped(inputs.shape), shaped(inputs.shape, low)], earlier=earlier
    )(inputs, gain)


def finish(base, sums, gain):
    def body(*refs):
        total = refs[0][...]
        for part in refs[1 : 1 + len(sums)]:
            total = total + part[...].astype(jnp.float32)
        if gain is None:
            refs[-1][...] = total.astype(low)
        else:
            refs[-2][...] = total
            refs[-1][...] = (unit_rows(total)[0] * refs[1 + len(sums)][...]).astype(low)

    if gain is None:
        return plain_call(body, [shaped(base.shape, low)])(base, *sums)[0]
    return plain_call(body, [shaped(base.shape), shaped(base.shape, low)])(base, *sums, gain)


def finish_back(flow, sums, stream, gain, carried=()):
    def body(flow, stream, gain, *refs):
        total = refs[0][...].astype(jnp.float32)
        for part in refs[1 : len(sums)]:
            total = total + part[...].astype(jnp.float32)
        unit, row_scale = unit_rows(stream[...])
        scaled = total * gain[...]
        inner_mean = jnp.mean(scaled * unit, axis=-1, keepdims=True)
        result = flow[...].astype(jnp.float32) + row_scale * (scaled - unit * inner_mean)
        refs[-3][...] = result
        refs[-2][...] = result.astype(low)
        refs[-1][...] = jnp.sum(total * unit, axis=0, keepdims=True)

    return plain_call(
        body,
        [shaped(flow.shape), shaped(flow.shape, low), shaped((1, flow.shape[1]))],
        carried=carried,
    )(flow, stream, gain, *sums)


def pair_sum(even, received):
    half, tokens, features = even.shape

    def body(even, received, *outs):
        for i in range(half):
            total = even[i] + received[i].astype(jnp.float32)
            outs[i][...] = total.astype(outs[i].dtype)

    outs = plain_call(
        body,
        [shaped((tokens, features))] + [shaped((tokens, features), low)] * (half - 1),
    )(even, received)
    return [outs[0]] + [seq_swap(outs[i], 2 * i) for i in range(1, half)]


def block_neighbour(place, i, count, step):
    order = list(range(0, count, 2)) + list(range(1, count, 2))
    owner = lax.bitwise_xor(place, jnp.int32(order[i])) + step
    inside = jnp.logical_and(owner >= 0, owner < count)
    number = lax.bitwise_xor(place, jnp.where(inside, owner, place))
    return lax.div(number, 2) + lax.rem(number, 2) * (count // 2), inside


def conv_forward(place, taps, gated, i, count):
    here = gated[i]
    tokens, chunk = here.shape
    at, inside = block_neighbour(place, i, count, -1)
    before = jnp.where(inside, gated[at, tokens - 8 :, :], 0.0)
    row = lax.broadcasted_iota(jnp.int32, (tokens, chunk), 0)
    last, second = before[7:8, :], before[6:7, :]
    one = jnp.where(row == 0, last, pltpu.roll(here, 1, 0))
    two = jnp.where(row == 0, second, jnp.where(row == 1, last, pltpu.roll(here, 2, 0)))
    return taps[0:1, :] * two + taps[1:2, :] * one + taps[2:3, :] * here, one, two


def mixer_forward(blocks, inner, outer, taps):
    half, tokens, features = blocks[0].shape
    count = 2 * half
    chunk = outer.shape[0]
    wide = inner.shape[1] // 3

    def body(place, even_in, odd_in, inner, outer, taps, *refs):
        projected, even, odd, gated, mixed = refs
        for k, rows in enumerate((even_in, odd_in)):
            rows = rows[...].reshape(half * tokens, features)
            for g in range(3):
                columns = slice(g * wide, (g + 1) * wide)
                part = dot(rows, inner[:, columns]).reshape(half, tokens, wide)
                projected[k * half : (k + 1) * half, :, columns] = part

        for i in range(count):
            product = projected[i, :, :wide] * projected[i, :, 2 * wide :]
            gated[i] = product[:, :chunk].astype(low).astype(jnp.float32)
        taps = taps[...]
        for i in range(count):
            conv_out = conv_forward(place[0], taps, gated, i, count)[0]
            mixed[i] = (projected[i, :, wide : wide + chunk] * conv_out).astype(low)
        rows = mixed[:half].reshape(half * tokens, chunk)
        even[...] = dot(rows, outer[...]).reshape(half, tokens, features)
        rows = mixed[half:].reshape(half * tokens, chunk)
        odd[...] = dot(rows, outer[...]).reshape(half, tokens, features).astype(low)

    return plain_call(
        body,
        [
            shaped((count, tokens, 3 * wide)),
            shaped((half, tokens, features)),
            shaped((half, tokens, features), low),
        ],
        scalars=1,
        scratch=[
            pltpu.VMEM((count, tokens, chunk), jnp.float32),
            pltpu.VMEM((count, tokens, chunk), low),
        ],
    )(place_of("seq"), *blocks, inner, outer, taps)


def mixer_backward(blocks, projected, inner, outer, taps):
    half, tokens, features = blocks[0].shape
    count = 2 * half
    chunk = outer.shape[0]
    wide = inner.shape[1] // 3

    def body(place, even_in, odd_in, projected, inner, outer, taps, *refs):
        even, odd, flows, mixed, tap_out, gated, flow = refs
        for i in range(count):
            product = projected[i, :, :wide] * projected[i, :, 2 * wide :]
            gated[i] = product[:, :chunk].astype(low).astype(jnp.float32)
        taps = taps[...]
        tap_sums = [jnp.zeros((1, chunk), jnp.float32)] * 3
        for k in range(2):
            rows = (even_in, odd_in)[k][...].reshape(half * tokens, features)
            back = dot(rows, outer[...], nt).reshape(half, tokens, chunk)
            for i in range(k * half, (k + 1) * half):
                conv_out, one, two = conv_forward(place[0], taps, gated, i, count)
                gate = projected[i, :, wide : wide + chunk]
                mixed[i] = (gate * conv_out).astype(low)
                mixed_flow = back[i - k * half]
                conv_flow = mixed_flow * gate
                flow[i] = conv_flow
                for j, shifted in enumerate((two, one, gated[i])):
                    term = jnp.sum(conv_flow * shifted, axis=0, keepdims=True)
                    tap_sums[j] = tap_sums[j] + term
                flows[i, :, wide : wide + chunk] = (mixed_flow * conv_out).astype(low)
        for j in range(3):
            tap_out[j : j + 1, :] = tap_sums[j]
        row = lax.broadcasted_iota(jnp.int32, (tokens, chunk), 0)
        for i in range(count):
            here = flow[i]
            at, inside = block_neighbour(place[0], i, count, 1)
            beyond = jnp.where(inside, flow[at, :8, :], 0.0)
            first, second = beyond[0:1, :], beyond[1:2, :]
            one = jnp.where(row == tokens - 1, first, pltpu.roll(here, tokens - 1, 0))
            two = jnp.where(
                row == tokens - 1,
                second,
                jnp.where(row == tokens - 2, first, pltpu.roll(here, tokens - 2, 0)),
            )
            gated_flow = taps[2:3, :] * here + taps[1:2, :] * one + taps[0:1, :] * two
            x_part = projected[i, :, 2 * wide : 2 * wide + chunk]
            b_part = projected[i, :, :chunk]
            flows[i, :, :chunk] = (gated_flow * x_part).astype(low)
            flows[i, :, 2 * wide : 2 * wide + chunk] = (gated_flow * b_part).astype(low)
            if wide > chunk:
                for g in range(3):
                    gap = jnp.zeros((tokens, wide - chunk), low)
                    flows[i, :, g * wide + chunk : (g + 1) * wide] = gap
        rows = flows[:half].reshape(half * tokens, 3 * wide)
        even[...] = dot(rows, inner[...], nt).reshape(half, tokens, features)
        rows = flows[half:].reshape(half * tokens, 3 * wide)
        odd[...] = dot(rows, inner[...], nt).reshape(half, tokens, features).astype(low)

    return plain_call(
        body,
        [
            shaped((half, tokens, features)),
            shaped((half, tokens, features), low),
            shaped((count, tokens, 3 * wide), low),
            shaped((count, tokens, chunk), low),
            shaped((3, chunk)),
        ],
        scalars=1,
        scratch=[pltpu.VMEM((count, tokens, chunk), jnp.float32)] * 2,
    )(place_of("seq"), *blocks, projected, inner, outer, taps)


def mixer_grads(normed, flows, mixed, lows, rows):
    seqs, rings = lax.axis_size("seq"), lax.axis_size("fsdp")
    features, width = normed[0].shape[-1], flows.shape[-1]
    half = normed[0].shape[0]
    wide = width // 3
    count = features // width

    def body(place, normed_even, normed_odd, flows, mixed, low_even, low_odd, *refs):
        outs, inner, outer = refs[:rings], refs[rings], refs[rings + 1]
        long = lambda array: array.reshape(-1, array.shape[-1])
        for g in range(3):
            at = slice(g * wide, (g + 1) * wide)
            part = dot(long(normed_even[...]), long(flows[:half, :, at]), tn)
            part = part + dot(long(normed_odd[...]), long(flows[half:, :, at]), tn)
            part = part.astype(low)
            for i in range(seqs * rings):
                inner[i // rings, i % rings, :, at] = part[i * rows : (i + 1) * rows]
        part = dot(long(mixed[:half]), long(low_even[...]), tn)
        part = part + dot(long(mixed[half:]), long(low_odd[...]), tn)
        part = part.astype(low)
        for f in range(rings):
            outer[f] = part[f * rows : (f + 1) * rows]
        for j in range(rings):
            f = lax.rem(place[0] + j, rings)
            for s in range(seqs):
                outs[j][s] = inner[s, f]
            for i in range(count):
                outs[j][seqs + i] = outer[f, :, i * width : (i + 1) * width]

    return plain_call(
        body,
        [shaped((seqs + count, rows, width), low)] * rings,
        scalars=1,
        scratch=[
            pltpu.VMEM((seqs, rings, rows, width), low),
            pltpu.VMEM((rings, rows, features), low),
        ],
        cost=(24 * half * normed[0].size, 8 * normed[0].size),
    )(place_of("fsdp"), *normed, flows, mixed, *lows)


def hidden_tile(hidden):
    return 256 if hidden % 256 == 0 else 128


def feed_specs(features, hidden):
    tile = hidden_tile(hidden)
    steps = hidden // tile
    return (
        pl.BlockSpec((features, tile), lambda i: (0, i)),
        pl.BlockSpec((features, tile), lambda i: (0, i + steps)),
        pl.BlockSpec((tile, features), lambda i: (i, 0)),
    )


def feed_forward(blocks, up_matrix, down, own):
    count = len(blocks)
    tokens, features = blocks[0].shape
    hidden = down.shape[0]
    tile = hidden_tile(hidden)
    steps = hidden // tile

    def body(*refs):
        gate_matrix, up_matrix, down = refs[count : count + 3]
        outs = refs[count + 3 : 2 * count + 3]
        gate_out, up_out, hidden_out, rows, total = refs[2 * count + 3 :]
        step = pl.program_id(0)

        @pl.when(step == 0)
        def _():
            for i in range(count):
                rows[i * tokens : (i + 1) * tokens] = refs[i][...]
            total[...] = jnp.zeros_like(total)

        gate = dot(rows[...], gate_matrix[...])
        up = dot(rows[...], up_matrix[...])
        gate_out[...] = gate
        up_out[...] = up
        value = (gate * jax.nn.sigmoid(gate) * up).astype(low)
        hidden_out[...] = value
        total[...] += dot(value, down[...])

        @pl.when(step == steps - 1)
        def _():
            for i in range(count):
                outs[i][...] = total[i * tokens : (i + 1) * tokens].astype(outs[i].dtype)

    columns = pl.BlockSpec((count * tokens, tile), lambda i: (0, i))
    outs = kernel_call(
        body,
        (steps,),
        [whole((tokens, features))] * count + list(feed_specs(features, hidden)),
        [whole((tokens, features))] * count + [columns] * 3,
        [
            shaped((tokens, features), jnp.float32 if own and i == 0 else low)
            for i in range(count)
        ]
        + [shaped((count * tokens, hidden), kind) for kind in (jnp.float32, jnp.float32, low)],
        scratch=[
            pltpu.VMEM((count * tokens, features), low),
            pltpu.VMEM((count * tokens, features), jnp.float32),
        ],
    )(*blocks, up_matrix, up_matrix, down)
    return outs[:count], outs[count:]


def feed_backward(blocks, gates, ups, up_matrix, down, own):
    count = len(blocks)
    tokens, features = blocks[0].shape
    hidden = down.shape[0]
    tile = hidden_tile(hidden)
    steps = hidden // tile

    def body(*refs):
        gate_part, up_part, gate_matrix, up_matrix, down = refs[count : count + 5]
        outs = refs[count + 5 : 2 * count + 5]
        gate_out, up_out, rows, total = refs[2 * count + 5 :]
        step = pl.program_id(0)

        @pl.when(step == 0)
        def _():
            for i in range(count):
                rows[i * tokens : (i + 1) * tokens] = refs[i][...]
            total[...] = jnp.zeros_like(total)

        flow = dot(rows[...], down[...], nt)
        gate = gate_part[...]
        smooth = jax.nn.sigmoid(gate)
        gate_flow = flow * up_part[...] * (smooth * (1.0 + gate * (1.0 - smooth)))
        gate_flow = gate_flow.astype(low)
        up_flow = (flow * (gate * smooth)).astype(low)
        gate_out[...] = gate_flow
        up_out[...] = up_flow
        total[...] += dot(gate_flow, gate_matrix[...], nt) + dot(up_flow, up_matrix[...], nt)

        @pl.when(step == steps - 1)
        def _():
            for i in range(count):
                outs[i][...] = total[i * tokens : (i + 1) * tokens].astype(outs[i].dtype)

    columns = pl.BlockSpec((count * tokens, tile), lambda i: (0, i))
    outs = kernel_call(
        body,
        (steps,),
        [whole((tokens, features))] * count + [columns] * 2 + list(feed_specs(features, hidden)),
        [whole((tokens, features))] * count + [columns] * 2,
        [
            shaped((tokens, features), jnp.float32 if own and i == 0 else low)
            for i in range(count)
        ]
        + [shaped((count * tokens, hidden), low)] * 2,
        scratch=[
            pltpu.VMEM((count * tokens, features), low),
            pltpu.VMEM((count * tokens, features), jnp.float32),
        ],
    )(*blocks, gates, ups, up_matrix, up_matrix, down)
    return outs[:count], outs[count:]


def feed_grads(normed, gate_flows, up_flows):
    count, groups = len(normed), len(gate_flows)
    tokens, features = normed[0].shape
    size, hidden = gate_flows[0].shape
    tile = hidden_tile(hidden)
    steps = hidden // tile

    def body(*refs):
        flows = refs[count : count + 2 * groups]
        out, rows, columns = refs[count + 2 * groups :]
        step = pl.program_id(0)

        @pl.when(step == 0)
        def _():
            for i in range(count):
                rows[i * tokens : (i + 1) * tokens] = refs[i][...]

        for half in range(2):

            @pl.when(lax.div(step, steps) == half)
            def _():
                for i in range(groups):
                    columns[i * size : (i + 1) * size] = flows[half * groups + i][...]

        out[...] = dot(rows[...], columns[...], tn).astype(low)

    gate_spec = pl.BlockSpec((size, tile), lambda i: (0, jnp.minimum(i, steps - 1)))
    up_spec = pl.BlockSpec((size, tile), lambda i: (0, jnp.maximum(i - steps, 0)))
    return kernel_call(
        body,
        (2 * steps,),
        [whole((tokens, features))] * count
        + [gate_spec] * groups
        + [up_spec] * groups,
        pl.BlockSpec((features, tile), lambda i: (0, i)),
        shaped((features, 2 * hidden), low),
        scratch=[
            pltpu.VMEM((count * tokens, features), low),
            pltpu.VMEM((groups * size, tile), low),
        ],
        cost=(12 * count * tokens * features * hidden, 24 * features * hidden),
    )(*normed, *gate_flows, *up_flows)


def down_grads(hiddens, flows):
    count, groups = len(flows), len(hiddens)
    tokens, features = flows[0].shape
    size, hidden = hiddens[0].shape
    tile = hidden_tile(hidden)

    def body(*refs):
        hiddens = refs[count : count + groups]
        out, rows, columns = refs[count + groups :]

        @pl.when(pl.program_id(0) == 0)
        def _():
            for i in range(count):
                rows[i * tokens : (i + 1) * tokens] = refs[i][...]

        for i in range(groups):
            columns[i * size : (i + 1) * size] = hiddens[i][...]
        out[...] = dot(columns[...], rows[...], tn).astype(low)

    return kernel_call(
        body,
        (hidden // tile,),
        [whole((tokens, features))] * count
        + [pl.BlockSpec((size, tile), lambda i: (0, i))] * groups,
        pl.BlockSpec((tile, features), lambda i: (i, 0)),
        shaped((hidden, features), low),
        scratch=[
            pltpu.VMEM((count * tokens, features), low),
            pltpu.VMEM((groups * size, tile), low),
        ],
        cost=(6 * count * tokens * features * hidden, 12 * features * hidden),
    )(*flows, *hiddens)


def join_blocks(blocks):
    def body(*refs):
        for i in range(len(blocks)):
            refs[len(blocks) + i][...] = refs[i][...]

    return plain_call(body, [shaped(block.shape, block.dtype) for block in blocks])(*blocks)


def groups_of(blocks):
    return [blocks[i : i + 2] for i in range(0, len(blocks), 2)]


def return_sums(sums):
    return [sums[0]] + [fsdp_shift(sums[j], j) for j in range(1, len(sums))]


def adam_update(weight, first, second, gradient, rate, decay):
    first_new = beta_one * first + (1.0 - beta_one) * gradient
    second_new = beta_two * second + (1.0 - beta_two) * gradient * gradient
    first_hat = first_new / (1.0 - beta_one**STEP)
    second_hat = second_new / (1.0 - beta_two**STEP)
    weight_new = weight - rate * (first_hat / (jnp.sqrt(second_hat) + eps_adam) + decay * weight)
    return (first_new, second_new, weight_new)


def local(
    inputs,
    cotangent,
    mix_weight,
    mix_first,
    mix_second,
    feed_weight,
    feed_first,
    feed_second,
    down_weight,
    down_first,
    down_second,
    gain_weight,
    gain_first,
    gain_second,
    tap_weight,
    tap_first,
    tap_second,
):
    sequences, length, features = inputs.shape
    seqs, rings = lax.axis_size("seq"), lax.axis_size("fsdp")
    rows = mix_weight.shape[1]
    chunk = features // seqs
    wide = -(-chunk // 128) * 128
    cotangent = cotangent.reshape(-1, features)
    Order.mark = jnp.zeros(mark_shape.shape, mark_shape.dtype)

    feed_swaps, mixes, feeds = [None] * LAYERS, [None] * LAYERS, [None] * LAYERS
    feed_swaps[0] = swap_feed(pack_feed(feed_weight, 0))
    mix_packed = pack_mix(mix_weight, 0, wide)
    mix_swap = swap_mix(mix_packed)
    down_rows = gather_rows(pack_down(down_weight, 0))
    vector_blocks = vectors_start(gain_weight, tap_weight)
    mix_pieces = gather_fsdp(join_mix(mix_swap, mix_packed))
    feeds[0] = (gather_rows(assemble_feed(feed_swaps[0])), down_rows)
    both, vector_blocks = vectors_middle(vector_blocks, mix_pieces[1:2])
    gain_rows, tap_rows = vectors_end(both, vector_blocks)
    stream, normed = first_norm(
        inputs.reshape(-1, features), gain_rows[0, 0], mix_pieces[2:-1]
    )
    blocks = send_seq(normed)
    later_packed = pack_mix(mix_weight, 1, wide)
    blocks = stack_pairs(blocks)
    mixes[0] = assemble_mix(mix_pieces, wide, features)

    kept = []
    for layer in range(LAYERS):
        last = layer + 1 == LAYERS
        gathered = blocks
        projected, even, odd = mixer_forward(blocks, *mixes[layer], tap_rows[layer])
        odd = seq_swap(odd, 1)
        if last:
            flow_blocks = gather_fsdp(cotangent)
        sums = pair_sum(even, odd)
        if last:
            flow_low = join_blocks(flow_blocks)
        else:
            feed_swaps[1] = swap_feed(pack_feed(feed_weight, 1))
        middle, normed_two = finish(stream, sums, gain_rows[layer, 1])
        two_blocks = gather_fsdp(normed_two)
        if not last:
            later_mix = join_mix(swap_mix(later_packed), later_packed)
            later_mix = lax.all_gather(later_mix, "fsdp", axis=0)
            feeds[1] = (
                gather_rows(assemble_feed(feed_swaps[1])),
                gather_rows(pack_down(down_weight, 1)),
            )
        sums, values = [], []
        for number, group in enumerate(groups_of(two_blocks)):
            outs, saved = feed_forward(group, *feeds[layer], number == 0)
            sums += outs
            values.append(saved)
        kept.append((stream, middle, gathered, projected, two_blocks, values))
        sums = return_sums(sums)
        if not last:
            stream, normed = finish(middle, sums, gain_rows[layer + 1, 0])
            blocks = stack_pairs(send_seq(normed))
            mixes[1] = assemble_mix(later_mix, wide, features)

    states = (
        (mix_weight, mix_first, mix_second),
        (feed_weight, feed_first, feed_second),
        (down_weight, down_first, down_second),
    )
    new = [None] * 3
    gain_grads, tap_grads = [None] * LAYERS, [None] * LAYERS
    flow = cotangent
    for layer in reversed(range(LAYERS)):
        last = layer + 1 == LAYERS
        stream, middle, gathered, projected, two_blocks, values = kept[layer]
        back_sums, gate_flows, up_flows = [], [], []
        for number, group in enumerate(groups_of(flow_low)):
            gates, ups, _ = values[number]
            outs, (gate_flow, up_flow) = feed_backward(
                group, gates, ups, *feeds[layer], number == 0
            )
            back_sums += outs
            gate_flows.append(gate_flow)
            up_flows.append(up_flow)
        if last:
            outputs = finish(middle, sums, None).reshape(inputs.shape)
        back_sums = return_sums(back_sums)
        down_part = down_grads([value[2] for value in values], flow_low)
        middle_flow, middle_low, gain_two, down_part = finish_back(
            flow, back_sums, middle, gain_rows[layer, 1], [down_part]
        )
        down_part = scatter_rows(down_part)
        blocks = send_seq(middle_low)
        feed_part = feed_grads(two_blocks, gate_flows, up_flows)
        even, odd, feed_part = stack_pairs(
            blocks, () if last else later_mix[1::2], [feed_part]
        )
        feed_part = scatter_rows(feed_part)
        blocks = even, odd
        even, odd, flows, mixed, tap_grads[layer] = mixer_backward(
            blocks, projected, *mixes[layer], tap_rows[layer]
        )
        sums = pair_sum(even, seq_swap(odd, 1))
        mix_part = return_sums(mixer_grads(gathered, flows, mixed, blocks, rows))
        if not last:
            later_mix = mix_reduce(later_mix)
        flow, low_flow, gain_one = finish_back(middle_flow, sums, stream, gain_rows[layer, 0])
        gain_grads[layer] = jnp.concatenate([gain_one, gain_two])
        if last:
            flow_low = gather_fsdp(low_flow)
            later_mix, later_feed, later_down = mix_part, feed_part, down_part
    later_feed = split_feed(later_feed, rows)
    new[2] = down_adam(later_down, states[2], 1, new[2])
    new[0] = mix_adam(later_mix, states[0], 1, new[0], wide)
    gain_grad, tap_grad = vector_gradients(
        jnp.stack(gain_grads), jnp.stack(tap_grads), gain_weight.shape[-1]
    )
    new[1] = feed_adam(later_feed, states[1], 1, new[1])
    mix_part = mix_reduce(mix_part)
    new[2] = down_adam(down_part, states[2], 0, new[2])
    feed_part = split_feed(feed_part, rows)
    new[0] = mix_adam(mix_part, states[0], 0, new[0], wide)
    new[1] = feed_adam(feed_part, states[1], 0, new[1])
    input_grad = flow.reshape(sequences, length, features)
    gain_new = adam_update(gain_weight, gain_first, gain_second, gain_grad, rate_vector, 0.0)
    tap_new = adam_update(tap_weight, tap_first, tap_second, tap_grad, rate_vector, 0.0)
    matrices = [(part[1], part[2], part[0]) for part in new]
    return (outputs, input_grad, *sum(matrices, ()), *gain_new, *tap_new)


def solution(mesh):
    tokens = P("fsdp", "seq", None)
    rows = P(None, ("seq", "fsdp"), None)
    last = P(None, None, ("seq", "fsdp"))
    return jax.shard_map(
        local,
        mesh=mesh,
        in_specs=(tokens,) * 2 + (rows,) * 9 + (last,) * 6,
        out_specs=(tokens,) * 2 + (rows,) * 9 + (last,) * 6,
        check_vma=False,
    )
```

```python
import math

import jax
import jax.numpy as jnp
from jax import lax
from jax.experimental import pallas as pl
from jax.experimental.pallas import tpu as pltpu
from jax.sharding import PartitionSpec as P

LAYERS = 2
STEP = 10

eps_norm = 1e-05
eps_adam = 1e-08
beta_one = 0.9
beta_two = 0.95
rate_matrix = 0.05
rate_vector = 0.6
decay_matrix = 0.1

low = jnp.bfloat16


def dot(left, right, sides=((1,), (0,))):
    return lax.dot_general(left, right, (sides, ((), ())), preferred_element_type=jnp.float32)


nt = ((1,), (1,))
tn = ((0,), (0,))


def seq_order():
    count = lax.axis_size("seq")
    return list(range(0, count, 2)) + list(range(1, count, 2))


def seq_swap(array, by):
    count = lax.axis_size("seq")
    return lax.ppermute(array, "seq", [(i, i ^ by) for i in range(count)])


def send_seq(array):
    return [array] + [seq_swap(array, by) for by in range(2, lax.axis_size("seq"), 2)]


def fsdp_swap(array, by):
    count = lax.axis_size("fsdp")
    return lax.ppermute(array, "fsdp", [(i, i ^ by) for i in range(count)])


def gather_fsdp(array):
    count = lax.axis_size("fsdp")
    return [array] + [fsdp_swap(array, by) for by in range(1, count)]


def small_scatter_seq(parts):
    half = parts.shape[0] // 2
    total = parts[:half] + seq_swap(parts[half:], 1)
    for i in range(1, half):
        total = total.at[0].add(seq_swap(total[i], 2 * i))
    return total[0]


def small_scatter_fsdp(parts):
    total = parts[0]
    for by in range(1, parts.shape[0]):
        total = total + fsdp_swap(parts[by], by)
    return total


def stack_pairs(blocks, earlier=(), carried=()):
    def body(*refs):
        for i in range(len(blocks)):
            refs[-1][i] = refs[i][...]

    shape = (len(blocks),) + blocks[0].shape
    even, *rest = plain_call(
        body, [shaped(shape, blocks[0].dtype)], earlier=earlier, carried=carried
    )(*blocks)
    return even, seq_swap(even, 1), *rest


def pad_last(array, width):
    return jnp.pad(array, [(0, 0)] * (array.ndim - 1) + [(0, width - array.shape[-1])])


def place_of(axis):
    return lax.axis_index(axis).astype(jnp.int32).reshape(1)


scalar = pl.BlockSpec(memory_space=pltpu.SMEM)
held = pl.BlockSpec(memory_space=pltpu.VMEM)


def shaped(shape, kind=jnp.float32):
    return jax.ShapeDtypeStruct(shape, kind)


class Order:
    mark = None


mark_shape = jax.ShapeDtypeStruct((8, 128), jnp.float32)
anywhere = pl.BlockSpec(memory_space=pl.ANY)


def bytes_of(shape, kind):
    return math.prod(shape) * jnp.dtype(kind).itemsize


def vmem_of(operands, in_specs, out_shape, out_specs, scratch, grid):
    total = 0
    for array, spec in [*zip(operands, in_specs), *zip(out_shape, out_specs)]:
        if spec is anywhere or spec is scalar:
            continue
        if grid:
            total += 2 * bytes_of(spec.block_shape, array.dtype)
        else:
            total += bytes_of(array.shape, array.dtype)
    for array in scratch:
        total += bytes_of(array.shape, array.dtype)
    return total + total // 2 + 4 * 1024 * 1024


def ordered_call(body, operands, in_specs, out_specs, out_shape, aliases, scratch, grid, cost):
    given, made = len(operands), len(out_shape)

    def marked(*refs):
        body(*refs[:given], *refs[given + 1 : given + 1 + made], *refs[given + 2 + made :])

    outs = pl.pallas_call(
        marked,
        in_specs=list(in_specs) + [anywhere],
        out_specs=list(out_specs) + [anywhere],
        out_shape=list(out_shape) + [mark_shape],
        scratch_shapes=list(scratch),
        input_output_aliases=aliases,
        compiler_params=pltpu.CompilerParams(
            vmem_limit_bytes=min(
                vmem_of(operands, in_specs, out_shape, out_specs, scratch, grid), 60 << 20
            )
        ),
        cost_estimate=pl.CostEstimate(
            flops=cost[0], bytes_accessed=cost[1], transcendentals=0
        ),
        **grid,
    )(*operands, Order.mark)
    Order.mark = outs[-1]
    return outs[:-1]


def kernel_call(
    body, grid, in_specs, out_specs, out_shape, aliases=None, scratch=(), cost=(0, 0)
):
    single = not isinstance(out_shape, list)

    def run(*operands):
        outs = ordered_call(
            body,
            operands,
            in_specs,
            [out_specs] if single else out_specs,
            [out_shape] if single else out_shape,
            aliases or {},
            scratch,
            dict(grid=grid),
            cost,
        )
        return outs[0] if single else outs

    return run


def plain_call(
    body, out_shape, scalars=0, scratch=(), earlier=(), carried=(), cost=(0, 0)
):
    def run(*operands):
        given, made, more = len(operands), len(out_shape), len(earlier) + len(carried)

        def rest(*refs):
            outs = refs[given + more :]
            body(*refs[:given], *outs[:made], *outs[made + len(carried) :])

        first = given + len(earlier)
        return ordered_call(
            rest,
            (*operands, *earlier, *carried),
            [scalar] * scalars + [held] * (given - scalars) + [anywhere] * more,
            [held] * made + [anywhere] * len(carried),
            [*out_shape, *(jax.ShapeDtypeStruct(x.shape, x.dtype) for x in carried)],
            {first + i: made + i for i in range(len(carried))},
            scratch,
            {},
            cost,
        )

    return run


def whole(shape):
    return pl.BlockSpec(shape, lambda i: (0,) * len(shape))


def pack_mix(mix_weight, layer, wide, earlier=()):
    seqs = lax.axis_size("seq")
    rows, columns = mix_weight.shape[1:]
    features = columns // 4
    chunk = features // seqs
    outer = features // (3 * wide)

    def body(place, weight, *refs):
        out = refs[-1]
        for s in range(seqs):
            slot = lax.bitwise_xor(place[0], jnp.int32(s))
            for g in range(3):
                start = g * features + s * chunk
                piece = weight[0, :, start : start + chunk].astype(low)
                if wide > chunk:
                    piece = jnp.concatenate([piece, jnp.zeros((rows, wide - chunk), low)], axis=1)
                out[slot, :, g * wide : (g + 1) * wide] = piece
        for i in range(outer):
            start = 3 * features + i * 3 * wide
            out[seqs + i] = weight[0, :, start : start + 3 * wide].astype(low)

    shape = (seqs + outer, rows, 3 * wide)
    return kernel_call(
        body,
        (1,),
        [scalar, pl.BlockSpec((1, rows, columns), lambda i: (layer, 0, 0))]
        + [anywhere] * len(earlier),
        whole(shape),
        jax.ShapeDtypeStruct(shape, low),
    )(place_of("seq"), mix_weight, *earlier)


def assemble_mix(pieces, wide, features):
    seqs, rings = lax.axis_size("seq"), lax.axis_size("fsdp")
    outer, rows, _ = pieces[0].shape
    outer = outer - seqs
    rotated = isinstance(pieces, list)
    pieces = pieces if rotated else [pieces]

    def body(place_seq, place_fsdp, *refs):
        inner_out, outer_out = refs[-2:]
        refs = refs if rotated else [refs[0].at[j] for j in range(rings)]
        for j in range(rings):
            f = lax.bitwise_xor(place_fsdp[0], jnp.int32(j)) if rotated else j
            for s in range(seqs):
                inner_out[lax.bitwise_xor(place_seq[0], jnp.int32(s)), f] = refs[j][s]
            for i in range(outer):
                outer_out[f, :, i * 3 * wide : (i + 1) * 3 * wide] = refs[j][seqs + i]

    inner_shape = (seqs, rings, rows, 3 * wide)
    outer_shape = (rings, rows, features)
    inner, out = plain_call(
        body, [shaped(inner_shape, low), shaped(outer_shape, low)], scalars=2
    )(place_of("seq"), place_of("fsdp"), *pieces)
    return inner.reshape(features, 3 * wide), out.reshape(rings * rows, features)


def swap_mix(packed):
    seqs = lax.axis_size("seq")
    return [packed[:1]] + [seq_swap(packed[by : by + 1], by) for by in range(1, seqs)]


def join_mix(parts, packed, earlier=()):
    seqs = len(parts)

    def body(*refs):
        out = refs[-1]
        for s in range(seqs):
            out[s] = refs[s][0]
        out[seqs:] = refs[seqs][seqs:]

    return plain_call(body, [shaped(packed.shape, low)], earlier=earlier)(*parts, packed)[0]


def tall_of(block):
    step = 128 // min(lax.axis_size("seq"), 128)
    return -(-block // step) * step


def pack_feed(feed_weight, layer):
    seqs, rings = lax.axis_size("seq"), lax.axis_size("fsdp")
    rows, columns = feed_weight.shape[1:]
    half = columns // 2
    block = half // (seqs * rings)
    tall = tall_of(block)

    def body(place, weight, out):
        for f in range(rings):
            slot = lax.bitwise_xor(place[0], jnp.int32(f))
            for g in range(2):
                for s in range(seqs):
                    start = g * half + (s * rings + f) * block
                    piece = weight[0, :, start : start + block].astype(low)
                    if tall > block:
                        piece = jnp.concatenate(
                            [piece, jnp.zeros((rows, tall - block), low)], axis=1
                        )
                    to = (g * seqs + s) * tall
                    out[slot, :, to : to + tall] = piece

    shape = (rings, rows, 2 * seqs * tall)
    return kernel_call(
        body,
        (1,),
        [scalar, pl.BlockSpec((1, rows, columns), lambda i: (layer, 0, 0))],
        whole(shape),
        jax.ShapeDtypeStruct(shape, low),
    )(place_of("fsdp"), feed_weight)


def assemble_feed(pieces):
    rings = len(pieces)

    def body(place, *refs):
        out = refs[rings]
        for j in range(rings):
            out[lax.bitwise_xor(place[0], jnp.int32(j))] = refs[j][0]

    shape = (rings,) + pieces[0].shape[1:]
    return kernel_call(
        body,
        (1,),
        [scalar] + [whole(piece.shape) for piece in pieces],
        whole(shape),
        jax.ShapeDtypeStruct(shape, low),
    )(place_of("fsdp"), *pieces)


def swap_feed(packed):
    rings = lax.axis_size("fsdp")
    return [packed[:1]] + [fsdp_swap(packed[by : by + 1], by) for by in range(1, rings)]


def gather_rows(part):
    return lax.all_gather(part.reshape(-1, part.shape[-1]), "seq", axis=0, tiled=True)


def pack_down(down_weight, layer):
    block = down_weight.shape[1]
    return jnp.pad(down_weight[layer].astype(low), ((0, tall_of(block) - block), (0, 0)))


def adam_kernel(load, scalars, grads, state, layer, previous, scratch=(), earlier=()):
    weight = state[0]
    rows, columns = weight.shape[1:]
    tile = 16 if rows % 16 == 0 else rows
    width = 768
    specs = [
        pl.BlockSpec(grad.shape if tile == rows else (tile, grad.shape[-1]), lambda i: (i, 0))
        for grad in grads
    ]
    part = pl.BlockSpec((1, tile, columns), lambda i: (layer, i, 0))
    kept = (0 if previous is None else 3) + len(earlier)
    before = len(scalars) + len(grads)

    def body(*refs):
        weight, first, second = refs[before : before + 3]
        weight_out, first_out, second_out, total = refs[before + 3 + kept : before + 7 + kept]
        load(refs[: len(scalars)], refs[len(scalars) : before], refs[before + 7 + kept :], total)
        for start in range(0, columns, width):
            at = slice(start, start + width)
            gradient = total[:, at]
            old = weight[0, :, at]
            first_new = beta_one * first[0, :, at] + (1.0 - beta_one) * gradient
            second_new = beta_two * second[0, :, at] + (1.0 - beta_two) * gradient * gradient
            first_hat = first_new / (1.0 - beta_one**STEP)
            second_hat = second_new / (1.0 - beta_two**STEP)
            step = first_hat / (jnp.sqrt(second_hat) + eps_adam) + decay_matrix * old
            first_out[0, :, at] = first_new
            second_out[0, :, at] = second_new
            weight_out[0, :, at] = old - rate_matrix * step

    return kernel_call(
        body,
        (rows // tile,),
        [scalar] * len(scalars)
        + specs
        + [part] * 3
        + [anywhere] * kept,
        [part] * 3,
        [shaped(weight.shape)] * 3,
        aliases={before + 3 + i: i for i in range(kept - len(earlier))},
        scratch=[pltpu.VMEM((tile, columns), jnp.float32), *(make(tile) for make in scratch)],
        cost=(0, 26 * rows * columns),
    )(*scalars, *grads, *state, *(previous or ()), *earlier)


def mix_reduce(pieces):
    seqs, rings = lax.axis_size("seq"), lax.axis_size("fsdp")
    count, rows, width = pieces[0].shape
    outer = count - seqs

    def body(place, *refs):
        inner_out, outer_out = refs[rings:]
        for s in range(seqs):
            total = refs[0][s].astype(jnp.float32)
            for j in range(1, rings):
                total = total + refs[j][s].astype(jnp.float32)
            inner_out[lax.bitwise_xor(place[0], jnp.int32(s))] = total.astype(low)
        for i in range(outer):
            total = refs[0][seqs + i].astype(jnp.float32)
            for j in range(1, rings):
                total = total + refs[j][seqs + i].astype(jnp.float32)
            outer_out[:, i * width : (i + 1) * width] = total

    inner, last = plain_call(
        body,
        [shaped((seqs, rows, width), low), shaped((rows, outer * width))],
        scalars=1,
    )(place_of("seq"), *pieces)
    return [inner[0]] + [seq_swap(inner[j], j) for j in range(1, seqs)] + [last]


def mix_adam(grads, state, layer, previous, wide):
    seqs = lax.axis_size("seq")
    features = state[0].shape[2] // 4
    chunk = features // seqs

    def load(scalars, grads, scratch, total):
        for s in range(seqs):
            scratch[0][lax.bitwise_xor(scalars[0][0], jnp.int32(s))] = grads[s][...]
        for s in range(seqs):
            for g in range(3):
                start = g * features + s * chunk
                piece = scratch[0][s, :, g * wide : g * wide + chunk]
                total[:, start : start + chunk] = piece.astype(jnp.float32)
        total[:, 3 * features :] = grads[seqs][...]

    return adam_kernel(
        load,
        [place_of("seq")],
        grads,
        state,
        layer,
        previous,
        [lambda tile: pltpu.VMEM((seqs, tile, 3 * wide), low)],
    )


def scatter_rows(grad):
    return lax.psum_scatter(grad, "seq", scatter_dimension=0, tiled=True)


def split_feed(part, rows):
    rings = lax.axis_size("fsdp")
    part = part.reshape(rings, rows, -1)

    def body(place, part, *outs):
        for j in range(rings):
            outs[j][...] = part[lax.bitwise_xor(place[0], jnp.int32(j))]

    pieces = plain_call(body, [shaped(part.shape[1:], low)] * rings, scalars=1)(
        place_of("fsdp"), part
    )
    return return_sums(pieces)


def feed_adam(grads, state, layer, previous):
    seqs, rings = lax.axis_size("seq"), lax.axis_size("fsdp")
    half = state[0].shape[2] // 2
    block = half // (seqs * rings)
    tall = tall_of(block)

    def load(scalars, grads, scratch, total):
        for j in range(rings):
            scratch[0][lax.bitwise_xor(scalars[0][0], jnp.int32(j))] = grads[j][...]
        for f in range(rings):
            for g in range(2):
                for s in range(seqs):
                    start = g * half + (s * rings + f) * block
                    at = (g * seqs + s) * tall
                    piece = scratch[0][f, :, at : at + block]
                    total[:, start : start + block] = piece.astype(jnp.float32)

    return adam_kernel(
        load,
        [place_of("fsdp")],
        grads,
        state,
        layer,
        previous,
        [lambda tile: pltpu.VMEM((rings, tile, 2 * seqs * tall), low)],
    )


def down_adam(parts, state, layer, previous, earlier):
    def load(scalars, grads, scratch, total):
        sums = grads[0][...].astype(jnp.float32)
        for grad in grads[1:]:
            sums = sums + grad[...].astype(jnp.float32)
        total[...] = sums[: total.shape[0]]

    return adam_kernel(load, [], parts, state, layer, previous, earlier=earlier)


def split_down(part):
    seqs = lax.axis_size("seq")
    part = part.reshape(seqs, -1, part.shape[-1])

    def body(place, part, even, odd):
        for i in range(seqs):
            owner = lax.bitwise_xor(place[0], jnp.int32(i))
            (even, odd)[i % 2][i // 2] = part[owner]

    return plain_call(
        body, [shaped((seqs // 2,) + part.shape[1:], part.dtype)] * 2, scalars=1
    )(place_of("seq"), part)


def place_blocks(blocks, owners, place, earlier=()):
    def body(place, *refs):
        if len(blocks[0].shape) == len(refs[-1].shape):
            refs = [ref.at[i] for ref in refs[:-1] for i in range(ref.shape[0])] + [refs[-1]]
        for block, owner in zip(refs, owners(place[0])):
            refs[-1][owner] = block[...]

    shape = blocks[0].shape
    if len(blocks) == 2:
        shape = (2 * shape[0],) + shape[1:]
    else:
        shape = (len(blocks),) + shape
    return plain_call(body, [shaped(shape, blocks[0].dtype)], scalars=1, earlier=earlier)(
        place, *blocks
    )[0]


def vectors_start(gain_weight, tap_weight):
    gains = gain_weight.reshape(2 * LAYERS, -1)
    taps = tap_weight.reshape(3 * LAYERS, -1)
    return gather_fsdp(jnp.concatenate([gains, taps], axis=0).astype(low))


def vectors_middle(blocks):
    rings = lax.axis_size("fsdp")
    both = place_blocks(
        blocks,
        lambda place: [lax.bitwise_xor(place, jnp.int32(j)) for j in range(rings)],
        place_of("fsdp"),
    )
    return both, send_seq(both)


def vectors_end(both, blocks):
    spread = place_blocks(
        blocks,
        lambda place: [lax.bitwise_xor(place, jnp.int32(i)) for i in seq_order()],
        place_of("seq"),
    )
    gains = jnp.transpose(spread[:, :, : 2 * LAYERS], (2, 0, 1, 3)).astype(jnp.float32)
    taps = jnp.transpose(both[:, 2 * LAYERS :], (1, 0, 2)).astype(jnp.float32)
    return gains.reshape(LAYERS, 2, 1, -1), taps.reshape(LAYERS, 3, -1)


def vector_gradients(gain_grads, tap_grads, short):
    seqs, rings = lax.axis_size("seq"), lax.axis_size("fsdp")
    place_seq, place_fsdp = lax.axis_index("seq"), lax.axis_index("fsdp")
    gains = gain_grads.reshape(2 * LAYERS, seqs, -1)
    owner = place_seq ^ jnp.array(seq_order())
    pick = (owner[:, None] == jnp.arange(seqs)[None, :]).astype(jnp.float32)
    gains = jnp.einsum("jo,koc->jkc", pick, gains, precision=lax.Precision.HIGHEST)
    gains = small_scatter_seq(gains)
    taps = tap_grads.reshape(3 * LAYERS, -1)[:, : rings * short]
    both = jnp.concatenate([gains, taps], axis=0).reshape(5 * LAYERS, rings, short)
    owner = place_fsdp ^ jnp.arange(rings)
    pick = (owner[:, None] == jnp.arange(rings)[None, :]).astype(jnp.float32)
    both = jnp.einsum("jo,koc->jkc", pick, both, precision=lax.Precision.HIGHEST)
    both = small_scatter_fsdp(both)
    return (
        both[: 2 * LAYERS].reshape(LAYERS, 2, short),
        both[2 * LAYERS :].reshape(LAYERS, 3, short),
    )


def unit_rows(values):
    row_scale = lax.rsqrt(jnp.mean(values * values, axis=-1, keepdims=True) + eps_norm)
    return values * row_scale, row_scale


def first_norm(inputs, gain, earlier):
    def body(inputs, gain, stream_out, normed_out):
        stream = inputs[...].astype(jnp.float32)
        stream_out[...] = stream
        normed_out[...] = (unit_rows(stream)[0] * gain[...]).astype(low)

    return plain_call(
        body, [shaped(inputs.shape), shaped(inputs.shape, low)], earlier=earlier
    )(inputs, gain)


def finish(base, sums, gain, earlier=(), carried=()):
    def body(*refs):
        total = refs[0][...]
        for part in refs[1 : 1 + len(sums)]:
            total = total + part[...].astype(jnp.float32)
        if gain is None:
            refs[-1][...] = total.astype(low)
        else:
            refs[-2][...] = total
            refs[-1][...] = (unit_rows(total)[0] * refs[1 + len(sums)][...]).astype(low)

    if gain is None:
        return plain_call(body, [shaped(base.shape, low)])(base, *sums)[0]
    return plain_call(
        body,
        [shaped(base.shape), shaped(base.shape, low)],
        earlier=earlier,
        carried=carried,
    )(base, *sums, gain)


def finish_back(flow, sums, stream, gain, carried=(), earlier=()):
    def body(flow, stream, gain, *refs):
        total = refs[0][...].astype(jnp.float32)
        for part in refs[1 : len(sums)]:
            total = total + part[...].astype(jnp.float32)
        unit, row_scale = unit_rows(stream[...])
        scaled = total * gain[...]
        inner_mean = jnp.mean(scaled * unit, axis=-1, keepdims=True)
        result = flow[...].astype(jnp.float32) + row_scale * (scaled - unit * inner_mean)
        refs[-3][...] = result
        refs[-2][...] = result.astype(low)
        refs[-1][...] = jnp.sum(total * unit, axis=0, keepdims=True)

    return plain_call(
        body,
        [shaped(flow.shape), shaped(flow.shape, low), shaped((1, flow.shape[1]))],
        carried=carried,
        earlier=earlier,
    )(flow, stream, gain, *sums)


def pair_sum(even, received, earlier=()):
    half, tokens, features = even.shape

    def body(even, received, *outs):
        for i in range(half):
            total = even[i] + received[i].astype(jnp.float32)
            outs[i][...] = total.astype(outs[i].dtype)

    outs = plain_call(
        body,
        [shaped((tokens, features))] + [shaped((tokens, features), low)] * (half - 1),
        earlier=earlier,
    )(even, received)
    return [outs[0]] + [seq_swap(outs[i], 2 * i) for i in range(1, half)]


def block_neighbour(place, i, count, step):
    order = list(range(0, count, 2)) + list(range(1, count, 2))
    owner = lax.bitwise_xor(place, jnp.int32(order[i])) + step
    inside = jnp.logical_and(owner >= 0, owner < count)
    number = lax.bitwise_xor(place, jnp.where(inside, owner, place))
    return lax.div(number, 2) + lax.rem(number, 2) * (count // 2), inside


def conv_forward(place, taps, gated, i, count):
    here = gated[i]
    tokens, chunk = here.shape
    at, inside = block_neighbour(place, i, count, -1)
    before = jnp.where(inside, gated[at, tokens - 8 :, :], 0.0)
    row = lax.broadcasted_iota(jnp.int32, (tokens, chunk), 0)
    last, second = before[7:8, :], before[6:7, :]
    one = jnp.where(row == 0, last, pltpu.roll(here, 1, 0))
    two = jnp.where(row == 0, second, jnp.where(row == 1, last, pltpu.roll(here, 2, 0)))
    return taps[0:1, :] * two + taps[1:2, :] * one + taps[2:3, :] * here, one, two


def mixer_forward(blocks, inner, outer, taps):
    half, tokens, features = blocks[0].shape
    count = 2 * half
    chunk = outer.shape[0]
    wide = inner.shape[1] // 3

    def body(place, even_in, odd_in, inner, outer, taps, *refs):
        projected, even, odd, gated, mixed = refs
        for k, rows in enumerate((even_in, odd_in)):
            rows = rows[...].reshape(half * tokens, features)
            for g in range(3):
                columns = slice(g * wide, (g + 1) * wide)
                part = dot(rows, inner[:, columns]).reshape(half, tokens, wide)
                projected[k * half : (k + 1) * half, :, columns] = part

        for i in range(count):
            product = projected[i, :, :wide] * projected[i, :, 2 * wide :]
            gated[i] = product[:, :chunk].astype(low).astype(jnp.float32)
        taps = taps[...]
        for i in range(count):
            conv_out = conv_forward(place[0], taps, gated, i, count)[0]
            mixed[i] = (projected[i, :, wide : wide + chunk] * conv_out).astype(low)
        rows = mixed[:half].reshape(half * tokens, chunk)
        even[...] = dot(rows, outer[...]).reshape(half, tokens, features)
        rows = mixed[half:].reshape(half * tokens, chunk)
        odd[...] = dot(rows, outer[...]).reshape(half, tokens, features).astype(low)

    return plain_call(
        body,
        [
            shaped((count, tokens, 3 * wide)),
            shaped((half, tokens, features)),
            shaped((half, tokens, features), low),
        ],
        scalars=1,
        scratch=[
            pltpu.VMEM((count, tokens, chunk), jnp.float32),
            pltpu.VMEM((count, tokens, chunk), low),
        ],
    )(place_of("seq"), *blocks, inner, outer, taps)


def mixer_backward(blocks, projected, inner, outer, taps):
    half, tokens, features = blocks[0].shape
    count = 2 * half
    chunk = outer.shape[0]
    wide = inner.shape[1] // 3

    def body(place, even_in, odd_in, projected, inner, outer, taps, *refs):
        even, odd, flows, mixed, tap_out, gated, flow = refs
        for i in range(count):
            product = projected[i, :, :wide] * projected[i, :, 2 * wide :]
            gated[i] = product[:, :chunk].astype(low).astype(jnp.float32)
        taps = taps[...]
        tap_sums = [jnp.zeros((1, chunk), jnp.float32)] * 3
        for k in range(2):
            rows = (even_in, odd_in)[k][...].reshape(half * tokens, features)
            back = dot(rows, outer[...], nt).reshape(half, tokens, chunk)
            for i in range(k * half, (k + 1) * half):
                conv_out, one, two = conv_forward(place[0], taps, gated, i, count)
                gate = projected[i, :, wide : wide + chunk]
                mixed[i] = (gate * conv_out).astype(low)
                mixed_flow = back[i - k * half]
                conv_flow = mixed_flow * gate
                flow[i] = conv_flow
                for j, shifted in enumerate((two, one, gated[i])):
                    term = jnp.sum(conv_flow * shifted, axis=0, keepdims=True)
                    tap_sums[j] = tap_sums[j] + term
                flows[i, :, wide : wide + chunk] = (mixed_flow * conv_out).astype(low)
        for j in range(3):
            tap_out[j : j + 1, :] = tap_sums[j]
        row = lax.broadcasted_iota(jnp.int32, (tokens, chunk), 0)
        for i in range(count):
            here = flow[i]
            at, inside = block_neighbour(place[0], i, count, 1)
            beyond = jnp.where(inside, flow[at, :8, :], 0.0)
            first, second = beyond[0:1, :], beyond[1:2, :]
            one = jnp.where(row == tokens - 1, first, pltpu.roll(here, tokens - 1, 0))
            two = jnp.where(
                row == tokens - 1,
                second,
                jnp.where(row == tokens - 2, first, pltpu.roll(here, tokens - 2, 0)),
            )
            gated_flow = taps[2:3, :] * here + taps[1:2, :] * one + taps[0:1, :] * two
            x_part = projected[i, :, 2 * wide : 2 * wide + chunk]
            b_part = projected[i, :, :chunk]
            flows[i, :, :chunk] = (gated_flow * x_part).astype(low)
            flows[i, :, 2 * wide : 2 * wide + chunk] = (gated_flow * b_part).astype(low)
            if wide > chunk:
                for g in range(3):
                    gap = jnp.zeros((tokens, wide - chunk), low)
                    flows[i, :, g * wide + chunk : (g + 1) * wide] = gap
        rows = flows[:half].reshape(half * tokens, 3 * wide)
        even[...] = dot(rows, inner[...], nt).reshape(half, tokens, features)
        rows = flows[half:].reshape(half * tokens, 3 * wide)
        odd[...] = dot(rows, inner[...], nt).reshape(half, tokens, features).astype(low)

    return plain_call(
        body,
        [
            shaped((half, tokens, features)),
            shaped((half, tokens, features), low),
            shaped((count, tokens, 3 * wide), low),
            shaped((count, tokens, chunk), low),
            shaped((3, chunk)),
        ],
        scalars=1,
        scratch=[pltpu.VMEM((count, tokens, chunk), jnp.float32)] * 2,
    )(place_of("seq"), *blocks, projected, inner, outer, taps)


def mixer_grads(normed, flows, mixed, lows, rows):
    seqs, rings = lax.axis_size("seq"), lax.axis_size("fsdp")
    features, width = normed[0].shape[-1], flows.shape[-1]
    half = normed[0].shape[0]
    wide = width // 3
    count = features // width

    def body(place, normed_even, normed_odd, flows, mixed, low_even, low_odd, *refs):
        outs, inner, outer = refs[:rings], refs[rings], refs[rings + 1]
        long = lambda array: array.reshape(-1, array.shape[-1])
        for g in range(3):
            at = slice(g * wide, (g + 1) * wide)
            part = dot(long(normed_even[...]), long(flows[:half, :, at]), tn)
            part = part + dot(long(normed_odd[...]), long(flows[half:, :, at]), tn)
            part = part.astype(low)
            for i in range(seqs * rings):
                inner[i // rings, i % rings, :, at] = part[i * rows : (i + 1) * rows]
        part = dot(long(mixed[:half]), long(low_even[...]), tn)
        part = part + dot(long(mixed[half:]), long(low_odd[...]), tn)
        part = part.astype(low)
        for f in range(rings):
            outer[f] = part[f * rows : (f + 1) * rows]
        for j in range(rings):
            f = lax.bitwise_xor(place[0], jnp.int32(j))
            for s in range(seqs):
                outs[j][s] = inner[s, f]
            for i in range(count):
                outs[j][seqs + i] = outer[f, :, i * width : (i + 1) * width]

    return plain_call(
        body,
        [shaped((seqs + count, rows, width), low)] * rings,
        scalars=1,
        scratch=[
            pltpu.VMEM((seqs, rings, rows, width), low),
            pltpu.VMEM((rings, rows, features), low),
        ],
        cost=(24 * half * normed[0].size, 8 * normed[0].size),
    )(place_of("fsdp"), *normed, flows, mixed, *lows)


def hidden_tile(hidden):
    return 256 if hidden % 256 == 0 else 128


def feed_specs(features, hidden):
    tile = hidden_tile(hidden)
    steps = hidden // tile
    return (
        pl.BlockSpec((features, tile), lambda i: (0, i)),
        pl.BlockSpec((features, tile), lambda i: (0, i + steps)),
        pl.BlockSpec((tile, features), lambda i: (i, 0)),
    )


def feed_forward(blocks, up_matrix, down, own):
    count = len(blocks)
    tokens, features = blocks[0].shape
    hidden = down.shape[0]
    tile = hidden_tile(hidden)
    steps = hidden // tile

    def body(*refs):
        gate_matrix, up_matrix, down = refs[count : count + 3]
        outs = refs[count + 3 : 2 * count + 3]
        gate_out, up_out, hidden_out, rows, total = refs[2 * count + 3 :]
        step = pl.program_id(0)

        @pl.when(step == 0)
        def _():
            for i in range(count):
                rows[i * tokens : (i + 1) * tokens] = refs[i][...]
            total[...] = jnp.zeros_like(total)

        gate = dot(rows[...], gate_matrix[...])
        up = dot(rows[...], up_matrix[...])
        gate_out[...] = gate
        up_out[...] = up
        value = (gate * jax.nn.sigmoid(gate) * up).astype(low)
        hidden_out[...] = value
        total[...] += dot(value, down[...])

        @pl.when(step == steps - 1)
        def _():
            for i in range(count):
                outs[i][...] = total[i * tokens : (i + 1) * tokens].astype(outs[i].dtype)

    columns = pl.BlockSpec((count * tokens, tile), lambda i: (0, i))
    outs = kernel_call(
        body,
        (steps,),
        [whole((tokens, features))] * count + list(feed_specs(features, hidden)),
        [whole((tokens, features))] * count + [columns] * 3,
        [
            shaped((tokens, features), jnp.float32 if own and i == 0 else low)
            for i in range(count)
        ]
        + [shaped((count * tokens, hidden), kind) for kind in (jnp.float32, jnp.float32, low)],
        scratch=[
            pltpu.VMEM((count * tokens, features), low),
            pltpu.VMEM((count * tokens, features), jnp.float32),
        ],
    )(*blocks, up_matrix, up_matrix, down)
    return outs[:count], outs[count:]


def feed_backward(blocks, gates, ups, up_matrix, down, own):
    count = len(blocks)
    tokens, features = blocks[0].shape
    hidden = down.shape[0]
    tile = hidden_tile(hidden)
    steps = hidden // tile

    def body(*refs):
        gate_part, up_part, gate_matrix, up_matrix, down = refs[count : count + 5]
        outs = refs[count + 5 : 2 * count + 5]
        gate_out, up_out, rows, total = refs[2 * count + 5 :]
        step = pl.program_id(0)

        @pl.when(step == 0)
        def _():
            for i in range(count):
                rows[i * tokens : (i + 1) * tokens] = refs[i][...]
            total[...] = jnp.zeros_like(total)

        flow = dot(rows[...], down[...], nt)
        gate = gate_part[...]
        smooth = jax.nn.sigmoid(gate)
        gate_flow = flow * up_part[...] * (smooth * (1.0 + gate * (1.0 - smooth)))
        gate_flow = gate_flow.astype(low)
        up_flow = (flow * (gate * smooth)).astype(low)
        gate_out[...] = gate_flow
        up_out[...] = up_flow
        total[...] += dot(gate_flow, gate_matrix[...], nt) + dot(up_flow, up_matrix[...], nt)

        @pl.when(step == steps - 1)
        def _():
            for i in range(count):
                outs[i][...] = total[i * tokens : (i + 1) * tokens].astype(outs[i].dtype)

    columns = pl.BlockSpec((count * tokens, tile), lambda i: (0, i))
    outs = kernel_call(
        body,
        (steps,),
        [whole((tokens, features))] * count + [columns] * 2 + list(feed_specs(features, hidden)),
        [whole((tokens, features))] * count + [columns] * 2,
        [
            shaped((tokens, features), jnp.float32 if own and i == 0 else low)
            for i in range(count)
        ]
        + [shaped((count * tokens, hidden), low)] * 2,
        scratch=[
            pltpu.VMEM((count * tokens, features), low),
            pltpu.VMEM((count * tokens, features), jnp.float32),
        ],
    )(*blocks, gates, ups, up_matrix, up_matrix, down)
    return outs[:count], outs[count:]


def feed_grads(normed, gate_flows, up_flows):
    count, groups = len(normed), len(gate_flows)
    tokens, features = normed[0].shape
    hidden = gate_flows[0].shape[1]
    sizes = [flow.shape[0] for flow in gate_flows]
    starts = [sum(sizes[:i]) for i in range(groups)]
    tile = hidden_tile(hidden)
    steps = hidden // tile

    def body(*refs):
        flows = refs[count : count + 2 * groups]
        out, rows, columns = refs[count + 2 * groups :]
        step = pl.program_id(0)

        @pl.when(step == 0)
        def _():
            for i in range(count):
                rows[i * tokens : (i + 1) * tokens] = refs[i][...]

        for half in range(2):

            @pl.when(lax.div(step, steps) == half)
            def _():
                for i in range(groups):
                    at = slice(starts[i], starts[i] + sizes[i])
                    columns[at] = flows[half * groups + i][...]

        out[...] = dot(rows[...], columns[...], tn).astype(low)

    gate_specs = [
        pl.BlockSpec((size, tile), lambda i: (0, jnp.minimum(i, steps - 1))) for size in sizes
    ]
    up_specs = [
        pl.BlockSpec((size, tile), lambda i: (0, jnp.maximum(i - steps, 0))) for size in sizes
    ]
    return kernel_call(
        body,
        (2 * steps,),
        [whole((tokens, features))] * count + gate_specs + up_specs,
        pl.BlockSpec((features, tile), lambda i: (0, i)),
        shaped((features, 2 * hidden), low),
        scratch=[
            pltpu.VMEM((count * tokens, features), low),
            pltpu.VMEM((count * tokens, tile), low),
        ],
        cost=(12 * count * tokens * features * hidden, 24 * features * hidden),
    )(*normed, *gate_flows, *up_flows)


def down_grads(hiddens, flows):
    count, groups = len(flows), len(hiddens)
    tokens, features = flows[0].shape
    hidden = hiddens[0].shape[1]
    sizes = [values.shape[0] for values in hiddens]
    starts = [sum(sizes[:i]) for i in range(groups)]
    tile = hidden_tile(hidden)

    def body(*refs):
        hiddens = refs[count : count + groups]
        out, rows, columns = refs[count + groups :]

        @pl.when(pl.program_id(0) == 0)
        def _():
            for i in range(count):
                rows[i * tokens : (i + 1) * tokens] = refs[i][...]

        for i in range(groups):
            columns[starts[i] : starts[i] + sizes[i]] = hiddens[i][...]
        out[...] = dot(columns[...], rows[...], tn).astype(low)

    return kernel_call(
        body,
        (hidden // tile,),
        [whole((tokens, features))] * count
        + [pl.BlockSpec((size, tile), lambda i: (0, i)) for size in sizes],
        pl.BlockSpec((tile, features), lambda i: (i, 0)),
        shaped((hidden, features), low),
        scratch=[
            pltpu.VMEM((count * tokens, features), low),
            pltpu.VMEM((count * tokens, tile), low),
        ],
        cost=(6 * count * tokens * features * hidden, 12 * features * hidden),
    )(*flows, *hiddens)


def join_blocks(blocks):
    def body(*refs):
        for i in range(len(blocks)):
            refs[len(blocks) + i][...] = refs[i][...]

    return plain_call(body, [shaped(block.shape, block.dtype) for block in blocks])(*blocks)


def groups_of(blocks):
    return [blocks[:2]] + [[block] for block in blocks[2:]]


def return_sums(sums):
    return [sums[0]] + [fsdp_swap(sums[j], j) for j in range(1, len(sums))]


def adam_update(weight, first, second, gradient, rate, decay):
    first_new = beta_one * first + (1.0 - beta_one) * gradient
    second_new = beta_two * second + (1.0 - beta_two) * gradient * gradient
    first_hat = first_new / (1.0 - beta_one**STEP)
    second_hat = second_new / (1.0 - beta_two**STEP)
    weight_new = weight - rate * (first_hat / (jnp.sqrt(second_hat) + eps_adam) + decay * weight)
    return (first_new, second_new, weight_new)


def local(
    inputs,
    cotangent,
    mix_weight,
    mix_first,
    mix_second,
    feed_weight,
    feed_first,
    feed_second,
    down_weight,
    down_first,
    down_second,
    gain_weight,
    gain_first,
    gain_second,
    tap_weight,
    tap_first,
    tap_second,
):
    sequences, length, features = inputs.shape
    seqs, rings = lax.axis_size("seq"), lax.axis_size("fsdp")
    rows = mix_weight.shape[1]
    chunk = features // seqs
    wide = -(-chunk // 128) * 128
    cotangent = cotangent.reshape(-1, features)
    Order.mark = jnp.zeros(mark_shape.shape, mark_shape.dtype)

    mixes, feeds = [None] * LAYERS, [None] * LAYERS
    vector_blocks = vectors_start(gain_weight, tap_weight)
    feed_swap = swap_feed(pack_feed(feed_weight, 0))
    mix_packed = pack_mix(mix_weight, 0, wide, vector_blocks[1:])
    mix_swap = swap_mix(mix_packed)
    down_rows = gather_rows(pack_down(down_weight, 0))
    both, vector_blocks = vectors_middle(vector_blocks)
    mix_pieces = gather_fsdp(join_mix(mix_swap, mix_packed))
    feed_part = assemble_feed(feed_swap)
    later_packed = pack_mix(mix_weight, 1, wide)
    later_swap = swap_mix(later_packed)
    vector_blocks = stack_pairs(vector_blocks)
    later_piece = join_mix(later_swap, later_packed, mix_pieces[1:2])
    gain_rows, tap_rows = vectors_end(both, vector_blocks)
    stream, normed = first_norm(
        inputs.reshape(-1, features), gain_rows[0, 0], mix_pieces[2:3]
    )
    blocks = send_seq(normed)
    later_feed = pack_feed(feed_weight, 1)
    *blocks, feed_part = stack_pairs(blocks, mix_pieces[3:], [feed_part])
    feeds[0] = (gather_rows(feed_part), down_rows)
    mixes[0] = assemble_mix(mix_pieces, wide, features)
    later_mix = [None, None, fsdp_swap(later_piece, 2)] if rings > 2 else [None, None]
    later_feed = swap_feed(later_feed)

    kept = []
    for layer in range(LAYERS):
        last = layer + 1 == LAYERS
        gathered = blocks
        projected, even, odd = mixer_forward(blocks, *mixes[layer], tap_rows[layer])
        odd = seq_swap(odd, 1)
        if last:
            flow_blocks = gather_fsdp(cotangent)
        sums = pair_sum(even, odd)
        if last:
            flow_low = join_blocks(flow_blocks)
            middle, normed_two = finish(stream, sums, gain_rows[layer, 1])
        else:
            middle, normed_two, later_piece, down_packed = finish(
                stream,
                sums,
                gain_rows[layer, 1],
                (*later_mix[2:], *later_feed[1:]),
                (later_piece, pack_down(down_weight, 1)),
            )
        two_blocks = gather_fsdp(normed_two)
        if not last:
            later_mix[0] = later_piece
            later_mix[1] = fsdp_swap(later_piece, 1)
            feeds[1] = (gather_rows(assemble_feed(later_feed)), gather_rows(down_packed))
        sums, values = [], []
        for number, group in enumerate(groups_of(two_blocks)):
            outs, saved = feed_forward(group, *feeds[layer], number == 0)
            sums += outs
            values.append(saved)
        kept.append((stream, middle, gathered, projected, two_blocks, values))
        sums = return_sums(sums)
        if not last:
            stream, normed, later_piece = finish(
                middle, sums, gain_rows[layer + 1, 0], later_mix[1:2], [later_piece]
            )
            blocks = send_seq(normed)
            later_mix += [fsdp_swap(later_piece, by) for by in range(3, rings)]
            blocks = stack_pairs(blocks)
            mixes[1] = assemble_mix(later_mix, wide, features)

    states = (
        (mix_weight, mix_first, mix_second),
        (feed_weight, feed_first, feed_second),
        (down_weight, down_first, down_second),
    )
    new = [None] * 3
    gain_grads, tap_grads = [None] * LAYERS, [None] * LAYERS
    flow = cotangent
    later_mix = ()
    for layer in reversed(range(LAYERS)):
        last = layer + 1 == LAYERS
        stream, middle, gathered, projected, two_blocks, values = kept[layer]
        back_sums, gate_flows, up_flows = [], [], []
        for number, group in enumerate(groups_of(flow_low)):
            gates, ups, _ = values[number]
            outs, (gate_flow, up_flow) = feed_backward(
                group, gates, ups, *feeds[layer], number == 0
            )
            back_sums += outs
            gate_flows.append(gate_flow)
            up_flows.append(up_flow)
        if last:
            outputs = finish(middle, sums, None).reshape(inputs.shape)
        back_sums = return_sums(back_sums)
        down_part = down_grads([value[2] for value in values], flow_low)
        middle_flow, middle_low, gain_two, down_part, *later_mix = finish_back(
            flow, back_sums, middle, gain_rows[layer, 1], [down_part, *later_mix]
        )
        later_mix = return_sums(later_mix) if later_mix else later_mix
        if last:
            down_part = [scatter_rows(down_part)]
        blocks = send_seq(middle_low)
        feed_part = feed_grads(two_blocks, gate_flows, up_flows)
        if not last:
            later_feed = split_feed(later_feed, rows)
        even, odd, feed_part = stack_pairs(
            blocks, () if last else later_mix[2:3], [feed_part]
        )
        feed_part = scatter_rows(feed_part)
        blocks = even, odd
        even, odd, flows, mixed, tap_grads[layer] = mixer_backward(
            blocks, projected, *mixes[layer], tap_rows[layer]
        )
        sums = pair_sum(even, seq_swap(odd, 1), () if last else later_mix[3:])
        mix_part = mixer_grads(gathered, flows, mixed, blocks, rows)
        flow, low_flow, gain_one, *mix_part = finish_back(
            middle_flow, sums, stream, gain_rows[layer, 0], mix_part, () if last else later_feed[1:]
        )
        if not last:
            mix_part = return_sums(mix_part)
        gain_grads[layer] = jnp.concatenate([gain_one, gain_two])
        if last:
            flow_low = gather_fsdp(low_flow)
            later_mix, later_feed, later_down = mix_part, feed_part, down_part
    later_mix = mix_reduce(later_mix)
    new[1] = feed_adam(later_feed, states[1], 1, new[1])
    even, odd = split_down(down_part)
    odd = seq_swap(odd, 1)
    new[2] = down_adam(later_down, states[2], 1, new[2], mix_part[2:3])
    down_part = pair_sum(even, odd)
    gain_grad, tap_grad = vector_gradients(
        jnp.stack(gain_grads), jnp.stack(tap_grads), gain_weight.shape[-1]
    )
    new[0] = mix_adam(later_mix, states[0], 1, new[0], wide)
    feed_part = split_feed(feed_part, rows)
    mix_part = mix_reduce(mix_part)
    new[2] = down_adam(down_part, states[2], 0, new[2], ())
    new[1] = feed_adam(feed_part, states[1], 0, new[1])
    new[0] = mix_adam(mix_part, states[0], 0, new[0], wide)
    input_grad = flow.reshape(sequences, length, features)
    gain_new = adam_update(gain_weight, gain_first, gain_second, gain_grad, rate_vector, 0.0)
    tap_new = adam_update(tap_weight, tap_first, tap_second, tap_grad, rate_vector, 0.0)
    matrices = [(part[1], part[2], part[0]) for part in new]
    return (outputs, input_grad, *sum(matrices, ()), *gain_new, *tap_new)


def solution(mesh):
    tokens = P("fsdp", "seq", None)
    rows = P(None, ("seq", "fsdp"), None)
    last = P(None, None, ("seq", "fsdp"))
    return jax.shard_map(
        local,
        mesh=mesh,
        in_specs=(tokens,) * 2 + (rows,) * 9 + (last,) * 6,
        out_specs=(tokens,) * 2 + (rows,) * 9 + (last,) * 6,
        check_vma=False,
    )
```

```python
import math

import jax
import jax.numpy as jnp
from jax import lax
from jax.experimental import pallas as pl
from jax.experimental.pallas import tpu as pltpu
from jax.sharding import PartitionSpec as P

LAYERS = 2
STEP = 10

eps_norm = 1e-05
eps_adam = 1e-08
beta_one = 0.9
beta_two = 0.95
rate_matrix = 0.05
rate_vector = 0.6
decay_matrix = 0.1

low = jnp.bfloat16


def dot(left, right, sides=((1,), (0,))):
    return lax.dot_general(left, right, (sides, ((), ())), preferred_element_type=jnp.float32)


nt = ((1,), (1,))
tn = ((0,), (0,))


def seq_order():
    count = lax.axis_size("seq")
    return list(range(0, count, 2)) + list(range(1, count, 2))


def seq_swap(array, by):
    count = lax.axis_size("seq")
    return lax.ppermute(array, "seq", [(i, i ^ by) for i in range(count)])


def send_seq(array):
    return [array] + [seq_swap(array, by) for by in range(2, lax.axis_size("seq"), 2)]


def fsdp_swap(array, by):
    count = lax.axis_size("fsdp")
    return lax.ppermute(array, "fsdp", [(i, i ^ by) for i in range(count)])


def gather_fsdp(array):
    count = lax.axis_size("fsdp")
    return [array] + [fsdp_swap(array, by) for by in range(1, count)]


def small_scatter_seq(parts):
    half = parts.shape[0] // 2
    total = parts[:half] + seq_swap(parts[half:], 1)
    for i in range(1, half):
        total = total.at[0].add(seq_swap(total[i], 2 * i))
    return total[0]


def small_scatter_fsdp(parts):
    total = parts[0]
    for by in range(1, parts.shape[0]):
        total = total + fsdp_swap(parts[by], by)
    return total


def stack_pairs(blocks, earlier=(), carried=()):
    def body(*refs):
        for i in range(len(blocks)):
            refs[-1][i] = refs[i][...]

    shape = (len(blocks),) + blocks[0].shape
    even, *rest = plain_call(
        body, [shaped(shape, blocks[0].dtype)], earlier=earlier, carried=carried
    )(*blocks)
    return even, seq_swap(even, 1), *rest


def pad_last(array, width):
    return jnp.pad(array, [(0, 0)] * (array.ndim - 1) + [(0, width - array.shape[-1])])


def place_of(axis):
    return lax.axis_index(axis).astype(jnp.int32).reshape(1)


scalar = pl.BlockSpec(memory_space=pltpu.SMEM)
held = pl.BlockSpec(memory_space=pltpu.VMEM)


def shaped(shape, kind=jnp.float32):
    return jax.ShapeDtypeStruct(shape, kind)


class Order:
    mark = None


mark_shape = jax.ShapeDtypeStruct((8, 128), jnp.float32)
anywhere = pl.BlockSpec(memory_space=pl.ANY)


def bytes_of(shape, kind):
    return math.prod(shape) * jnp.dtype(kind).itemsize


def vmem_of(operands, in_specs, out_shape, out_specs, scratch, grid):
    total = 0
    for array, spec in [*zip(operands, in_specs), *zip(out_shape, out_specs)]:
        if spec is anywhere or spec is scalar:
            continue
        if grid:
            total += 2 * bytes_of(spec.block_shape, array.dtype)
        else:
            total += bytes_of(array.shape, array.dtype)
    for array in scratch:
        total += bytes_of(array.shape, array.dtype)
    return total + total // 2 + 4 * 1024 * 1024


def ordered_call(body, operands, in_specs, out_specs, out_shape, aliases, scratch, grid, cost):
    given, made = len(operands), len(out_shape)

    def marked(*refs):
        body(*refs[:given], *refs[given + 1 : given + 1 + made], *refs[given + 2 + made :])

    outs = pl.pallas_call(
        marked,
        in_specs=list(in_specs) + [anywhere],
        out_specs=list(out_specs) + [anywhere],
        out_shape=list(out_shape) + [mark_shape],
        scratch_shapes=list(scratch),
        input_output_aliases=aliases,
        compiler_params=pltpu.CompilerParams(
            vmem_limit_bytes=56 << 20
            if cost[0]
            else min(vmem_of(operands, in_specs, out_shape, out_specs, scratch, grid), 60 << 20)
        ),
        cost_estimate=pl.CostEstimate(
            flops=cost[0], bytes_accessed=cost[1], transcendentals=0
        ),
        **grid,
    )(*operands, Order.mark)
    Order.mark = outs[-1]
    return outs[:-1]


def kernel_call(
    body, grid, in_specs, out_specs, out_shape, aliases=None, scratch=(), cost=(0, 0)
):
    single = not isinstance(out_shape, list)

    def run(*operands):
        outs = ordered_call(
            body,
            operands,
            in_specs,
            [out_specs] if single else out_specs,
            [out_shape] if single else out_shape,
            aliases or {},
            scratch,
            dict(grid=grid),
            cost,
        )
        return outs[0] if single else outs

    return run


def plain_call(
    body, out_shape, scalars=0, scratch=(), earlier=(), carried=(), cost=(0, 0)
):
    def run(*operands):
        given, made, more = len(operands), len(out_shape), len(earlier) + len(carried)

        def rest(*refs):
            outs = refs[given + more :]
            body(*refs[:given], *outs[:made], *outs[made + len(carried) :])

        first = given + len(earlier)
        return ordered_call(
            rest,
            (*operands, *earlier, *carried),
            [scalar] * scalars + [held] * (given - scalars) + [anywhere] * more,
            [held] * made + [anywhere] * len(carried),
            [*out_shape, *(jax.ShapeDtypeStruct(x.shape, x.dtype) for x in carried)],
            {first + i: made + i for i in range(len(carried))},
            scratch,
            {},
            cost,
        )

    return run


def whole(shape):
    return pl.BlockSpec(shape, lambda i: (0,) * len(shape))


def pack_mix(mix_weight, layer, earlier=()):
    seqs = lax.axis_size("seq")
    rows, columns = mix_weight.shape[1:]
    features = columns // 4
    chunk = features // seqs

    def body(place, weight, *refs):
        out = refs[-1]
        for s in range(seqs):
            slot = lax.bitwise_xor(place[0], jnp.int32(s))
            for g in range(4):
                start = g * features + s * chunk
                piece = weight[0, :, start : start + chunk].astype(low)
                out[slot if g < 3 else s, :, g * chunk : (g + 1) * chunk] = piece

    shape = (seqs, rows, 4 * chunk)
    return kernel_call(
        body,
        (1,),
        [scalar, pl.BlockSpec((1, rows, columns), lambda i: (layer, 0, 0))]
        + [anywhere] * len(earlier),
        whole(shape),
        jax.ShapeDtypeStruct(shape, low),
    )(place_of("seq"), mix_weight, *earlier)


def assemble_mix(pieces, wide):
    rings = len(pieces)
    seqs, rows, width = pieces[0].shape
    chunk = width // 4
    features = seqs * chunk

    def body(place_seq, place_fsdp, *refs):
        inner_out, outer_out = refs[rings:]
        for j in range(rings):
            f = lax.bitwise_xor(place_fsdp[0], jnp.int32(j))
            for s in range(seqs):
                owner = lax.bitwise_xor(place_seq[0], jnp.int32(s))
                for g in range(3):
                    piece = refs[j][s, :, g * chunk : (g + 1) * chunk]
                    if wide > chunk:
                        gap = jnp.zeros((rows, wide - chunk), low)
                        piece = jnp.concatenate([piece, gap], axis=1)
                    inner_out[owner, f, :, g * wide : (g + 1) * wide] = piece
                outer_out[f, :, s * chunk : (s + 1) * chunk] = refs[j][s, :, 3 * chunk :]

    inner_shape = (seqs, rings, rows, 3 * wide)
    outer_shape = (rings, rows, features)
    inner, out = plain_call(
        body, [shaped(inner_shape, low), shaped(outer_shape, low)], scalars=2
    )(place_of("seq"), place_of("fsdp"), *pieces)
    return inner.reshape(features, 3 * wide), out.reshape(rings * rows, features)


def swap_mix(packed):
    seqs = lax.axis_size("seq")
    return [packed[:1]] + [seq_swap(packed[by : by + 1], by) for by in range(1, seqs)]


def join_mix(parts, packed, earlier=()):
    seqs = len(parts)

    def body(*refs):
        out = refs[-1]
        split = out.shape[-1] // 4 * 3
        for s in range(seqs):
            out[s, :, :split] = refs[s][0, :, :split]
            out[s, :, split:] = refs[seqs][s, :, split:]

    return plain_call(body, [shaped(packed.shape, low)], earlier=earlier)(*parts, packed)[0]


def tall_of(block):
    step = 128 // min(lax.axis_size("seq"), 128)
    return -(-block // step) * step


def pack_feed(feed_weight, layer):
    seqs, rings = lax.axis_size("seq"), lax.axis_size("fsdp")
    rows, columns = feed_weight.shape[1:]
    half = columns // 2
    block = half // (seqs * rings)
    tall = tall_of(block)

    def body(place, weight, out):
        for f in range(rings):
            slot = lax.bitwise_xor(place[0], jnp.int32(f))
            for g in range(2):
                for s in range(seqs):
                    start = g * half + (s * rings + f) * block
                    piece = weight[0, :, start : start + block].astype(low)
                    if tall > block:
                        piece = jnp.concatenate(
                            [piece, jnp.zeros((rows, tall - block), low)], axis=1
                        )
                    to = (g * seqs + s) * tall
                    out[slot, :, to : to + tall] = piece

    shape = (rings, rows, 2 * seqs * tall)
    return kernel_call(
        body,
        (1,),
        [scalar, pl.BlockSpec((1, rows, columns), lambda i: (layer, 0, 0))],
        whole(shape),
        jax.ShapeDtypeStruct(shape, low),
    )(place_of("fsdp"), feed_weight)


def assemble_feed(pieces):
    rings = len(pieces)

    def body(place, *refs):
        out = refs[rings]
        for j in range(rings):
            out[lax.bitwise_xor(place[0], jnp.int32(j))] = refs[j][0]

    shape = (rings,) + pieces[0].shape[1:]
    return kernel_call(
        body,
        (1,),
        [scalar] + [whole(piece.shape) for piece in pieces],
        whole(shape),
        jax.ShapeDtypeStruct(shape, low),
    )(place_of("fsdp"), *pieces)


def swap_feed(packed):
    rings = lax.axis_size("fsdp")
    return [packed[:1]] + [fsdp_swap(packed[by : by + 1], by) for by in range(1, rings)]


def gather_rows(part):
    return lax.all_gather(part.reshape(-1, part.shape[-1]), "seq", axis=0, tiled=True)


def pack_down(down_weight, layer):
    block = down_weight.shape[1]
    return jnp.pad(down_weight[layer].astype(low), ((0, tall_of(block) - block), (0, 0)))


def adam_kernel(load, scalars, grads, state, layer, previous, scratch=(), earlier=()):
    weight = state[0]
    rows, columns = weight.shape[1:]
    tile = 16 if rows % 16 == 0 else rows
    width = 768
    steps = rows // tile
    if layer is None:
        each = steps
        where = lambda i: (lax.div(i, each), lax.rem(i, each), 0)
        specs = [pl.BlockSpec((1, tile, grad.shape[-1]), where) for grad in grads]
        steps = LAYERS * each
    else:
        where = lambda i: (layer, i, 0)
        specs = [
            pl.BlockSpec(
                grad.shape if tile == rows else (tile, grad.shape[-1]), lambda i: (i, 0)
            )
            for grad in grads
        ]
    part = pl.BlockSpec((1, tile, columns), where)
    kept = (0 if previous is None else 3) + len(earlier)
    before = len(scalars) + len(grads)

    def body(*refs):
        weight, first, second = refs[before : before + 3]
        weight_out, first_out, second_out, total = refs[before + 3 + kept : before + 7 + kept]
        load(refs[: len(scalars)], refs[len(scalars) : before], refs[before + 7 + kept :], total)
        for start in range(0, columns, width):
            at = slice(start, start + width)
            gradient = total[:, at]
            old = weight[0, :, at]
            first_new = beta_one * first[0, :, at] + (1.0 - beta_one) * gradient
            second_new = beta_two * second[0, :, at] + (1.0 - beta_two) * gradient * gradient
            first_hat = first_new / (1.0 - beta_one**STEP)
            second_hat = second_new / (1.0 - beta_two**STEP)
            step = first_hat / (jnp.sqrt(second_hat) + eps_adam) + decay_matrix * old
            first_out[0, :, at] = first_new
            second_out[0, :, at] = second_new
            weight_out[0, :, at] = old - rate_matrix * step

    return kernel_call(
        body,
        (steps,),
        [scalar] * len(scalars)
        + specs
        + [part] * 3
        + [anywhere] * kept,
        [part] * 3,
        [shaped(weight.shape)] * 3,
        aliases={before + 3 + i: i for i in range(kept - len(earlier))},
        scratch=[pltpu.VMEM((tile, columns), jnp.float32), *(make(tile) for make in scratch)],
        cost=(0, 26 * rows * columns),
    )(*scalars, *grads, *state, *(previous or ()), *earlier)


def mix_reduce(layers):
    seqs, rows, width = layers[0][0].shape
    count, rings = len(layers), len(layers[0])
    chunk = width // 4

    def body(place, *refs):
        inner_out, outer_out = refs[count * rings :]
        for layer in range(count):
            parts = refs[layer * rings : (layer + 1) * rings]
            for s in range(seqs):
                total = parts[0][s].astype(jnp.float32)
                for part in parts[1:]:
                    total = total + part[s].astype(jnp.float32)
                inner_out[lax.bitwise_xor(place[0], jnp.int32(s)), layer] = total.astype(low)
                outer_out[layer, :, s * chunk : (s + 1) * chunk] = total[:, 3 * chunk :]

    inner, last = plain_call(
        body,
        [shaped((seqs, count, rows, width), low), shaped((count, rows, seqs * chunk))],
        scalars=1,
    )(place_of("seq"), *sum((list(pieces) for pieces in layers), []))
    return [inner[0]] + [seq_swap(inner[j], j) for j in range(1, seqs)] + [last]


def mix_adam(grads, state):
    seqs = lax.axis_size("seq")
    features = state[0].shape[2] // 4
    chunk = features // seqs

    def load(scalars, grads, scratch, total):
        for s in range(seqs):
            scratch[0][lax.bitwise_xor(scalars[0][0], jnp.int32(s))] = grads[s][0]
        for s in range(seqs):
            for g in range(3):
                start = g * features + s * chunk
                piece = scratch[0][s, :, g * chunk : (g + 1) * chunk]
                total[:, start : start + chunk] = piece.astype(jnp.float32)
        total[:, 3 * features :] = grads[seqs][0]

    return adam_kernel(
        load,
        [place_of("seq")],
        grads,
        state,
        None,
        None,
        [lambda tile: pltpu.VMEM((seqs, tile, 4 * chunk), low)],
    )


def scatter_rows(grad):
    return lax.psum_scatter(grad, "seq", scatter_dimension=0, tiled=True)


def split_feed(part, rows):
    rings = lax.axis_size("fsdp")
    part = part.reshape(rings, rows, -1)

    def body(place, part, *outs):
        for j in range(rings):
            outs[j][...] = part[lax.bitwise_xor(place[0], jnp.int32(j))]

    pieces = plain_call(body, [shaped(part.shape[1:], low)] * rings, scalars=1)(
        place_of("fsdp"), part
    )
    return return_sums(pieces)


def feed_adam(grads, state, layer, previous):
    seqs, rings = lax.axis_size("seq"), lax.axis_size("fsdp")
    half = state[0].shape[2] // 2
    block = half // (seqs * rings)
    tall = tall_of(block)

    def load(scalars, grads, scratch, total):
        for j in range(rings):
            scratch[0][lax.bitwise_xor(scalars[0][0], jnp.int32(j))] = grads[j][...]
        for f in range(rings):
            for g in range(2):
                for s in range(seqs):
                    start = g * half + (s * rings + f) * block
                    at = (g * seqs + s) * tall
                    piece = scratch[0][f, :, at : at + block]
                    total[:, start : start + block] = piece.astype(jnp.float32)

    return adam_kernel(
        load,
        [place_of("fsdp")],
        grads,
        state,
        layer,
        previous,
        [lambda tile: pltpu.VMEM((rings, tile, 2 * seqs * tall), low)],
    )


def down_adam(parts, state, layer, previous):
    def load(scalars, grads, scratch, total):
        sums = grads[0][...].astype(jnp.float32)
        for grad in grads[1:]:
            sums = sums + grad[...].astype(jnp.float32)
        total[...] = sums[: total.shape[0]]

    return adam_kernel(load, [], parts, state, layer, previous)


def split_down(part, earlier):
    seqs = lax.axis_size("seq")
    part = part.reshape(seqs, -1, part.shape[-1])

    def body(place, part, even, odd):
        for i in range(seqs):
            owner = lax.bitwise_xor(place[0], jnp.int32(i))
            (even, odd)[i % 2][i // 2] = part[owner]

    return plain_call(
        body,
        [shaped((seqs // 2,) + part.shape[1:], part.dtype)] * 2,
        scalars=1,
        earlier=earlier,
    )(place_of("seq"), part)


def place_blocks(blocks, owners, place, earlier=()):
    def body(place, *refs):
        if len(blocks[0].shape) == len(refs[-1].shape):
            refs = [ref.at[i] for ref in refs[:-1] for i in range(ref.shape[0])] + [refs[-1]]
        for block, owner in zip(refs, owners(place[0])):
            refs[-1][owner] = block[...]

    shape = blocks[0].shape
    if len(blocks) == 2:
        shape = (2 * shape[0],) + shape[1:]
    else:
        shape = (len(blocks),) + shape
    return plain_call(body, [shaped(shape, blocks[0].dtype)], scalars=1, earlier=earlier)(
        place, *blocks
    )[0]


def vectors_start(gain_weight, tap_weight):
    gains = gain_weight.reshape(2 * LAYERS, -1)
    taps = tap_weight.reshape(3 * LAYERS, -1)
    return gather_fsdp(jnp.concatenate([gains, taps], axis=0).astype(low))


def vectors_middle(blocks):
    rings = lax.axis_size("fsdp")
    both = place_blocks(
        blocks,
        lambda place: [lax.bitwise_xor(place, jnp.int32(j)) for j in range(rings)],
        place_of("fsdp"),
    )
    return both, send_seq(both)


def vectors_end(both, blocks):
    spread = place_blocks(
        blocks,
        lambda place: [lax.bitwise_xor(place, jnp.int32(i)) for i in seq_order()],
        place_of("seq"),
    )
    gains = jnp.transpose(spread[:, :, : 2 * LAYERS], (2, 0, 1, 3)).astype(jnp.float32)
    taps = jnp.transpose(both[:, 2 * LAYERS :], (1, 0, 2)).astype(jnp.float32)
    return gains.reshape(LAYERS, 2, 1, -1), taps.reshape(LAYERS, 3, -1)


def vector_gradients(gain_grads, tap_grads, short):
    seqs, rings = lax.axis_size("seq"), lax.axis_size("fsdp")
    place_seq, place_fsdp = lax.axis_index("seq"), lax.axis_index("fsdp")
    gains = gain_grads.reshape(2 * LAYERS, seqs, -1)
    owner = place_seq ^ jnp.array(seq_order())
    pick = (owner[:, None] == jnp.arange(seqs)[None, :]).astype(jnp.float32)
    gains = jnp.einsum("jo,koc->jkc", pick, gains, precision=lax.Precision.HIGHEST)
    gains = small_scatter_seq(gains)
    taps = tap_grads.reshape(3 * LAYERS, -1)[:, : rings * short]
    both = jnp.concatenate([gains, taps], axis=0).reshape(5 * LAYERS, rings, short)
    owner = place_fsdp ^ jnp.arange(rings)
    pick = (owner[:, None] == jnp.arange(rings)[None, :]).astype(jnp.float32)
    both = jnp.einsum("jo,koc->jkc", pick, both, precision=lax.Precision.HIGHEST)
    both = small_scatter_fsdp(both)
    return (
        both[: 2 * LAYERS].reshape(LAYERS, 2, short),
        both[2 * LAYERS :].reshape(LAYERS, 3, short),
    )


def unit_rows(values):
    row_scale = lax.rsqrt(jnp.mean(values * values, axis=-1, keepdims=True) + eps_norm)
    return values * row_scale, row_scale


def first_norm(inputs, gain, earlier):
    def body(inputs, gain, stream_out, normed_out):
        stream = inputs[...].astype(jnp.float32)
        stream_out[...] = stream
        normed_out[...] = (unit_rows(stream)[0] * gain[...]).astype(low)

    return plain_call(
        body, [shaped(inputs.shape), shaped(inputs.shape, low)], earlier=earlier
    )(inputs, gain)


def finish(base, sums, gain, earlier=(), carried=()):
    def body(*refs):
        total = refs[0][...]
        for part in refs[1 : 1 + len(sums)]:
            total = total + part[...].astype(jnp.float32)
        if gain is None:
            refs[-1][...] = total.astype(low)
        else:
            refs[-2][...] = total
            refs[-1][...] = (unit_rows(total)[0] * refs[1 + len(sums)][...]).astype(low)

    if gain is None:
        return plain_call(body, [shaped(base.shape, low)])(base, *sums)[0]
    return plain_call(
        body,
        [shaped(base.shape), shaped(base.shape, low)],
        earlier=earlier,
        carried=carried,
    )(base, *sums, gain)


def finish_back(flow, sums, stream, gain, carried=(), earlier=()):
    def body(flow, stream, gain, *refs):
        total = refs[0][...].astype(jnp.float32)
        for part in refs[1 : len(sums)]:
            total = total + part[...].astype(jnp.float32)
        unit, row_scale = unit_rows(stream[...])
        scaled = total * gain[...]
        inner_mean = jnp.mean(scaled * unit, axis=-1, keepdims=True)
        result = flow[...].astype(jnp.float32) + row_scale * (scaled - unit * inner_mean)
        refs[-3][...] = result
        refs[-2][...] = result.astype(low)
        refs[-1][...] = jnp.sum(total * unit, axis=0, keepdims=True)

    return plain_call(
        body,
        [shaped(flow.shape), shaped(flow.shape, low), shaped((1, flow.shape[1]))],
        carried=carried,
        earlier=earlier,
    )(flow, stream, gain, *sums)


def pair_sum(even, received, earlier=(), carried=()):
    half, tokens, features = even.shape

    def body(even, received, *outs):
        for i in range(half):
            total = even[i] + received[i].astype(jnp.float32)
            outs[i][...] = total.astype(outs[i].dtype)

    outs = plain_call(
        body,
        [shaped((tokens, features))] + [shaped((tokens, features), low)] * (half - 1),
        earlier=earlier,
        carried=carried,
    )(even, received)
    return [outs[0]] + [seq_swap(outs[i], 2 * i) for i in range(1, half)], *outs[half:]


def block_neighbour(place, i, count, step):
    order = list(range(0, count, 2)) + list(range(1, count, 2))
    owner = lax.bitwise_xor(place, jnp.int32(order[i])) + step
    inside = jnp.logical_and(owner >= 0, owner < count)
    number = lax.bitwise_xor(place, jnp.where(inside, owner, place))
    return lax.div(number, 2) + lax.rem(number, 2) * (count // 2), inside


def conv_forward(place, taps, gated, i, count):
    here = gated[i]
    tokens, chunk = here.shape
    at, inside = block_neighbour(place, i, count, -1)
    before = jnp.where(inside, gated[at, tokens - 8 :, :], 0.0)
    row = lax.broadcasted_iota(jnp.int32, (tokens, chunk), 0)
    last, second = before[7:8, :], before[6:7, :]
    one = jnp.where(row == 0, last, pltpu.roll(here, 1, 0))
    two = jnp.where(row == 0, second, jnp.where(row == 1, last, pltpu.roll(here, 2, 0)))
    return taps[0:1, :] * two + taps[1:2, :] * one + taps[2:3, :] * here, one, two


def mixer_forward(blocks, inner, outer, taps):
    half, tokens, features = blocks[0].shape
    count = 2 * half
    chunk = outer.shape[0]
    wide = inner.shape[1] // 3

    def body(place, even_in, odd_in, inner, outer, taps, *refs):
        projected, even, odd, gated, mixed = refs
        for k, rows in enumerate((even_in, odd_in)):
            rows = rows[...].reshape(half * tokens, features)
            for g in range(3):
                columns = slice(g * wide, (g + 1) * wide)
                part = dot(rows, inner[:, columns]).reshape(half, tokens, wide)
                projected[k * half : (k + 1) * half, :, columns] = part

        for i in range(count):
            product = projected[i, :, :wide] * projected[i, :, 2 * wide :]
            gated[i] = product[:, :chunk].astype(low).astype(jnp.float32)
        taps = taps[...]
        for i in range(count):
            conv_out = conv_forward(place[0], taps, gated, i, count)[0]
            mixed[i] = (projected[i, :, wide : wide + chunk] * conv_out).astype(low)
        rows = mixed[:half].reshape(half * tokens, chunk)
        even[...] = dot(rows, outer[...]).reshape(half, tokens, features)
        rows = mixed[half:].reshape(half * tokens, chunk)
        odd[...] = dot(rows, outer[...]).reshape(half, tokens, features).astype(low)

    return plain_call(
        body,
        [
            shaped((count, tokens, 3 * wide)),
            shaped((half, tokens, features)),
            shaped((half, tokens, features), low),
        ],
        scalars=1,
        scratch=[
            pltpu.VMEM((count, tokens, chunk), jnp.float32),
            pltpu.VMEM((count, tokens, chunk), low),
        ],
    )(place_of("seq"), *blocks, inner, outer, taps)


def mixer_backward(blocks, projected, inner, outer, taps):
    half, tokens, features = blocks[0].shape
    count = 2 * half
    chunk = outer.shape[0]
    wide = inner.shape[1] // 3

    def body(place, even_in, odd_in, projected, inner, outer, taps, *refs):
        even, odd, flows, mixed, tap_out, gated, flow = refs
        for i in range(count):
            product = projected[i, :, :wide] * projected[i, :, 2 * wide :]
            gated[i] = product[:, :chunk].astype(low).astype(jnp.float32)
        taps = taps[...]
        tap_sums = [jnp.zeros((1, chunk), jnp.float32)] * 3
        for k in range(2):
            rows = (even_in, odd_in)[k][...].reshape(half * tokens, features)
            back = dot(rows, outer[...], nt).reshape(half, tokens, chunk)
            for i in range(k * half, (k + 1) * half):
                conv_out, one, two = conv_forward(place[0], taps, gated, i, count)
                gate = projected[i, :, wide : wide + chunk]
                mixed[i] = (gate * conv_out).astype(low)
                mixed_flow = back[i - k * half]
                conv_flow = mixed_flow * gate
                flow[i] = conv_flow
                for j, shifted in enumerate((two, one, gated[i])):
                    term = jnp.sum(conv_flow * shifted, axis=0, keepdims=True)
                    tap_sums[j] = tap_sums[j] + term
                flows[i, :, wide : wide + chunk] = (mixed_flow * conv_out).astype(low)
        for j in range(3):
            tap_out[j : j + 1, :] = tap_sums[j]
        row = lax.broadcasted_iota(jnp.int32, (tokens, chunk), 0)
        for i in range(count):
            here = flow[i]
            at, inside = block_neighbour(place[0], i, count, 1)
            beyond = jnp.where(inside, flow[at, :8, :], 0.0)
            first, second = beyond[0:1, :], beyond[1:2, :]
            one = jnp.where(row == tokens - 1, first, pltpu.roll(here, tokens - 1, 0))
            two = jnp.where(
                row == tokens - 1,
                second,
                jnp.where(row == tokens - 2, first, pltpu.roll(here, tokens - 2, 0)),
            )
            gated_flow = taps[2:3, :] * here + taps[1:2, :] * one + taps[0:1, :] * two
            x_part = projected[i, :, 2 * wide : 2 * wide + chunk]
            b_part = projected[i, :, :chunk]
            flows[i, :, :chunk] = (gated_flow * x_part).astype(low)
            flows[i, :, 2 * wide : 2 * wide + chunk] = (gated_flow * b_part).astype(low)
            if wide > chunk:
                for g in range(3):
                    gap = jnp.zeros((tokens, wide - chunk), low)
                    flows[i, :, g * wide + chunk : (g + 1) * wide] = gap
        rows = flows[:half].reshape(half * tokens, 3 * wide)
        even[...] = dot(rows, inner[...], nt).reshape(half, tokens, features)
        rows = flows[half:].reshape(half * tokens, 3 * wide)
        odd[...] = dot(rows, inner[...], nt).reshape(half, tokens, features).astype(low)

    return plain_call(
        body,
        [
            shaped((half, tokens, features)),
            shaped((half, tokens, features), low),
            shaped((count, tokens, 3 * wide), low),
            shaped((count, tokens, chunk), low),
            shaped((3, chunk)),
        ],
        scalars=1,
        scratch=[pltpu.VMEM((count, tokens, chunk), jnp.float32)] * 2,
    )(place_of("seq"), *blocks, projected, inner, outer, taps)


def mixer_grads(normed, flows, mixed, lows, rows):
    seqs, rings = lax.axis_size("seq"), lax.axis_size("fsdp")
    features, width = normed[0].shape[-1], flows.shape[-1]
    half = normed[0].shape[0]
    wide = width // 3
    chunk = mixed.shape[-1]

    def body(place, normed_even, normed_odd, flows, mixed, low_even, low_odd, *refs):
        outs, inner, outer = refs[:rings], refs[rings], refs[rings + 1]
        long = lambda array: array.reshape(-1, array.shape[-1])
        for g in range(3):
            at = slice(g * wide, (g + 1) * wide)
            part = dot(long(normed_even[...]), long(flows[:half, :, at]), tn)
            part = part + dot(long(normed_odd[...]), long(flows[half:, :, at]), tn)
            part = part.astype(low)
            for i in range(seqs * rings):
                inner[i // rings, i % rings, :, at] = part[i * rows : (i + 1) * rows]
        part = dot(long(mixed[:half]), long(low_even[...]), tn)
        part = part + dot(long(mixed[half:]), long(low_odd[...]), tn)
        part = part.astype(low)
        for f in range(rings):
            outer[f] = part[f * rows : (f + 1) * rows]
        for j in range(rings):
            f = lax.bitwise_xor(place[0], jnp.int32(j))
            for s in range(seqs):
                for g in range(3):
                    piece = inner[s, f, :, g * wide : g * wide + chunk]
                    outs[j][s, :, g * chunk : (g + 1) * chunk] = piece
                outs[j][s, :, 3 * chunk :] = outer[f, :, s * chunk : (s + 1) * chunk]

    return plain_call(
        body,
        [shaped((seqs, rows, 4 * chunk), low)] * rings,
        scalars=1,
        scratch=[
            pltpu.VMEM((seqs, rings, rows, width), low),
            pltpu.VMEM((rings, rows, features), low),
        ],
        cost=(24 * half * normed[0].size, 8 * normed[0].size),
    )(place_of("fsdp"), *normed, flows, mixed, *lows)


def hidden_tile(hidden):
    return 256 if hidden % 256 == 0 else 128


def feed_specs(features, hidden):
    tile = hidden_tile(hidden)
    steps = hidden // tile
    return (
        pl.BlockSpec((features, tile), lambda i: (0, i)),
        pl.BlockSpec((features, tile), lambda i: (0, i + steps)),
        pl.BlockSpec((tile, features), lambda i: (i, 0)),
    )


def feed_forward(blocks, up_matrix, down, own):
    count = len(blocks)
    tokens, features = blocks[0].shape
    hidden = down.shape[0]
    tile = hidden_tile(hidden)
    steps = hidden // tile

    def body(*refs):
        gate_matrix, up_matrix, down = refs[count : count + 3]
        outs = refs[count + 3 : 2 * count + 3]
        gate_out, up_out, hidden_out, rows, total = refs[2 * count + 3 :]
        step = pl.program_id(0)

        @pl.when(step == 0)
        def _():
            for i in range(count):
                rows[i * tokens : (i + 1) * tokens] = refs[i][...]
            total[...] = jnp.zeros_like(total)

        gate = dot(rows[...], gate_matrix[...])
        up = dot(rows[...], up_matrix[...])
        gate_out[...] = gate
        up_out[...] = up
        value = (gate * jax.nn.sigmoid(gate) * up).astype(low)
        hidden_out[...] = value
        total[...] += dot(value, down[...])

        @pl.when(step == steps - 1)
        def _():
            for i in range(count):
                outs[i][...] = total[i * tokens : (i + 1) * tokens].astype(outs[i].dtype)

    columns = pl.BlockSpec((count * tokens, tile), lambda i: (0, i))
    outs = kernel_call(
        body,
        (steps,),
        [whole((tokens, features))] * count + list(feed_specs(features, hidden)),
        [whole((tokens, features))] * count + [columns] * 3,
        [
            shaped((tokens, features), jnp.float32 if own and i == 0 else low)
            for i in range(count)
        ]
        + [shaped((count * tokens, hidden), kind) for kind in (jnp.float32, jnp.float32, low)],
        scratch=[
            pltpu.VMEM((count * tokens, features), low),
            pltpu.VMEM((count * tokens, features), jnp.float32),
        ],
    )(*blocks, up_matrix, up_matrix, down)
    return outs[:count], outs[count:]


def feed_backward(blocks, gates, ups, up_matrix, down, own):
    count = len(blocks)
    tokens, features = blocks[0].shape
    hidden = down.shape[0]
    tile = hidden_tile(hidden)
    steps = hidden // tile

    def body(*refs):
        gate_part, up_part, gate_matrix, up_matrix, down = refs[count : count + 5]
        outs = refs[count + 5 : 2 * count + 5]
        gate_out, up_out, rows, total = refs[2 * count + 5 :]
        step = pl.program_id(0)

        @pl.when(step == 0)
        def _():
            for i in range(count):
                rows[i * tokens : (i + 1) * tokens] = refs[i][...]
            total[...] = jnp.zeros_like(total)

        flow = dot(rows[...], down[...], nt)
        gate = gate_part[...]
        smooth = jax.nn.sigmoid(gate)
        gate_flow = flow * up_part[...] * (smooth * (1.0 + gate * (1.0 - smooth)))
        gate_flow = gate_flow.astype(low)
        up_flow = (flow * (gate * smooth)).astype(low)
        gate_out[...] = gate_flow
        up_out[...] = up_flow
        total[...] += dot(gate_flow, gate_matrix[...], nt) + dot(up_flow, up_matrix[...], nt)

        @pl.when(step == steps - 1)
        def _():
            for i in range(count):
                outs[i][...] = total[i * tokens : (i + 1) * tokens].astype(outs[i].dtype)

    columns = pl.BlockSpec((count * tokens, tile), lambda i: (0, i))
    outs = kernel_call(
        body,
        (steps,),
        [whole((tokens, features))] * count + [columns] * 2 + list(feed_specs(features, hidden)),
        [whole((tokens, features))] * count + [columns] * 2,
        [
            shaped((tokens, features), jnp.float32 if own and i == 0 else low)
            for i in range(count)
        ]
        + [shaped((count * tokens, hidden), low)] * 2,
        scratch=[
            pltpu.VMEM((count * tokens, features), low),
            pltpu.VMEM((count * tokens, features), jnp.float32),
        ],
    )(*blocks, gates, ups, up_matrix, up_matrix, down)
    return outs[:count], outs[count:]


def feed_grads(normed, gate_flows, up_flows):
    count, groups = len(normed), len(gate_flows)
    tokens, features = normed[0].shape
    hidden = gate_flows[0].shape[1]
    sizes = [flow.shape[0] for flow in gate_flows]
    starts = [sum(sizes[:i]) for i in range(groups)]
    tile = hidden_tile(hidden)
    steps = hidden // tile

    def body(*refs):
        flows = refs[count : count + 2 * groups]
        out, rows, columns = refs[count + 2 * groups :]
        step = pl.program_id(0)

        @pl.when(step == 0)
        def _():
            for i in range(count):
                rows[i * tokens : (i + 1) * tokens] = refs[i][...]

        for half in range(2):

            @pl.when(lax.div(step, steps) == half)
            def _():
                for i in range(groups):
                    at = slice(starts[i], starts[i] + sizes[i])
                    columns[at] = flows[half * groups + i][...]

        out[...] = dot(rows[...], columns[...], tn).astype(low)

    gate_specs = [
        pl.BlockSpec((size, tile), lambda i: (0, jnp.minimum(i, steps - 1))) for size in sizes
    ]
    up_specs = [
        pl.BlockSpec((size, tile), lambda i: (0, jnp.maximum(i - steps, 0))) for size in sizes
    ]
    return kernel_call(
        body,
        (2 * steps,),
        [whole((tokens, features))] * count + gate_specs + up_specs,
        pl.BlockSpec((features, tile), lambda i: (0, i)),
        shaped((features, 2 * hidden), low),
        scratch=[
            pltpu.VMEM((count * tokens, features), low),
            pltpu.VMEM((count * tokens, tile), low),
        ],
        cost=(12 * count * tokens * features * hidden, 24 * features * hidden),
    )(*normed, *gate_flows, *up_flows)


def down_grads(hiddens, flows):
    count, groups = len(flows), len(hiddens)
    tokens, features = flows[0].shape
    hidden = hiddens[0].shape[1]
    sizes = [values.shape[0] for values in hiddens]
    starts = [sum(sizes[:i]) for i in range(groups)]
    tile = hidden_tile(hidden)

    def body(*refs):
        hiddens = refs[count : count + groups]
        out, rows, columns = refs[count + groups :]

        @pl.when(pl.program_id(0) == 0)
        def _():
            for i in range(count):
                rows[i * tokens : (i + 1) * tokens] = refs[i][...]

        for i in range(groups):
            columns[starts[i] : starts[i] + sizes[i]] = hiddens[i][...]
        out[...] = dot(columns[...], rows[...], tn).astype(low)

    return kernel_call(
        body,
        (hidden // tile,),
        [whole((tokens, features))] * count
        + [pl.BlockSpec((size, tile), lambda i: (0, i)) for size in sizes],
        pl.BlockSpec((tile, features), lambda i: (i, 0)),
        shaped((hidden, features), low),
        scratch=[
            pltpu.VMEM((count * tokens, features), low),
            pltpu.VMEM((count * tokens, tile), low),
        ],
        cost=(6 * count * tokens * features * hidden, 12 * features * hidden),
    )(*flows, *hiddens)


def join_blocks(blocks):
    def body(*refs):
        for i in range(len(blocks)):
            refs[len(blocks) + i][...] = refs[i][...]

    return plain_call(body, [shaped(block.shape, block.dtype) for block in blocks])(*blocks)


def groups_of(blocks):
    return [blocks[:2]] + [[block] for block in blocks[2:]]


def return_sums(sums):
    return [sums[0]] + [fsdp_swap(sums[j], j) for j in range(1, len(sums))]


def adam_update(weight, first, second, gradient, rate, decay):
    first_new = beta_one * first + (1.0 - beta_one) * gradient
    second_new = beta_two * second + (1.0 - beta_two) * gradient * gradient
    first_hat = first_new / (1.0 - beta_one**STEP)
    second_hat = second_new / (1.0 - beta_two**STEP)
    weight_new = weight - rate * (first_hat / (jnp.sqrt(second_hat) + eps_adam) + decay * weight)
    return (first_new, second_new, weight_new)


def local(
    inputs,
    cotangent,
    mix_weight,
    mix_first,
    mix_second,
    feed_weight,
    feed_first,
    feed_second,
    down_weight,
    down_first,
    down_second,
    gain_weight,
    gain_first,
    gain_second,
    tap_weight,
    tap_first,
    tap_second,
):
    sequences, length, features = inputs.shape
    seqs, rings = lax.axis_size("seq"), lax.axis_size("fsdp")
    rows = mix_weight.shape[1]
    chunk = features // seqs
    wide = -(-chunk // 128) * 128
    cotangent = cotangent.reshape(-1, features)
    Order.mark = jnp.zeros(mark_shape.shape, mark_shape.dtype)

    mixes, feeds = [None] * LAYERS, [None] * LAYERS
    vector_blocks = vectors_start(gain_weight, tap_weight)
    feed_swap = swap_feed(pack_feed(feed_weight, 0))
    mix_packed = pack_mix(mix_weight, 0, vector_blocks[1:])
    mix_swap = swap_mix(mix_packed)
    down_rows = gather_rows(pack_down(down_weight, 0))
    both, vector_blocks = vectors_middle(vector_blocks)
    mix_pieces = gather_fsdp(join_mix(mix_swap, mix_packed))
    feed_part = assemble_feed(feed_swap)
    later_packed = pack_mix(mix_weight, 1)
    later_swap = swap_mix(later_packed)
    vector_blocks = stack_pairs(vector_blocks)
    later_piece = join_mix(later_swap, later_packed, mix_pieces[1:2])
    gain_rows, tap_rows = vectors_end(both, vector_blocks)
    stream, normed = first_norm(inputs.reshape(-1, features), gain_rows[0, 0], ())
    blocks = send_seq(normed)
    later_feed = pack_feed(feed_weight, 1)
    *blocks, feed_part = stack_pairs(blocks, mix_pieces[2:], [feed_part])
    feeds[0] = (gather_rows(feed_part), down_rows)
    mixes[0] = assemble_mix(mix_pieces, wide)
    later_mix = [None, None, fsdp_swap(later_piece, 2)] if rings > 2 else [None, None]
    later_feed = swap_feed(later_feed)

    kept = []
    for layer in range(LAYERS):
        last = layer + 1 == LAYERS
        gathered = blocks
        projected, even, odd = mixer_forward(blocks, *mixes[layer], tap_rows[layer])
        odd = seq_swap(odd, 1)
        if last:
            sums, flow_low = pair_sum(even, odd, (), [cotangent])
            flow_low = gather_fsdp(flow_low)
            middle, normed_two = finish(stream, sums, gain_rows[layer, 1])
            flow_low = join_blocks(flow_low)
        else:
            (sums,) = pair_sum(even, odd, later_feed[1:])
            middle, normed_two, later_piece, down_packed = finish(
                stream,
                sums,
                gain_rows[layer, 1],
                later_mix[2:],
                (later_piece, pack_down(down_weight, 1)),
            )
        two_blocks = gather_fsdp(normed_two)
        if not last:
            later_mix[0] = later_piece
            later_mix[1] = fsdp_swap(later_piece, 1)
            feeds[1] = (gather_rows(assemble_feed(later_feed)), gather_rows(down_packed))
        sums, values = [], []
        for number, group in enumerate(groups_of(two_blocks)):
            outs, saved = feed_forward(group, *feeds[layer], number == 0)
            sums += outs
            values.append(saved)
        kept.append((stream, middle, gathered, projected, two_blocks, values))
        sums = return_sums(sums)
        if not last:
            stream, normed, later_piece = finish(
                middle, sums, gain_rows[layer + 1, 0], later_mix[1:2], [later_piece]
            )
            blocks = send_seq(normed)
            later_mix += [fsdp_swap(later_piece, by) for by in range(3, rings)]
            blocks = stack_pairs(blocks)
            mixes[1] = assemble_mix(later_mix, wide)

    states = (
        (mix_weight, mix_first, mix_second),
        (feed_weight, feed_first, feed_second),
        (down_weight, down_first, down_second),
    )
    new = [None] * 3
    gain_grads, tap_grads = [None] * LAYERS, [None] * LAYERS
    flow = cotangent
    later_mix = ()
    for layer in reversed(range(LAYERS)):
        last = layer + 1 == LAYERS
        stream, middle, gathered, projected, two_blocks, values = kept[layer]
        back_sums, gate_flows, up_flows = [], [], []
        for number, group in enumerate(groups_of(flow_low)):
            gates, ups, _ = values[number]
            outs, (gate_flow, up_flow) = feed_backward(
                group, gates, ups, *feeds[layer], number == 0
            )
            back_sums += outs
            gate_flows.append(gate_flow)
            up_flows.append(up_flow)
        if last:
            outputs = finish(middle, sums, None).reshape(inputs.shape)
        back_sums = return_sums(back_sums)
        down_part = down_grads([value[2] for value in values], flow_low)
        middle_flow, middle_low, gain_two, down_part, *later_mix = finish_back(
            flow, back_sums, middle, gain_rows[layer, 1], [down_part, *later_mix]
        )
        later_mix = return_sums(later_mix) if later_mix else later_mix
        if last:
            down_part = [scatter_rows(down_part)]
        blocks = send_seq(middle_low)
        feed_part = feed_grads(two_blocks, gate_flows, up_flows)
        if not last:
            later_feed = split_feed(later_feed, rows)
        even, odd, feed_part = stack_pairs(
            blocks, () if last else later_mix[2:3], [feed_part]
        )
        feed_part = scatter_rows(feed_part)
        blocks = even, odd
        even, odd, flows, mixed, tap_grads[layer] = mixer_backward(
            blocks, projected, *mixes[layer], tap_rows[layer]
        )
        (sums,) = pair_sum(even, seq_swap(odd, 1), () if last else later_feed[1:])
        mix_part = mixer_grads(gathered, flows, mixed, blocks, rows)
        flow, low_flow, gain_one, *mix_part = finish_back(
            middle_flow,
            sums,
            stream,
            gain_rows[layer, 0],
            mix_part,
            () if last else (later_mix[1], *later_mix[3:]),
        )
        if not last:
            mix_part = return_sums(mix_part)
        gain_grads[layer] = jnp.concatenate([gain_one, gain_two])
        if last:
            flow_low = gather_fsdp(low_flow)
            later_mix, later_feed, later_down = mix_part, feed_part, down_part
    new[1] = feed_adam(later_feed, states[1], 1, new[1])
    even, odd = split_down(down_part, mix_part[1:3])
    odd = seq_swap(odd, 1)
    new[2] = down_adam(later_down, states[2], 1, new[2])
    (down_part,) = pair_sum(even, odd, mix_part[3:])
    gain_grad, tap_grad = vector_gradients(
        jnp.stack(gain_grads), jnp.stack(tap_grads), gain_weight.shape[-1]
    )
    mix_part = mix_reduce([mix_part, later_mix])
    feed_part = split_feed(feed_part, rows)
    new[2] = down_adam(down_part, states[2], 0, new[2])
    new[0] = mix_adam(mix_part, states[0])
    new[1] = feed_adam(feed_part, states[1], 0, new[1])
    input_grad = flow.reshape(sequences, length, features)
    gain_new = adam_update(gain_weight, gain_first, gain_second, gain_grad, rate_vector, 0.0)
    tap_new = adam_update(tap_weight, tap_first, tap_second, tap_grad, rate_vector, 0.0)
    matrices = [(part[1], part[2], part[0]) for part in new]
    return (outputs, input_grad, *sum(matrices, ()), *gain_new, *tap_new)


def solution(mesh):
    tokens = P("fsdp", "seq", None)
    rows = P(None, ("seq", "fsdp"), None)
    last = P(None, None, ("seq", "fsdp"))
    return jax.shard_map(
        local,
        mesh=mesh,
        in_specs=(tokens,) * 2 + (rows,) * 9 + (last,) * 6,
        out_specs=(tokens,) * 2 + (rows,) * 9 + (last,) * 6,
        check_vma=False,
    )
```

```python
import math

import jax
import jax.numpy as jnp
from jax import lax
from jax.experimental import pallas as pl
from jax.experimental.pallas import tpu as pltpu
from jax.sharding import PartitionSpec as P

LAYERS = 2
STEP = 10

eps_norm = 1e-05
eps_adam = 1e-08
beta_one = 0.9
beta_two = 0.95
rate_matrix = 0.05
rate_vector = 0.6
decay_matrix = 0.1

low = jnp.bfloat16


def dot(left, right, sides=((1,), (0,))):
    return lax.dot_general(left, right, (sides, ((), ())), preferred_element_type=jnp.float32)


nt = ((1,), (1,))
tn = ((0,), (0,))


def seq_order():
    count = lax.axis_size("seq")
    return list(range(0, count, 2)) + list(range(1, count, 2))


def seq_swap(array, by):
    count = lax.axis_size("seq")
    return lax.ppermute(array, "seq", [(i, i ^ by) for i in range(count)])


def send_seq(array):
    return [array] + [seq_swap(array, by) for by in range(2, lax.axis_size("seq"), 2)]


def fsdp_swap(array, by):
    count = lax.axis_size("fsdp")
    return lax.ppermute(array, "fsdp", [(i, i ^ by) for i in range(count)])


def gather_fsdp(array):
    count = lax.axis_size("fsdp")
    return [array] + [fsdp_swap(array, by) for by in range(1, count)]


def small_scatter_seq(parts):
    half = parts.shape[0] // 2
    total = parts[:half] + seq_swap(parts[half:], 1)
    for i in range(1, half):
        total = total.at[0].add(seq_swap(total[i], 2 * i))
    return total[0]


def small_scatter_fsdp(parts):
    total = parts[0]
    for by in range(1, parts.shape[0]):
        total = total + fsdp_swap(parts[by], by)
    return total


def stack_pairs(blocks, earlier=(), carried=()):
    def body(*refs):
        for i in range(len(blocks)):
            refs[-1][i] = refs[i][...]

    shape = (len(blocks),) + blocks[0].shape
    even, *rest = plain_call(
        body, [shaped(shape, blocks[0].dtype)], earlier=earlier, carried=carried
    )(*blocks)
    return even, seq_swap(even, 1), *rest


def pad_last(array, width):
    return jnp.pad(array, [(0, 0)] * (array.ndim - 1) + [(0, width - array.shape[-1])])


def place_of(axis):
    return lax.axis_index(axis).astype(jnp.int32).reshape(1)


scalar = pl.BlockSpec(memory_space=pltpu.SMEM)
held = pl.BlockSpec(memory_space=pltpu.VMEM)


def shaped(shape, kind=jnp.float32):
    return jax.ShapeDtypeStruct(shape, kind)


class Order:
    mark = None


mark_shape = jax.ShapeDtypeStruct((8, 128), jnp.float32)
anywhere = pl.BlockSpec(memory_space=pltpu.HBM)


def bytes_of(shape, kind):
    return math.prod(shape) * jnp.dtype(kind).itemsize


def vmem_of(operands, in_specs, out_shape, out_specs, scratch, grid):
    total = 0
    for array, spec in [*zip(operands, in_specs), *zip(out_shape, out_specs)]:
        if spec is anywhere or spec is scalar:
            continue
        if grid:
            total += 2 * bytes_of(spec.block_shape, array.dtype)
        else:
            total += bytes_of(array.shape, array.dtype)
    for array in scratch:
        total += bytes_of(array.shape, array.dtype)
    return total + total // 2 + 4 * 1024 * 1024


def ordered_call(body, operands, in_specs, out_specs, out_shape, aliases, scratch, grid, cost):
    given, made = len(operands), len(out_shape)

    def marked(*refs):
        body(*refs[:given], *refs[given + 1 : given + 1 + made], *refs[given + 2 + made :])

    outs = pl.pallas_call(
        marked,
        in_specs=list(in_specs) + [anywhere],
        out_specs=list(out_specs) + [anywhere],
        out_shape=list(out_shape) + [mark_shape],
        scratch_shapes=list(scratch),
        input_output_aliases=aliases,
        compiler_params=pltpu.CompilerParams(
            vmem_limit_bytes=56 << 20
            if cost[0]
            else min(vmem_of(operands, in_specs, out_shape, out_specs, scratch, grid), 60 << 20)
        ),
        cost_estimate=pl.CostEstimate(
            flops=cost[0], bytes_accessed=cost[1], transcendentals=0
        ),
        **grid,
    )(*operands, Order.mark)
    Order.mark = outs[-1]
    return outs[:-1]


def kernel_call(
    body, grid, in_specs, out_specs, out_shape, aliases=None, scratch=(), cost=(0, 0)
):
    single = not isinstance(out_shape, list)

    def run(*operands):
        outs = ordered_call(
            body,
            operands,
            in_specs,
            [out_specs] if single else out_specs,
            [out_shape] if single else out_shape,
            aliases or {},
            scratch,
            dict(grid=grid),
            cost,
        )
        return outs[0] if single else outs

    return run


def plain_call(
    body, out_shape, scalars=0, scratch=(), earlier=(), carried=(), cost=(0, 0)
):
    def run(*operands):
        given, made, more = len(operands), len(out_shape), len(earlier) + len(carried)

        def rest(*refs):
            outs = refs[given + more :]
            body(*refs[:given], *outs[:made], *outs[made + len(carried) :])

        first = given + len(earlier)
        return ordered_call(
            rest,
            (*operands, *earlier, *carried),
            [scalar] * scalars + [held] * (given - scalars) + [anywhere] * more,
            [held] * made + [anywhere] * len(carried),
            [*out_shape, *(jax.ShapeDtypeStruct(x.shape, x.dtype) for x in carried)],
            {first + i: made + i for i in range(len(carried))},
            scratch,
            {},
            cost,
        )

    return run


def whole(shape):
    return pl.BlockSpec(shape, lambda i: (0,) * len(shape))


def pack_mix(mix_weight, layer, earlier=()):
    seqs = lax.axis_size("seq")
    rows, columns = mix_weight.shape[1:]
    features = columns // 4
    chunk = features // seqs

    def body(place, weight, *refs):
        out = refs[-1]
        for s in range(seqs):
            slot = lax.bitwise_xor(place[0], jnp.int32(s))
            for g in range(4):
                start = g * features + s * chunk
                piece = weight[0, :, start : start + chunk].astype(low)
                out[slot if g < 3 else s, :, g * chunk : (g + 1) * chunk] = piece

    shape = (seqs, rows, 4 * chunk)
    return kernel_call(
        body,
        (1,),
        [scalar, pl.BlockSpec((1, rows, columns), lambda i: (layer, 0, 0))]
        + [anywhere] * len(earlier),
        whole(shape),
        jax.ShapeDtypeStruct(shape, low),
    )(place_of("seq"), mix_weight, *earlier)


def assemble_mix(pieces, wide):
    rings = lax.axis_size("fsdp")
    rotated = len(pieces) == rings
    seqs, rows, width = pieces[0].shape[-3:]
    chunk = width // 4
    features = seqs * chunk

    def body(place_seq, place_fsdp, *refs):
        inner_out, outer_out = refs[-2:]
        for j in range(rings):
            f = lax.bitwise_xor(place_fsdp[0], jnp.int32(j)) if rotated else j
            part = refs[j] if rotated else refs[0].at[j]
            for s in range(seqs):
                owner = lax.bitwise_xor(place_seq[0], jnp.int32(s))
                for g in range(3):
                    piece = part[s, :, g * chunk : (g + 1) * chunk]
                    if wide > chunk:
                        gap = jnp.zeros((rows, wide - chunk), low)
                        piece = jnp.concatenate([piece, gap], axis=1)
                    inner_out[owner, f, :, g * wide : (g + 1) * wide] = piece
                outer_out[f, :, s * chunk : (s + 1) * chunk] = part[s, :, 3 * chunk :]

    inner_shape = (seqs, rings, rows, 3 * wide)
    outer_shape = (rings, rows, features)
    inner, out = plain_call(
        body, [shaped(inner_shape, low), shaped(outer_shape, low)], scalars=2
    )(place_of("seq"), place_of("fsdp"), *pieces)
    return inner.reshape(features, 3 * wide), out.reshape(rings * rows, features)


def swap_mix(packed):
    seqs = lax.axis_size("seq")
    return [packed[:1]] + [seq_swap(packed[by : by + 1], by) for by in range(1, seqs)]


def join_mix(parts, packed, earlier=()):
    seqs = len(parts)

    def body(*refs):
        out = refs[-1]
        split = out.shape[-1] // 4 * 3
        for s in range(seqs):
            out[s, :, :split] = refs[s][0, :, :split]
            out[s, :, split:] = refs[seqs][s, :, split:]

    return plain_call(body, [shaped(packed.shape, low)], earlier=earlier)(*parts, packed)[0]


def tall_of(block):
    step = 128 // min(lax.axis_size("seq"), 128)
    return -(-block // step) * step


def pack_feed(feed_weight, layer):
    seqs, rings = lax.axis_size("seq"), lax.axis_size("fsdp")
    rows, columns = feed_weight.shape[1:]
    half = columns // 2
    block = half // (seqs * rings)
    tall = tall_of(block)

    def body(place, weight, out):
        for f in range(rings):
            slot = lax.bitwise_xor(place[0], jnp.int32(f))
            for g in range(2):
                for s in range(seqs):
                    start = g * half + (s * rings + f) * block
                    piece = weight[0, :, start : start + block].astype(low)
                    if tall > block:
                        piece = jnp.concatenate(
                            [piece, jnp.zeros((rows, tall - block), low)], axis=1
                        )
                    to = (g * seqs + s) * tall
                    out[slot, :, to : to + tall] = piece

    shape = (rings, rows, 2 * seqs * tall)
    return kernel_call(
        body,
        (1,),
        [scalar, pl.BlockSpec((1, rows, columns), lambda i: (layer, 0, 0))],
        whole(shape),
        jax.ShapeDtypeStruct(shape, low),
    )(place_of("fsdp"), feed_weight)


def assemble_feed(pieces):
    rings = len(pieces)

    def body(place, *refs):
        out = refs[rings]
        for j in range(rings):
            out[lax.bitwise_xor(place[0], jnp.int32(j))] = refs[j][0]

    shape = (rings,) + pieces[0].shape[1:]
    return kernel_call(
        body,
        (1,),
        [scalar] + [whole(piece.shape) for piece in pieces],
        whole(shape),
        jax.ShapeDtypeStruct(shape, low),
    )(place_of("fsdp"), *pieces)


def swap_feed(packed):
    rings = lax.axis_size("fsdp")
    return [packed[:1]] + [fsdp_swap(packed[by : by + 1], by) for by in range(1, rings)]


def gather_rows(part):
    return lax.all_gather(part.reshape(-1, part.shape[-1]), "seq", axis=0, tiled=True)


def pack_down(down_weight, layer):
    block = down_weight.shape[1]
    return jnp.pad(down_weight[layer].astype(low), ((0, tall_of(block) - block), (0, 0)))


def adam_kernel(load, scalars, grads, state, layer, previous, scratch=(), earlier=()):
    weight = state[0]
    rows, columns = weight.shape[1:]
    tile = 16 if rows % 16 == 0 else rows
    width = 768
    steps = rows // tile
    if layer is None:
        each = steps
        where = lambda i: (lax.div(i, each), lax.rem(i, each), 0)
        specs = [pl.BlockSpec((1, tile, grad.shape[-1]), where) for grad in grads]
        steps = LAYERS * each
    else:
        where = lambda i: (layer, i, 0)
        specs = [
            pl.BlockSpec(
                grad.shape if tile == rows else (tile, grad.shape[-1]), lambda i: (i, 0)
            )
            for grad in grads
        ]
    part = pl.BlockSpec((1, tile, columns), where)
    kept = (0 if previous is None else 3) + len(earlier)
    before = len(scalars) + len(grads)

    def body(*refs):
        weight, first, second = refs[before : before + 3]
        weight_out, first_out, second_out, total = refs[before + 3 + kept : before + 7 + kept]
        load(refs[: len(scalars)], refs[len(scalars) : before], refs[before + 7 + kept :], total)
        for start in range(0, columns, width):
            at = slice(start, start + width)
            gradient = total[:, at]
            old = weight[0, :, at]
            first_new = beta_one * first[0, :, at] + (1.0 - beta_one) * gradient
            second_new = beta_two * second[0, :, at] + (1.0 - beta_two) * gradient * gradient
            first_hat = first_new / (1.0 - beta_one**STEP)
            second_hat = second_new / (1.0 - beta_two**STEP)
            step = first_hat / (jnp.sqrt(second_hat) + eps_adam) + decay_matrix * old
            first_out[0, :, at] = first_new
            second_out[0, :, at] = second_new
            weight_out[0, :, at] = old - rate_matrix * step

    return kernel_call(
        body,
        (steps,),
        [scalar] * len(scalars)
        + specs
        + [part] * 3
        + [anywhere] * kept,
        [part] * 3,
        [shaped(weight.shape)] * 3,
        aliases={before + 3 + i: i for i in range(kept - len(earlier))},
        scratch=[pltpu.VMEM((tile, columns), jnp.float32), *(make(tile) for make in scratch)],
        cost=(0, 26 * rows * columns),
    )(*scalars, *grads, *state, *(previous or ()), *earlier)


def mix_reduce(layers):
    seqs, rows, width = layers[0][0].shape
    count = len(layers)
    chunk = width // 4
    starts = [sum(len(pieces) for pieces in layers[:i]) for i in range(count + 1)]

    def body(place, *refs):
        inner_out, outer_out = refs[starts[-1] :]
        for layer in range(count):
            parts = refs[starts[layer] : starts[layer + 1]]
            for s in range(seqs):
                total = parts[0][s].astype(jnp.float32)
                for part in parts[1:]:
                    total = total + part[s].astype(jnp.float32)
                inner_out[lax.bitwise_xor(place[0], jnp.int32(s)), layer] = total.astype(low)
                outer_out[layer, :, s * chunk : (s + 1) * chunk] = total[:, 3 * chunk :]

    inner, last = plain_call(
        body,
        [shaped((seqs, count, rows, width), low), shaped((count, rows, seqs * chunk))],
        scalars=1,
    )(place_of("seq"), *sum((list(pieces) for pieces in layers), []))
    return [inner[0]] + [seq_swap(inner[j], j) for j in range(1, seqs)] + [last]


def mix_adam(grads, state):
    seqs = lax.axis_size("seq")
    features = state[0].shape[2] // 4
    chunk = features // seqs

    def load(scalars, grads, scratch, total):
        for s in range(seqs):
            scratch[0][lax.bitwise_xor(scalars[0][0], jnp.int32(s))] = grads[s][0]
        for s in range(seqs):
            for g in range(3):
                start = g * features + s * chunk
                piece = scratch[0][s, :, g * chunk : (g + 1) * chunk]
                total[:, start : start + chunk] = piece.astype(jnp.float32)
        total[:, 3 * features :] = grads[seqs][0]

    return adam_kernel(
        load,
        [place_of("seq")],
        grads,
        state,
        None,
        None,
        [lambda tile: pltpu.VMEM((seqs, tile, 4 * chunk), low)],
    )


def scatter_rows(grad):
    return lax.psum_scatter(grad, "seq", scatter_dimension=0, tiled=True)


def split_feed(part, rows):
    rings = lax.axis_size("fsdp")
    part = part.reshape(rings, rows, -1)

    def body(place, part, *outs):
        for j in range(rings):
            outs[j][...] = part[lax.bitwise_xor(place[0], jnp.int32(j))]

    pieces = plain_call(body, [shaped(part.shape[1:], low)] * rings, scalars=1)(
        place_of("fsdp"), part
    )
    return return_sums(pieces)


def feed_adam(grads, state, layer, previous):
    seqs, rings = lax.axis_size("seq"), lax.axis_size("fsdp")
    half = state[0].shape[2] // 2
    block = half // (seqs * rings)
    tall = tall_of(block)

    def load(scalars, grads, scratch, total):
        for j in range(rings):
            scratch[0][lax.bitwise_xor(scalars[0][0], jnp.int32(j))] = grads[j][...]
        for f in range(rings):
            for g in range(2):
                for s in range(seqs):
                    start = g * half + (s * rings + f) * block
                    at = (g * seqs + s) * tall
                    piece = scratch[0][f, :, at : at + block]
                    total[:, start : start + block] = piece.astype(jnp.float32)

    return adam_kernel(
        load,
        [place_of("fsdp")],
        grads,
        state,
        layer,
        previous,
        [lambda tile: pltpu.VMEM((rings, tile, 2 * seqs * tall), low)],
    )


def down_adam(parts, state, layer, previous):
    def load(scalars, grads, scratch, total):
        sums = grads[0][...].astype(jnp.float32)
        for grad in grads[1:]:
            sums = sums + grad[...].astype(jnp.float32)
        total[...] = sums[: total.shape[0]]

    return adam_kernel(load, [], parts, state, layer, previous)


def split_down(part, earlier):
    seqs = lax.axis_size("seq")
    part = part.reshape(seqs, -1, part.shape[-1])

    def body(place, part, even, odd):
        for i in range(seqs):
            owner = lax.bitwise_xor(place[0], jnp.int32(i))
            (even, odd)[i % 2][i // 2] = part[owner]

    return plain_call(
        body,
        [shaped((seqs // 2,) + part.shape[1:], part.dtype)] * 2,
        scalars=1,
        earlier=earlier,
    )(place_of("seq"), part)


def place_blocks(blocks, owners, place, earlier=()):
    def body(place, *refs):
        if len(blocks[0].shape) == len(refs[-1].shape):
            refs = [ref.at[i] for ref in refs[:-1] for i in range(ref.shape[0])] + [refs[-1]]
        for block, owner in zip(refs, owners(place[0])):
            refs[-1][owner] = block[...]

    shape = blocks[0].shape
    if len(blocks) == 2:
        shape = (2 * shape[0],) + shape[1:]
    else:
        shape = (len(blocks),) + shape
    return plain_call(body, [shaped(shape, blocks[0].dtype)], scalars=1, earlier=earlier)(
        place, *blocks
    )[0]


def vectors_start(gain_weight, tap_weight):
    gains = gain_weight.reshape(2 * LAYERS, -1)
    taps = tap_weight.reshape(3 * LAYERS, -1)
    return gather_fsdp(jnp.concatenate([gains, taps], axis=0).astype(low))


def vectors_middle(blocks):
    rings = lax.axis_size("fsdp")
    both = place_blocks(
        blocks,
        lambda place: [lax.bitwise_xor(place, jnp.int32(j)) for j in range(rings)],
        place_of("fsdp"),
    )
    return both, send_seq(both)


def vectors_end(both, blocks):
    spread = place_blocks(
        blocks,
        lambda place: [lax.bitwise_xor(place, jnp.int32(i)) for i in seq_order()],
        place_of("seq"),
    )
    gains = jnp.transpose(spread[:, :, : 2 * LAYERS], (2, 0, 1, 3)).astype(jnp.float32)
    taps = jnp.transpose(both[:, 2 * LAYERS :], (1, 0, 2)).astype(jnp.float32)
    return gains.reshape(LAYERS, 2, 1, -1), taps.reshape(LAYERS, 3, -1)


def vector_gradients(gain_grads, tap_grads, short):
    seqs, rings = lax.axis_size("seq"), lax.axis_size("fsdp")
    place_seq, place_fsdp = lax.axis_index("seq"), lax.axis_index("fsdp")
    gains = gain_grads.reshape(2 * LAYERS, seqs, -1)
    owner = place_seq ^ jnp.array(seq_order())
    pick = (owner[:, None] == jnp.arange(seqs)[None, :]).astype(jnp.float32)
    gains = jnp.einsum("jo,koc->jkc", pick, gains, precision=lax.Precision.HIGHEST)
    gains = small_scatter_seq(gains)
    taps = tap_grads.reshape(3 * LAYERS, -1)[:, : rings * short]
    both = jnp.concatenate([gains, taps], axis=0).reshape(5 * LAYERS, rings, short)
    owner = place_fsdp ^ jnp.arange(rings)
    pick = (owner[:, None] == jnp.arange(rings)[None, :]).astype(jnp.float32)
    both = jnp.einsum("jo,koc->jkc", pick, both, precision=lax.Precision.HIGHEST)
    both = small_scatter_fsdp(both)
    return (
        both[: 2 * LAYERS].reshape(LAYERS, 2, short),
        both[2 * LAYERS :].reshape(LAYERS, 3, short),
    )


def unit_rows(values):
    row_scale = lax.rsqrt(jnp.mean(values * values, axis=-1, keepdims=True) + eps_norm)
    return values * row_scale, row_scale


def first_norm(inputs, gain, earlier):
    def body(inputs, gain, stream_out, normed_out):
        stream = inputs[...].astype(jnp.float32)
        stream_out[...] = stream
        normed_out[...] = (unit_rows(stream)[0] * gain[...]).astype(low)

    return plain_call(
        body, [shaped(inputs.shape), shaped(inputs.shape, low)], earlier=earlier
    )(inputs, gain)


def finish(base, sums, gain, earlier=(), carried=()):
    def body(*refs):
        total = refs[0][...]
        for part in refs[1 : 1 + len(sums)]:
            total = total + part[...].astype(jnp.float32)
        if gain is None:
            refs[-1][...] = total.astype(low)
        else:
            refs[-2][...] = total
            refs[-1][...] = (unit_rows(total)[0] * refs[1 + len(sums)][...]).astype(low)

    if gain is None:
        return plain_call(body, [shaped(base.shape, low)])(base, *sums)[0]
    return plain_call(
        body,
        [shaped(base.shape), shaped(base.shape, low)],
        earlier=earlier,
        carried=carried,
    )(base, *sums, gain)


def finish_back(flow, sums, stream, gain, carried=(), earlier=()):
    def body(flow, stream, gain, *refs):
        total = refs[0][...].astype(jnp.float32)
        for part in refs[1 : len(sums)]:
            total = total + part[...].astype(jnp.float32)
        unit, row_scale = unit_rows(stream[...])
        scaled = total * gain[...]
        inner_mean = jnp.mean(scaled * unit, axis=-1, keepdims=True)
        result = flow[...].astype(jnp.float32) + row_scale * (scaled - unit * inner_mean)
        refs[-3][...] = result
        refs[-2][...] = result.astype(low)
        refs[-1][...] = jnp.sum(total * unit, axis=0, keepdims=True)

    return plain_call(
        body,
        [shaped(flow.shape), shaped(flow.shape, low), shaped((1, flow.shape[1]))],
        carried=carried,
        earlier=earlier,
    )(flow, stream, gain, *sums)


def pair_sum(even, received, earlier=(), carried=()):
    half, tokens, features = even.shape

    def body(even, received, *outs):
        for i in range(half):
            total = even[i] + received[i].astype(jnp.float32)
            outs[i][...] = total.astype(outs[i].dtype)

    outs = plain_call(
        body,
        [shaped((tokens, features))] + [shaped((tokens, features), low)] * (half - 1),
        earlier=earlier,
        carried=carried,
    )(even, received)
    return [outs[0]] + [seq_swap(outs[i], 2 * i) for i in range(1, half)], *outs[half:]


def block_neighbour(place, i, count, step):
    order = list(range(0, count, 2)) + list(range(1, count, 2))
    owner = lax.bitwise_xor(place, jnp.int32(order[i])) + step
    inside = jnp.logical_and(owner >= 0, owner < count)
    number = lax.bitwise_xor(place, jnp.where(inside, owner, place))
    return lax.div(number, 2) + lax.rem(number, 2) * (count // 2), inside


def conv_forward(place, taps, gated, i, count):
    here = gated[i]
    tokens, chunk = here.shape
    at, inside = block_neighbour(place, i, count, -1)
    before = jnp.where(inside, gated[at, tokens - 8 :, :], 0.0)
    row = lax.broadcasted_iota(jnp.int32, (tokens, chunk), 0)
    last, second = before[7:8, :], before[6:7, :]
    one = jnp.where(row == 0, last, pltpu.roll(here, 1, 0))
    two = jnp.where(row == 0, second, jnp.where(row == 1, last, pltpu.roll(here, 2, 0)))
    return taps[0:1, :] * two + taps[1:2, :] * one + taps[2:3, :] * here, one, two


def mixer_forward(blocks, inner, outer, taps):
    half, tokens, features = blocks[0].shape
    count = 2 * half
    chunk = outer.shape[0]
    wide = inner.shape[1] // 3

    def body(place, even_in, odd_in, inner, outer, taps, *refs):
        projected, even, odd, gated, mixed = refs
        for k, rows in enumerate((even_in, odd_in)):
            rows = rows[...].reshape(half * tokens, features)
            for g in range(3):
                columns = slice(g * wide, (g + 1) * wide)
                part = dot(rows, inner[:, columns]).reshape(half, tokens, wide)
                projected[k * half : (k + 1) * half, :, columns] = part

        for i in range(count):
            product = projected[i, :, :wide] * projected[i, :, 2 * wide :]
            gated[i] = product[:, :chunk].astype(low).astype(jnp.float32)
        taps = taps[...]
        for i in range(count):
            conv_out = conv_forward(place[0], taps, gated, i, count)[0]
            mixed[i] = (projected[i, :, wide : wide + chunk] * conv_out).astype(low)
        rows = mixed[:half].reshape(half * tokens, chunk)
        even[...] = dot(rows, outer[...]).reshape(half, tokens, features)
        rows = mixed[half:].reshape(half * tokens, chunk)
        odd[...] = dot(rows, outer[...]).reshape(half, tokens, features).astype(low)

    return plain_call(
        body,
        [
            shaped((count, tokens, 3 * wide)),
            shaped((half, tokens, features)),
            shaped((half, tokens, features), low),
        ],
        scalars=1,
        scratch=[
            pltpu.VMEM((count, tokens, chunk), jnp.float32),
            pltpu.VMEM((count, tokens, chunk), low),
        ],
    )(place_of("seq"), *blocks, inner, outer, taps)


def mixer_backward(blocks, projected, inner, outer, taps):
    half, tokens, features = blocks[0].shape
    count = 2 * half
    chunk = outer.shape[0]
    wide = inner.shape[1] // 3

    def body(place, even_in, odd_in, projected, inner, outer, taps, *refs):
        even, odd, flows, mixed, tap_out, gated, flow = refs
        for i in range(count):
            product = projected[i, :, :wide] * projected[i, :, 2 * wide :]
            gated[i] = product[:, :chunk].astype(low).astype(jnp.float32)
        taps = taps[...]
        tap_sums = [jnp.zeros((1, chunk), jnp.float32)] * 3
        for k in range(2):
            rows = (even_in, odd_in)[k][...].reshape(half * tokens, features)
            back = dot(rows, outer[...], nt).reshape(half, tokens, chunk)
            for i in range(k * half, (k + 1) * half):
                conv_out, one, two = conv_forward(place[0], taps, gated, i, count)
                gate = projected[i, :, wide : wide + chunk]
                mixed[i] = (gate * conv_out).astype(low)
                mixed_flow = back[i - k * half]
                conv_flow = mixed_flow * gate
                flow[i] = conv_flow
                for j, shifted in enumerate((two, one, gated[i])):
                    term = jnp.sum(conv_flow * shifted, axis=0, keepdims=True)
                    tap_sums[j] = tap_sums[j] + term
                flows[i, :, wide : wide + chunk] = (mixed_flow * conv_out).astype(low)
        for j in range(3):
            tap_out[j : j + 1, :] = tap_sums[j]
        row = lax.broadcasted_iota(jnp.int32, (tokens, chunk), 0)
        for i in range(count):
            here = flow[i]
            at, inside = block_neighbour(place[0], i, count, 1)
            beyond = jnp.where(inside, flow[at, :8, :], 0.0)
            first, second = beyond[0:1, :], beyond[1:2, :]
            one = jnp.where(row == tokens - 1, first, pltpu.roll(here, tokens - 1, 0))
            two = jnp.where(
                row == tokens - 1,
                second,
                jnp.where(row == tokens - 2, first, pltpu.roll(here, tokens - 2, 0)),
            )
            gated_flow = taps[2:3, :] * here + taps[1:2, :] * one + taps[0:1, :] * two
            x_part = projected[i, :, 2 * wide : 2 * wide + chunk]
            b_part = projected[i, :, :chunk]
            flows[i, :, :chunk] = (gated_flow * x_part).astype(low)
            flows[i, :, 2 * wide : 2 * wide + chunk] = (gated_flow * b_part).astype(low)
            if wide > chunk:
                for g in range(3):
                    gap = jnp.zeros((tokens, wide - chunk), low)
                    flows[i, :, g * wide + chunk : (g + 1) * wide] = gap
        rows = flows[:half].reshape(half * tokens, 3 * wide)
        even[...] = dot(rows, inner[...], nt).reshape(half, tokens, features)
        rows = flows[half:].reshape(half * tokens, 3 * wide)
        odd[...] = dot(rows, inner[...], nt).reshape(half, tokens, features).astype(low)

    return plain_call(
        body,
        [
            shaped((half, tokens, features)),
            shaped((half, tokens, features), low),
            shaped((count, tokens, 3 * wide), low),
            shaped((count, tokens, chunk), low),
            shaped((3, chunk)),
        ],
        scalars=1,
        scratch=[pltpu.VMEM((count, tokens, chunk), jnp.float32)] * 2,
    )(place_of("seq"), *blocks, projected, inner, outer, taps)


def mixer_grads(normed, flows, mixed, lows, rows, rotated):
    seqs, rings = lax.axis_size("seq"), lax.axis_size("fsdp")
    features, width = normed[0].shape[-1], flows.shape[-1]
    half = normed[0].shape[0]
    wide = width // 3
    chunk = mixed.shape[-1]

    def body(place, normed_even, normed_odd, flows, mixed, low_even, low_odd, *refs):
        inner, outer = refs[-2:]
        outs = refs[:rings] if rotated else [refs[0].at[j] for j in range(rings)]
        long = lambda array: array.reshape(-1, array.shape[-1])
        for g in range(3):
            at = slice(g * wide, (g + 1) * wide)
            part = dot(long(normed_even[...]), long(flows[:half, :, at]), tn)
            part = part + dot(long(normed_odd[...]), long(flows[half:, :, at]), tn)
            part = part.astype(low)
            for i in range(seqs * rings):
                inner[i // rings, i % rings, :, at] = part[i * rows : (i + 1) * rows]
        part = dot(long(mixed[:half]), long(low_even[...]), tn)
        part = part + dot(long(mixed[half:]), long(low_odd[...]), tn)
        part = part.astype(low)
        for f in range(rings):
            outer[f] = part[f * rows : (f + 1) * rows]
        for j in range(rings):
            f = lax.bitwise_xor(place[0], jnp.int32(j)) if rotated else j
            for s in range(seqs):
                for g in range(3):
                    piece = inner[s, f, :, g * wide : g * wide + chunk]
                    outs[j][s, :, g * chunk : (g + 1) * chunk] = piece
                outs[j][s, :, 3 * chunk :] = outer[f, :, s * chunk : (s + 1) * chunk]

    shape = (seqs, rows, 4 * chunk)
    return plain_call(
        body,
        [shaped(shape, low)] * rings if rotated else [shaped((rings,) + shape, low)],
        scalars=1,
        scratch=[
            pltpu.VMEM((seqs, rings, rows, width), low),
            pltpu.VMEM((rings, rows, features), low),
        ],
        cost=(24 * half * normed[0].size, 8 * normed[0].size),
    )(place_of("fsdp"), *normed, flows, mixed, *lows)


def hidden_tile(hidden):
    return 256 if hidden % 256 == 0 else 128


def feed_specs(features, hidden):
    tile = hidden_tile(hidden)
    steps = hidden // tile
    return (
        pl.BlockSpec((features, tile), lambda i: (0, i)),
        pl.BlockSpec((features, tile), lambda i: (0, i + steps)),
        pl.BlockSpec((tile, features), lambda i: (i, 0)),
    )


def feed_forward(blocks, up_matrix, down, own):
    count = len(blocks)
    tokens, features = blocks[0].shape
    hidden = down.shape[0]
    tile = hidden_tile(hidden)
    steps = hidden // tile

    def body(*refs):
        gate_matrix, up_matrix, down = refs[count : count + 3]
        outs = refs[count + 3 : 2 * count + 3]
        gate_out, up_out, hidden_out, rows, total = refs[2 * count + 3 :]
        step = pl.program_id(0)

        @pl.when(step == 0)
        def _():
            for i in range(count):
                rows[i * tokens : (i + 1) * tokens] = refs[i][...]
            total[...] = jnp.zeros_like(total)

        gate = dot(rows[...], gate_matrix[...])
        up = dot(rows[...], up_matrix[...])
        gate_out[...] = gate
        up_out[...] = up
        value = (gate * jax.nn.sigmoid(gate) * up).astype(low)
        hidden_out[...] = value
        total[...] += dot(value, down[...])

        @pl.when(step == steps - 1)
        def _():
            for i in range(count):
                outs[i][...] = total[i * tokens : (i + 1) * tokens].astype(outs[i].dtype)

    columns = pl.BlockSpec((count * tokens, tile), lambda i: (0, i))
    outs = kernel_call(
        body,
        (steps,),
        [whole((tokens, features))] * count + list(feed_specs(features, hidden)),
        [whole((tokens, features))] * count + [columns] * 3,
        [
            shaped((tokens, features), jnp.float32 if own and i == 0 else low)
            for i in range(count)
        ]
        + [shaped((count * tokens, hidden), kind) for kind in (jnp.float32, jnp.float32, low)],
        scratch=[
            pltpu.VMEM((count * tokens, features), low),
            pltpu.VMEM((count * tokens, features), jnp.float32),
        ],
    )(*blocks, up_matrix, up_matrix, down)
    return outs[:count], outs[count:]


def feed_backward(blocks, gates, ups, up_matrix, down, own):
    count = len(blocks)
    tokens, features = blocks[0].shape
    hidden = down.shape[0]
    tile = hidden_tile(hidden)
    steps = hidden // tile

    def body(*refs):
        gate_part, up_part, gate_matrix, up_matrix, down = refs[count : count + 5]
        outs = refs[count + 5 : 2 * count + 5]
        gate_out, up_out, rows, total = refs[2 * count + 5 :]
        step = pl.program_id(0)

        @pl.when(step == 0)
        def _():
            for i in range(count):
                rows[i * tokens : (i + 1) * tokens] = refs[i][...]
            total[...] = jnp.zeros_like(total)

        flow = dot(rows[...], down[...], nt)
        gate = gate_part[...]
        smooth = jax.nn.sigmoid(gate)
        gate_flow = flow * up_part[...] * (smooth * (1.0 + gate * (1.0 - smooth)))
        gate_flow = gate_flow.astype(low)
        up_flow = (flow * (gate * smooth)).astype(low)
        gate_out[...] = gate_flow
        up_out[...] = up_flow
        total[...] += dot(gate_flow, gate_matrix[...], nt) + dot(up_flow, up_matrix[...], nt)

        @pl.when(step == steps - 1)
        def _():
            for i in range(count):
                outs[i][...] = total[i * tokens : (i + 1) * tokens].astype(outs[i].dtype)

    columns = pl.BlockSpec((count * tokens, tile), lambda i: (0, i))
    outs = kernel_call(
        body,
        (steps,),
        [whole((tokens, features))] * count + [columns] * 2 + list(feed_specs(features, hidden)),
        [whole((tokens, features))] * count + [columns] * 2,
        [
            shaped((tokens, features), jnp.float32 if own and i == 0 else low)
            for i in range(count)
        ]
        + [shaped((count * tokens, hidden), low)] * 2,
        scratch=[
            pltpu.VMEM((count * tokens, features), low),
            pltpu.VMEM((count * tokens, features), jnp.float32),
        ],
    )(*blocks, gates, ups, up_matrix, up_matrix, down)
    return outs[:count], outs[count:]


def feed_grads(normed, gate_flows, up_flows):
    count, groups = len(normed), len(gate_flows)
    tokens, features = normed[0].shape
    hidden = gate_flows[0].shape[1]
    sizes = [flow.shape[0] for flow in gate_flows]
    starts = [sum(sizes[:i]) for i in range(groups)]
    tile = hidden_tile(hidden)
    steps = hidden // tile

    def body(*refs):
        flows = refs[count : count + 2 * groups]
        out, rows, columns = refs[count + 2 * groups :]
        step = pl.program_id(0)

        @pl.when(step == 0)
        def _():
            for i in range(count):
                rows[i * tokens : (i + 1) * tokens] = refs[i][...]

        for half in range(2):

            @pl.when(lax.div(step, steps) == half)
            def _():
                for i in range(groups):
                    at = slice(starts[i], starts[i] + sizes[i])
                    columns[at] = flows[half * groups + i][...]

        out[...] = dot(rows[...], columns[...], tn).astype(low)

    gate_specs = [
        pl.BlockSpec((size, tile), lambda i: (0, jnp.minimum(i, steps - 1))) for size in sizes
    ]
    up_specs = [
        pl.BlockSpec((size, tile), lambda i: (0, jnp.maximum(i - steps, 0))) for size in sizes
    ]
    return kernel_call(
        body,
        (2 * steps,),
        [whole((tokens, features))] * count + gate_specs + up_specs,
        pl.BlockSpec((features, tile), lambda i: (0, i)),
        shaped((features, 2 * hidden), low),
        scratch=[
            pltpu.VMEM((count * tokens, features), low),
            pltpu.VMEM((count * tokens, tile), low),
        ],
        cost=(12 * count * tokens * features * hidden, 24 * features * hidden),
    )(*normed, *gate_flows, *up_flows)


def down_grads(hiddens, flows):
    count, groups = len(flows), len(hiddens)
    tokens, features = flows[0].shape
    hidden = hiddens[0].shape[1]
    sizes = [values.shape[0] for values in hiddens]
    starts = [sum(sizes[:i]) for i in range(groups)]
    tile = hidden_tile(hidden)

    def body(*refs):
        hiddens = refs[count : count + groups]
        out, rows, columns = refs[count + groups :]

        @pl.when(pl.program_id(0) == 0)
        def _():
            for i in range(count):
                rows[i * tokens : (i + 1) * tokens] = refs[i][...]

        for i in range(groups):
            columns[starts[i] : starts[i] + sizes[i]] = hiddens[i][...]
        out[...] = dot(columns[...], rows[...], tn).astype(low)

    return kernel_call(
        body,
        (hidden // tile,),
        [whole((tokens, features))] * count
        + [pl.BlockSpec((size, tile), lambda i: (0, i)) for size in sizes],
        pl.BlockSpec((tile, features), lambda i: (i, 0)),
        shaped((hidden, features), low),
        scratch=[
            pltpu.VMEM((count * tokens, features), low),
            pltpu.VMEM((count * tokens, tile), low),
        ],
        cost=(6 * count * tokens * features * hidden, 12 * features * hidden),
    )(*flows, *hiddens)


def join_blocks(blocks):
    def body(*refs):
        for i in range(len(blocks)):
            refs[len(blocks) + i][...] = refs[i][...]

    return plain_call(body, [shaped(block.shape, block.dtype) for block in blocks])(*blocks)


def groups_of(blocks):
    return [blocks[:2]] + [[block] for block in blocks[2:]]


def return_sums(sums):
    return [sums[0]] + [fsdp_swap(sums[j], j) for j in range(1, len(sums))]


def adam_update(weight, first, second, gradient, rate, decay):
    first_new = beta_one * first + (1.0 - beta_one) * gradient
    second_new = beta_two * second + (1.0 - beta_two) * gradient * gradient
    first_hat = first_new / (1.0 - beta_one**STEP)
    second_hat = second_new / (1.0 - beta_two**STEP)
    weight_new = weight - rate * (first_hat / (jnp.sqrt(second_hat) + eps_adam) + decay * weight)
    return (first_new, second_new, weight_new)


def local(
    inputs,
    cotangent,
    mix_weight,
    mix_first,
    mix_second,
    feed_weight,
    feed_first,
    feed_second,
    down_weight,
    down_first,
    down_second,
    gain_weight,
    gain_first,
    gain_second,
    tap_weight,
    tap_first,
    tap_second,
):
    sequences, length, features = inputs.shape
    seqs, rings = lax.axis_size("seq"), lax.axis_size("fsdp")
    rows = mix_weight.shape[1]
    chunk = features // seqs
    wide = -(-chunk // 128) * 128
    cotangent = cotangent.reshape(-1, features)
    Order.mark = jnp.zeros(mark_shape.shape, mark_shape.dtype)

    mixes, feeds = [None] * LAYERS, [None] * LAYERS
    vector_blocks = vectors_start(gain_weight, tap_weight)
    feed_swap = swap_feed(pack_feed(feed_weight, 0))
    mix_packed = pack_mix(mix_weight, 0, vector_blocks[1:])
    mix_swap = swap_mix(mix_packed)
    down_rows = gather_rows(pack_down(down_weight, 0))
    both, vector_blocks = vectors_middle(vector_blocks)
    mix_pieces = gather_fsdp(join_mix(mix_swap, mix_packed))
    feeds[0] = (gather_rows(assemble_feed(feed_swap)), down_rows)
    later_packed = pack_mix(mix_weight, 1)
    later_swap = swap_mix(later_packed)
    vector_blocks = stack_pairs(vector_blocks)
    later_piece = join_mix(later_swap, later_packed, mix_pieces[1:2])
    later_mix = lax.all_gather(
        later_piece.reshape(-1, later_piece.shape[-1]), "fsdp", axis=0, tiled=True
    ).reshape((rings,) + later_piece.shape)
    gain_rows, tap_rows = vectors_end(both, vector_blocks)
    stream, normed = first_norm(inputs.reshape(-1, features), gain_rows[0, 0], ())
    blocks = send_seq(normed)
    later_feed = pack_feed(feed_weight, 1)
    *blocks, down_packed = stack_pairs(blocks, mix_pieces[2:], [pack_down(down_weight, 1)])
    later_down = gather_rows(down_packed)
    mixes[0] = assemble_mix(mix_pieces, wide)

    kept = []
    for layer in range(LAYERS):
        last = layer + 1 == LAYERS
        gathered = blocks
        projected, even, odd = mixer_forward(blocks, *mixes[layer], tap_rows[layer])
        odd = seq_swap(odd, 1)
        if last:
            flow_low = join_blocks(gather_fsdp(flow_low))
            (sums,) = pair_sum(even, odd)
        else:
            sums, later_feed = pair_sum(even, odd, (), [later_feed])
            later_feed = swap_feed(later_feed)
        middle, normed_two = finish(
            stream, sums, gain_rows[layer, 1], feeds[layer] if last else ()
        )
        two_blocks = gather_fsdp(normed_two)
        if not last:
            feeds[1] = (gather_rows(assemble_feed(later_feed)), later_down)
        sums, values = [], []
        for number, group in enumerate(groups_of(two_blocks)):
            outs, saved = feed_forward(group, *feeds[layer], number == 0)
            sums += outs
            values.append(saved)
        kept.append((stream, middle, gathered, projected, two_blocks, values))
        sums = return_sums(sums)
        if not last:
            stream, normed, flow_low = finish(
                middle, sums, gain_rows[layer + 1, 0], (), [cotangent]
            )
            blocks = stack_pairs(send_seq(normed))
            mixes[1] = assemble_mix([later_mix], wide)

    states = (
        (mix_weight, mix_first, mix_second),
        (feed_weight, feed_first, feed_second),
        (down_weight, down_first, down_second),
    )
    new = [None] * 3
    gain_grads, tap_grads = [None] * LAYERS, [None] * LAYERS
    flow = cotangent
    for layer in reversed(range(LAYERS)):
        last = layer + 1 == LAYERS
        stream, middle, gathered, projected, two_blocks, values = kept[layer]
        back_sums, gate_flows, up_flows = [], [], []
        if not last:
            even, odd = split_down(later_down, ())
            odd = seq_swap(odd, 1)
        for number, group in enumerate(groups_of(flow_low)):
            gates, ups, _ = values[number]
            outs, (gate_flow, up_flow) = feed_backward(
                group, gates, ups, *feeds[layer], number == 0
            )
            back_sums += outs
            gate_flows.append(gate_flow)
            up_flows.append(up_flow)
            if number == 0 and not last:
                (later_down,) = pair_sum(even, odd)
        if last:
            outputs = finish(middle, sums, None).reshape(inputs.shape)
        back_sums = return_sums(back_sums)
        down_part = down_grads([value[2] for value in values], flow_low)
        middle_flow, middle_low, gain_two = finish_back(
            flow, back_sums, middle, gain_rows[layer, 1]
        )
        blocks = send_seq(middle_low)
        feed_part = feed_grads(two_blocks, gate_flows, up_flows)
        if not last:
            later_feed = split_feed(later_feed, rows)
        even, odd, feed_part = stack_pairs(blocks, (), [feed_part])
        feed_part = scatter_rows(feed_part)
        blocks = even, odd
        even, odd, flows, mixed, tap_grads[layer] = mixer_backward(
            blocks, projected, *mixes[layer], tap_rows[layer]
        )
        (sums,) = pair_sum(even, seq_swap(odd, 1))
        mix_part = mixer_grads(gathered, flows, mixed, blocks, rows, not last)
        flow, low_flow, gain_one, *mix_part = finish_back(
            middle_flow,
            sums,
            stream,
            gain_rows[layer, 0],
            mix_part,
            () if last else later_feed[1:],
        )
        if not last:
            mix_part = return_sums(mix_part)
        gain_grads[layer] = jnp.concatenate([gain_one, gain_two])
        if last:
            flow_low = gather_fsdp(low_flow)
            later_mix = lax.psum_scatter(
                mix_part[0].reshape(-1, mix_part[0].shape[-1]),
                "fsdp",
                scatter_dimension=0,
                tiled=True,
            ).reshape(mix_part[0].shape[1:])
            later_feed, later_down = feed_part, down_part
    new[1] = feed_adam(later_feed, states[1], 1, new[1])
    even, odd = split_down(down_part, mix_part[1:3])
    odd = seq_swap(odd, 1)
    new[2] = down_adam(later_down, states[2], 1, new[2])
    (down_part,) = pair_sum(even, odd, mix_part[3:])
    gain_grad, tap_grad = vector_gradients(
        jnp.stack(gain_grads), jnp.stack(tap_grads), gain_weight.shape[-1]
    )
    mix_part = mix_reduce([mix_part, [later_mix]])
    feed_part = split_feed(feed_part, rows)
    new[2] = down_adam(down_part, states[2], 0, new[2])
    new[0] = mix_adam(mix_part, states[0])
    new[1] = feed_adam(feed_part, states[1], 0, new[1])
    input_grad = flow.reshape(sequences, length, features)
    gain_new = adam_update(gain_weight, gain_first, gain_second, gain_grad, rate_vector, 0.0)
    tap_new = adam_update(tap_weight, tap_first, tap_second, tap_grad, rate_vector, 0.0)
    matrices = [(part[1], part[2], part[0]) for part in new]
    return (outputs, input_grad, *sum(matrices, ()), *gain_new, *tap_new)


def solution(mesh):
    tokens = P("fsdp", "seq", None)
    rows = P(None, ("seq", "fsdp"), None)
    last = P(None, None, ("seq", "fsdp"))
    return jax.shard_map(
        local,
        mesh=mesh,
        in_specs=(tokens,) * 2 + (rows,) * 9 + (last,) * 6,
        out_specs=(tokens,) * 2 + (rows,) * 9 + (last,) * 6,
        check_vma=False,
    )
```

```python
import math

import jax
import jax.numpy as jnp
from jax import lax
from jax.experimental import pallas as pl
from jax.experimental.pallas import tpu as pltpu
from jax.sharding import PartitionSpec as P

LAYERS = 2
STEP = 10

eps_norm = 1e-05
eps_adam = 1e-08
beta_one = 0.9
beta_two = 0.95
rate_matrix = 0.05
rate_vector = 0.6
decay_matrix = 0.1

low = jnp.bfloat16


def dot(left, right, sides=((1,), (0,))):
    return lax.dot_general(left, right, (sides, ((), ())), preferred_element_type=jnp.float32)


nt = ((1,), (1,))
tn = ((0,), (0,))


def seq_order():
    count = lax.axis_size("seq")
    return list(range(0, count, 2)) + list(range(1, count, 2))


def seq_swap(array, by):
    count = lax.axis_size("seq")
    return lax.ppermute(array, "seq", [(i, i ^ by) for i in range(count)])


def send_seq(array):
    return [array] + [seq_swap(array, by) for by in range(2, lax.axis_size("seq"), 2)]


def fsdp_swap(array, by):
    count = lax.axis_size("fsdp")
    return lax.ppermute(array, "fsdp", [(i, i ^ by) for i in range(count)])


def gather_fsdp(array):
    count = lax.axis_size("fsdp")
    return [array] + [fsdp_swap(array, by) for by in range(1, count)]


def small_scatter_seq(parts):
    half = parts.shape[0] // 2
    total = parts[:half] + seq_swap(parts[half:], 1)
    for i in range(1, half):
        total = total.at[0].add(seq_swap(total[i], 2 * i))
    return total[0]


def small_scatter_fsdp(parts):
    total = parts[0]
    for by in range(1, parts.shape[0]):
        total = total + fsdp_swap(parts[by], by)
    return total


def stack_pairs(blocks, earlier=(), carried=()):
    def body(*refs):
        for i in range(len(blocks)):
            refs[-1][i] = refs[i][...]

    shape = (len(blocks),) + blocks[0].shape
    even, *rest = plain_call(
        body, [shaped(shape, blocks[0].dtype)], earlier=earlier, carried=carried
    )(*blocks)
    return even, seq_swap(even, 1), *rest


def pad_last(array, width):
    return jnp.pad(array, [(0, 0)] * (array.ndim - 1) + [(0, width - array.shape[-1])])


def place_of(axis):
    return lax.axis_index(axis).astype(jnp.int32).reshape(1)


scalar = pl.BlockSpec(memory_space=pltpu.SMEM)
held = pl.BlockSpec(memory_space=pltpu.VMEM)


def shaped(shape, kind=jnp.float32):
    return jax.ShapeDtypeStruct(shape, kind)


class Order:
    mark = None


mark_shape = jax.ShapeDtypeStruct((8, 128), jnp.float32)
anywhere = pl.BlockSpec(memory_space=pltpu.HBM)


def bytes_of(shape, kind):
    return math.prod(shape) * jnp.dtype(kind).itemsize


def vmem_of(operands, in_specs, out_shape, out_specs, scratch, grid):
    total = 0
    for array, spec in [*zip(operands, in_specs), *zip(out_shape, out_specs)]:
        if spec is anywhere or spec is scalar:
            continue
        if grid:
            total += 2 * bytes_of(spec.block_shape, array.dtype)
        else:
            total += bytes_of(array.shape, array.dtype)
    for array in scratch:
        total += bytes_of(array.shape, array.dtype)
    return total + total // 2 + 4 * 1024 * 1024


def ordered_call(body, operands, in_specs, out_specs, out_shape, aliases, scratch, grid, cost):
    given, made = len(operands), len(out_shape)

    def marked(*refs):
        body(*refs[:given], *refs[given + 1 : given + 1 + made], *refs[given + 2 + made :])

    outs = pl.pallas_call(
        marked,
        in_specs=list(in_specs) + [anywhere],
        out_specs=list(out_specs) + [anywhere],
        out_shape=list(out_shape) + [mark_shape],
        scratch_shapes=list(scratch),
        input_output_aliases=aliases,
        compiler_params=pltpu.CompilerParams(
            vmem_limit_bytes=56 << 20
            if cost[0] or aliases and not grid
            else min(vmem_of(operands, in_specs, out_shape, out_specs, scratch, grid), 60 << 20)
        ),
        cost_estimate=pl.CostEstimate(
            flops=cost[0], bytes_accessed=cost[1], transcendentals=0
        ),
        **grid,
    )(*operands, Order.mark)
    Order.mark = outs[-1]
    return outs[:-1]


def kernel_call(
    body, grid, in_specs, out_specs, out_shape, aliases=None, scratch=(), cost=(0, 0)
):
    single = not isinstance(out_shape, list)

    def run(*operands):
        outs = ordered_call(
            body,
            operands,
            in_specs,
            [out_specs] if single else out_specs,
            [out_shape] if single else out_shape,
            aliases or {},
            scratch,
            dict(grid=grid),
            cost,
        )
        return outs[0] if single else outs

    return run


def plain_call(
    body, out_shape, scalars=0, scratch=(), earlier=(), carried=(), cost=(0, 0)
):
    def run(*operands):
        given, made, more = len(operands), len(out_shape), len(earlier) + len(carried)

        def rest(*refs):
            outs = refs[given + more :]
            body(*refs[:given], *outs[:made], *outs[made + len(carried) :])

        first = given + len(earlier)
        return ordered_call(
            rest,
            (*operands, *earlier, *carried),
            [scalar] * scalars + [held] * (given - scalars) + [anywhere] * more,
            [held] * made + [anywhere] * len(carried),
            [*out_shape, *(jax.ShapeDtypeStruct(x.shape, x.dtype) for x in carried)],
            {first + i: made + i for i in range(len(carried))},
            scratch,
            {},
            cost,
        )

    return run


def whole(shape):
    return pl.BlockSpec(shape, lambda i: (0,) * len(shape))


def pack_mix(mix_weight, layer, earlier=()):
    seqs = lax.axis_size("seq")
    rows, columns = mix_weight.shape[1:]
    features = columns // 4
    chunk = features // seqs

    def body(place, weight, *refs):
        out = refs[-1]
        for s in range(seqs):
            slot = lax.bitwise_xor(place[0], jnp.int32(s))
            for g in range(4):
                start = g * features + s * chunk
                piece = weight[0, :, start : start + chunk].astype(low)
                out[slot if g < 3 else s, :, g * chunk : (g + 1) * chunk] = piece

    shape = (seqs, rows, 4 * chunk)
    return kernel_call(
        body,
        (1,),
        [scalar, pl.BlockSpec((1, rows, columns), lambda i: (layer, 0, 0))]
        + [anywhere] * len(earlier),
        whole(shape),
        jax.ShapeDtypeStruct(shape, low),
    )(place_of("seq"), mix_weight, *earlier)


def assemble_mix(pieces, wide):
    rings = lax.axis_size("fsdp")
    rotated = len(pieces) == rings
    seqs, rows, width = pieces[0].shape[-3:]
    chunk = width // 4
    features = seqs * chunk

    def body(place_seq, place_fsdp, *refs):
        inner_out, outer_out = refs[-2:]
        for j in range(rings):
            f = lax.bitwise_xor(place_fsdp[0], jnp.int32(j)) if rotated else j
            part = refs[j] if rotated else refs[0].at[j]
            for s in range(seqs):
                owner = lax.bitwise_xor(place_seq[0], jnp.int32(s))
                for g in range(3):
                    piece = part[s, :, g * chunk : (g + 1) * chunk]
                    if wide > chunk:
                        gap = jnp.zeros((rows, wide - chunk), low)
                        piece = jnp.concatenate([piece, gap], axis=1)
                    inner_out[owner, f, :, g * wide : (g + 1) * wide] = piece
                outer_out[f, :, s * chunk : (s + 1) * chunk] = part[s, :, 3 * chunk :]

    inner_shape = (seqs, rings, rows, 3 * wide)
    outer_shape = (rings, rows, features)
    inner, out = plain_call(
        body, [shaped(inner_shape, low), shaped(outer_shape, low)], scalars=2
    )(place_of("seq"), place_of("fsdp"), *pieces)
    return inner.reshape(features, 3 * wide), out.reshape(rings * rows, features)


def swap_mix(packed):
    seqs = lax.axis_size("seq")
    return [packed[:1]] + [seq_swap(packed[by : by + 1], by) for by in range(1, seqs)]


def join_mix(parts, packed, earlier=()):
    seqs = len(parts)

    def body(*refs):
        out = refs[-1]
        split = out.shape[-1] // 4 * 3
        for s in range(seqs):
            out[s, :, :split] = refs[s][0, :, :split]
            out[s, :, split:] = refs[seqs][s, :, split:]

    return plain_call(body, [shaped(packed.shape, low)], earlier=earlier)(*parts, packed)[0]


def tall_of(block):
    step = 128 // min(lax.axis_size("seq"), 128)
    return -(-block // step) * step


def pack_feed(feed_weight, layer):
    seqs, rings = lax.axis_size("seq"), lax.axis_size("fsdp")
    rows, columns = feed_weight.shape[1:]
    half = columns // 2
    block = half // (seqs * rings)
    tall = tall_of(block)

    def body(place, weight, out):
        for f in range(rings):
            slot = lax.bitwise_xor(place[0], jnp.int32(f))
            for g in range(2):
                for s in range(seqs):
                    start = g * half + (s * rings + f) * block
                    piece = weight[0, :, start : start + block].astype(low)
                    if tall > block:
                        piece = jnp.concatenate(
                            [piece, jnp.zeros((rows, tall - block), low)], axis=1
                        )
                    to = (g * seqs + s) * tall
                    out[slot, :, to : to + tall] = piece

    shape = (rings, rows, 2 * seqs * tall)
    return kernel_call(
        body,
        (1,),
        [scalar, pl.BlockSpec((1, rows, columns), lambda i: (layer, 0, 0))],
        whole(shape),
        jax.ShapeDtypeStruct(shape, low),
    )(place_of("fsdp"), feed_weight)


def assemble_feed(pieces):
    rings = len(pieces)

    def body(place, *refs):
        out = refs[rings]
        for j in range(rings):
            out[lax.bitwise_xor(place[0], jnp.int32(j))] = refs[j][0]

    shape = (rings,) + pieces[0].shape[1:]
    return kernel_call(
        body,
        (1,),
        [scalar] + [whole(piece.shape) for piece in pieces],
        whole(shape),
        jax.ShapeDtypeStruct(shape, low),
    )(place_of("fsdp"), *pieces)


def swap_feed(packed):
    rings = lax.axis_size("fsdp")
    return [packed[:1]] + [fsdp_swap(packed[by : by + 1], by) for by in range(1, rings)]


def gather_rows(part):
    return lax.all_gather(part.reshape(-1, part.shape[-1]), "seq", axis=0, tiled=True)


def pack_down(down_weight, layer):
    block = down_weight.shape[1]
    return jnp.pad(down_weight[layer].astype(low), ((0, tall_of(block) - block), (0, 0)))


def adam_kernel(load, scalars, grads, state, layer, previous, scratch=(), earlier=()):
    weight = state[0]
    rows, columns = weight.shape[1:]
    tile = 16 if rows % 16 == 0 else rows
    width = 768
    steps = rows // tile
    if layer is None:
        each = steps
        where = lambda i: (lax.div(i, each), lax.rem(i, each), 0)
        specs = [pl.BlockSpec((1, tile, grad.shape[-1]), where) for grad in grads]
        steps = LAYERS * each
    else:
        where = lambda i: (layer, i, 0)
        specs = [
            pl.BlockSpec(
                grad.shape if tile == rows else (tile, grad.shape[-1]), lambda i: (i, 0)
            )
            for grad in grads
        ]
    part = pl.BlockSpec((1, tile, columns), where)
    kept = (0 if previous is None else 3) + len(earlier)
    before = len(scalars) + len(grads)

    def body(*refs):
        weight, first, second = refs[before : before + 3]
        weight_out, first_out, second_out, total = refs[before + 3 + kept : before + 7 + kept]
        load(refs[: len(scalars)], refs[len(scalars) : before], refs[before + 7 + kept :], total)
        for start in range(0, columns, width):
            at = slice(start, start + width)
            gradient = total[:, at]
            old = weight[0, :, at]
            first_new = beta_one * first[0, :, at] + (1.0 - beta_one) * gradient
            second_new = beta_two * second[0, :, at] + (1.0 - beta_two) * gradient * gradient
            first_hat = first_new / (1.0 - beta_one**STEP)
            second_hat = second_new / (1.0 - beta_two**STEP)
            step = first_hat / (jnp.sqrt(second_hat) + eps_adam) + decay_matrix * old
            first_out[0, :, at] = first_new
            second_out[0, :, at] = second_new
            weight_out[0, :, at] = old - rate_matrix * step

    return kernel_call(
        body,
        (steps,),
        [scalar] * len(scalars)
        + specs
        + [part] * 3
        + [anywhere] * kept,
        [part] * 3,
        [shaped(weight.shape)] * 3,
        aliases={before + 3 + i: i for i in range(kept - len(earlier))},
        scratch=[pltpu.VMEM((tile, columns), jnp.float32), *(make(tile) for make in scratch)],
        cost=(0, 26 * rows * columns),
    )(*scalars, *grads, *state, *(previous or ()), *earlier)


def mix_reduce(layers, earlier):
    seqs, rows, width = layers[0][0].shape
    count = len(layers)
    chunk = width // 4
    starts = [sum(len(pieces) for pieces in layers[:i]) for i in range(count + 1)]

    def body(place, *refs):
        inner_out, outer_out = refs[starts[-1] :]
        for layer in range(count):
            parts = refs[starts[layer] : starts[layer + 1]]
            for s in range(seqs):
                total = parts[0][s].astype(jnp.float32)
                for part in parts[1:]:
                    total = total + part[s].astype(jnp.float32)
                inner_out[lax.bitwise_xor(place[0], jnp.int32(s)), layer] = total.astype(low)
                outer_out[layer, :, s * chunk : (s + 1) * chunk] = total[:, 3 * chunk :]

    inner, last = plain_call(
        body,
        [shaped((seqs, count, rows, width), low), shaped((count, rows, seqs * chunk))],
        scalars=1,
        earlier=earlier,
    )(place_of("seq"), *sum((list(pieces) for pieces in layers), []))
    return [inner[0]] + [seq_swap(inner[j], j) for j in range(1, seqs)] + [last]


def mix_adam(grads, state):
    seqs = lax.axis_size("seq")
    features = state[0].shape[2] // 4
    chunk = features // seqs

    def load(scalars, grads, scratch, total):
        for s in range(seqs):
            scratch[0][lax.bitwise_xor(scalars[0][0], jnp.int32(s))] = grads[s][0]
        for s in range(seqs):
            for g in range(3):
                start = g * features + s * chunk
                piece = scratch[0][s, :, g * chunk : (g + 1) * chunk]
                total[:, start : start + chunk] = piece.astype(jnp.float32)
        total[:, 3 * features :] = grads[seqs][0]

    return adam_kernel(
        load,
        [place_of("seq")],
        grads,
        state,
        None,
        None,
        [lambda tile: pltpu.VMEM((seqs, tile, 4 * chunk), low)],
    )


def scatter_rows(grad):
    return lax.psum_scatter(grad, "seq", scatter_dimension=0, tiled=True)


def split_feed(part, rows):
    rings = lax.axis_size("fsdp")
    part = part.reshape(rings, rows, -1)

    def body(place, part, *outs):
        for j in range(rings):
            outs[j][...] = part[lax.bitwise_xor(place[0], jnp.int32(j))]

    pieces = plain_call(body, [shaped(part.shape[1:], low)] * rings, scalars=1)(
        place_of("fsdp"), part
    )
    return return_sums(pieces)


def feed_adam(grads, state, layer, previous):
    seqs, rings = lax.axis_size("seq"), lax.axis_size("fsdp")
    half = state[0].shape[2] // 2
    block = half // (seqs * rings)
    tall = tall_of(block)

    def load(scalars, grads, scratch, total):
        for j in range(rings):
            scratch[0][lax.bitwise_xor(scalars[0][0], jnp.int32(j))] = grads[j][...]
        for f in range(rings):
            for g in range(2):
                for s in range(seqs):
                    start = g * half + (s * rings + f) * block
                    at = (g * seqs + s) * tall
                    piece = scratch[0][f, :, at : at + block]
                    total[:, start : start + block] = piece.astype(jnp.float32)

    return adam_kernel(
        load,
        [place_of("fsdp")],
        grads,
        state,
        layer,
        previous,
        [lambda tile: pltpu.VMEM((rings, tile, 2 * seqs * tall), low)],
    )


def down_adam(parts, state, layer, previous, earlier=()):
    def load(scalars, grads, scratch, total):
        sums = grads[0][...].astype(jnp.float32)
        for grad in grads[1:]:
            sums = sums + grad[...].astype(jnp.float32)
        total[...] = sums[: total.shape[0]]

    return adam_kernel(load, [], parts, state, layer, previous, earlier=earlier)


def split_down(part, earlier):
    seqs = lax.axis_size("seq")
    part = part.reshape(seqs, -1, part.shape[-1])

    def body(place, part, even, odd):
        for i in range(seqs):
            owner = lax.bitwise_xor(place[0], jnp.int32(i))
            (even, odd)[i % 2][i // 2] = part[owner]

    return plain_call(
        body,
        [shaped((seqs // 2,) + part.shape[1:], part.dtype)] * 2,
        scalars=1,
        earlier=earlier,
    )(place_of("seq"), part)


def place_blocks(blocks, owners, place, earlier=()):
    def body(place, *refs):
        if len(blocks[0].shape) == len(refs[-1].shape):
            refs = [ref.at[i] for ref in refs[:-1] for i in range(ref.shape[0])] + [refs[-1]]
        for block, owner in zip(refs, owners(place[0])):
            refs[-1][owner] = block[...]

    shape = blocks[0].shape
    if len(blocks) == 2:
        shape = (2 * shape[0],) + shape[1:]
    else:
        shape = (len(blocks),) + shape
    return plain_call(body, [shaped(shape, blocks[0].dtype)], scalars=1, earlier=earlier)(
        place, *blocks
    )[0]


def vectors_start(gain_weight, tap_weight):
    gains = gain_weight.reshape(2 * LAYERS, -1)
    taps = tap_weight.reshape(3 * LAYERS, -1)
    return gather_fsdp(jnp.concatenate([gains, taps], axis=0).astype(low))


def vectors_middle(blocks, earlier):
    rings = lax.axis_size("fsdp")
    both = place_blocks(
        blocks,
        lambda place: [lax.bitwise_xor(place, jnp.int32(j)) for j in range(rings)],
        place_of("fsdp"),
        earlier,
    )
    return both, send_seq(both)


def vectors_end(both, blocks):
    spread = place_blocks(
        blocks,
        lambda place: [lax.bitwise_xor(place, jnp.int32(i)) for i in seq_order()],
        place_of("seq"),
    )
    gains = jnp.transpose(spread[:, :, : 2 * LAYERS], (2, 0, 1, 3)).astype(jnp.float32)
    taps = jnp.transpose(both[:, 2 * LAYERS :], (1, 0, 2)).astype(jnp.float32)
    return gains.reshape(LAYERS, 2, 1, -1), taps.reshape(LAYERS, 3, -1)


def vector_gradients(gain_grads, tap_grads, short):
    seqs, rings = lax.axis_size("seq"), lax.axis_size("fsdp")
    place_seq, place_fsdp = lax.axis_index("seq"), lax.axis_index("fsdp")
    gains = gain_grads.reshape(2 * LAYERS, seqs, -1)
    owner = place_seq ^ jnp.array(seq_order())
    pick = (owner[:, None] == jnp.arange(seqs)[None, :]).astype(jnp.float32)
    gains = jnp.einsum("jo,koc->jkc", pick, gains, precision=lax.Precision.HIGHEST)
    gains = small_scatter_seq(gains)
    taps = tap_grads.reshape(3 * LAYERS, -1)[:, : rings * short]
    both = jnp.concatenate([gains, taps], axis=0).reshape(5 * LAYERS, rings, short)
    owner = place_fsdp ^ jnp.arange(rings)
    pick = (owner[:, None] == jnp.arange(rings)[None, :]).astype(jnp.float32)
    both = jnp.einsum("jo,koc->jkc", pick, both, precision=lax.Precision.HIGHEST)
    both = small_scatter_fsdp(both)
    return (
        both[: 2 * LAYERS].reshape(LAYERS, 2, short),
        both[2 * LAYERS :].reshape(LAYERS, 3, short),
    )


def unit_rows(values):
    row_scale = lax.rsqrt(jnp.mean(values * values, axis=-1, keepdims=True) + eps_norm)
    return values * row_scale, row_scale


def first_norm(inputs, gain, earlier):
    def body(inputs, gain, stream_out, normed_out):
        stream = inputs[...].astype(jnp.float32)
        stream_out[...] = stream
        normed_out[...] = (unit_rows(stream)[0] * gain[...]).astype(low)

    return plain_call(
        body, [shaped(inputs.shape), shaped(inputs.shape, low)], earlier=earlier
    )(inputs, gain)


def finish(base, sums, gain, earlier=(), carried=()):
    def body(*refs):
        total = refs[0][...]
        for part in refs[1 : 1 + len(sums)]:
            total = total + part[...].astype(jnp.float32)
        if gain is None:
            refs[-1][...] = total.astype(low)
        else:
            refs[-2][...] = total
            refs[-1][...] = (unit_rows(total)[0] * refs[1 + len(sums)][...]).astype(low)

    if gain is None:
        return plain_call(body, [shaped(base.shape, low)])(base, *sums)[0]
    return plain_call(
        body,
        [shaped(base.shape), shaped(base.shape, low)],
        earlier=earlier,
        carried=carried,
    )(base, *sums, gain)


def finish_back(flow, sums, stream, gain, carried=(), earlier=()):
    def body(flow, stream, gain, *refs):
        total = refs[0][...].astype(jnp.float32)
        for part in refs[1 : len(sums)]:
            total = total + part[...].astype(jnp.float32)
        unit, row_scale = unit_rows(stream[...])
        scaled = total * gain[...]
        inner_mean = jnp.mean(scaled * unit, axis=-1, keepdims=True)
        result = flow[...].astype(jnp.float32) + row_scale * (scaled - unit * inner_mean)
        refs[-3][...] = result
        refs[-2][...] = result.astype(low)
        refs[-1][...] = jnp.sum(total * unit, axis=0, keepdims=True)

    return plain_call(
        body,
        [shaped(flow.shape), shaped(flow.shape, low), shaped((1, flow.shape[1]))],
        carried=carried,
        earlier=earlier,
    )(flow, stream, gain, *sums)


def pair_sum(even, received, earlier=(), carried=()):
    half, tokens, features = even.shape

    def body(even, received, *outs):
        for i in range(half):
            total = even[i] + received[i].astype(jnp.float32)
            outs[i][...] = total.astype(outs[i].dtype)

    outs = plain_call(
        body,
        [shaped((tokens, features))] + [shaped((tokens, features), low)] * (half - 1),
        earlier=earlier,
        carried=carried,
    )(even, received)
    return [outs[0]] + [seq_swap(outs[i], 2 * i) for i in range(1, half)], *outs[half:]


def block_neighbour(place, i, count, step):
    order = list(range(0, count, 2)) + list(range(1, count, 2))
    owner = lax.bitwise_xor(place, jnp.int32(order[i])) + step
    inside = jnp.logical_and(owner >= 0, owner < count)
    number = lax.bitwise_xor(place, jnp.where(inside, owner, place))
    return lax.div(number, 2) + lax.rem(number, 2) * (count // 2), inside


def conv_forward(place, taps, gated, i, count):
    here = gated[i]
    tokens, chunk = here.shape
    at, inside = block_neighbour(place, i, count, -1)
    before = jnp.where(inside, gated[at, tokens - 8 :, :], 0.0)
    row = lax.broadcasted_iota(jnp.int32, (tokens, chunk), 0)
    last, second = before[7:8, :], before[6:7, :]
    one = jnp.where(row == 0, last, pltpu.roll(here, 1, 0))
    two = jnp.where(row == 0, second, jnp.where(row == 1, last, pltpu.roll(here, 2, 0)))
    return taps[0:1, :] * two + taps[1:2, :] * one + taps[2:3, :] * here, one, two


def mixer_forward(blocks, inner, outer, taps):
    half, tokens, features = blocks[0].shape
    count = 2 * half
    chunk = outer.shape[0]
    wide = inner.shape[1] // 3

    def body(place, even_in, odd_in, inner, outer, taps, *refs):
        projected, even, odd, gated, mixed = refs
        for k, rows in enumerate((even_in, odd_in)):
            rows = rows[...].reshape(half * tokens, features)
            for g in range(3):
                columns = slice(g * wide, (g + 1) * wide)
                part = dot(rows, inner[:, columns]).reshape(half, tokens, wide)
                projected[k * half : (k + 1) * half, :, columns] = part

        for i in range(count):
            product = projected[i, :, :wide] * projected[i, :, 2 * wide :]
            gated[i] = product[:, :chunk].astype(low).astype(jnp.float32)
        taps = taps[...]
        for i in range(count):
            conv_out = conv_forward(place[0], taps, gated, i, count)[0]
            mixed[i] = (projected[i, :, wide : wide + chunk] * conv_out).astype(low)
        rows = mixed[:half].reshape(half * tokens, chunk)
        even[...] = dot(rows, outer[...]).reshape(half, tokens, features)
        rows = mixed[half:].reshape(half * tokens, chunk)
        odd[...] = dot(rows, outer[...]).reshape(half, tokens, features).astype(low)

    return plain_call(
        body,
        [
            shaped((count, tokens, 3 * wide)),
            shaped((half, tokens, features)),
            shaped((half, tokens, features), low),
        ],
        scalars=1,
        scratch=[
            pltpu.VMEM((count, tokens, chunk), jnp.float32),
            pltpu.VMEM((count, tokens, chunk), low),
        ],
    )(place_of("seq"), *blocks, inner, outer, taps)


def mixer_backward(blocks, projected, inner, outer, taps):
    half, tokens, features = blocks[0].shape
    count = 2 * half
    chunk = outer.shape[0]
    wide = inner.shape[1] // 3

    def body(place, even_in, odd_in, projected, inner, outer, taps, *refs):
        even, odd, flows, mixed, tap_out, gated, flow = refs
        for i in range(count):
            product = projected[i, :, :wide] * projected[i, :, 2 * wide :]
            gated[i] = product[:, :chunk].astype(low).astype(jnp.float32)
        taps = taps[...]
        tap_sums = [jnp.zeros((1, chunk), jnp.float32)] * 3
        for k in range(2):
            rows = (even_in, odd_in)[k][...].reshape(half * tokens, features)
            back = dot(rows, outer[...], nt).reshape(half, tokens, chunk)
            for i in range(k * half, (k + 1) * half):
                conv_out, one, two = conv_forward(place[0], taps, gated, i, count)
                gate = projected[i, :, wide : wide + chunk]
                mixed[i] = (gate * conv_out).astype(low)
                mixed_flow = back[i - k * half]
                conv_flow = mixed_flow * gate
                flow[i] = conv_flow
                for j, shifted in enumerate((two, one, gated[i])):
                    term = jnp.sum(conv_flow * shifted, axis=0, keepdims=True)
                    tap_sums[j] = tap_sums[j] + term
                flows[i, :, wide : wide + chunk] = (mixed_flow * conv_out).astype(low)
        for j in range(3):
            tap_out[j : j + 1, :] = tap_sums[j]
        row = lax.broadcasted_iota(jnp.int32, (tokens, chunk), 0)
        for i in range(count):
            here = flow[i]
            at, inside = block_neighbour(place[0], i, count, 1)
            beyond = jnp.where(inside, flow[at, :8, :], 0.0)
            first, second = beyond[0:1, :], beyond[1:2, :]
            one = jnp.where(row == tokens - 1, first, pltpu.roll(here, tokens - 1, 0))
            two = jnp.where(
                row == tokens - 1,
                second,
                jnp.where(row == tokens - 2, first, pltpu.roll(here, tokens - 2, 0)),
            )
            gated_flow = taps[2:3, :] * here + taps[1:2, :] * one + taps[0:1, :] * two
            x_part = projected[i, :, 2 * wide : 2 * wide + chunk]
            b_part = projected[i, :, :chunk]
            flows[i, :, :chunk] = (gated_flow * x_part).astype(low)
            flows[i, :, 2 * wide : 2 * wide + chunk] = (gated_flow * b_part).astype(low)
            if wide > chunk:
                for g in range(3):
                    gap = jnp.zeros((tokens, wide - chunk), low)
                    flows[i, :, g * wide + chunk : (g + 1) * wide] = gap
        rows = flows[:half].reshape(half * tokens, 3 * wide)
        even[...] = dot(rows, inner[...], nt).reshape(half, tokens, features)
        rows = flows[half:].reshape(half * tokens, 3 * wide)
        odd[...] = dot(rows, inner[...], nt).reshape(half, tokens, features).astype(low)

    return plain_call(
        body,
        [
            shaped((half, tokens, features)),
            shaped((half, tokens, features), low),
            shaped((count, tokens, 3 * wide), low),
            shaped((count, tokens, chunk), low),
            shaped((3, chunk)),
        ],
        scalars=1,
        scratch=[pltpu.VMEM((count, tokens, chunk), jnp.float32)] * 2,
    )(place_of("seq"), *blocks, projected, inner, outer, taps)


def mixer_grads(normed, flows, mixed, lows, rows, rotated):
    seqs, rings = lax.axis_size("seq"), lax.axis_size("fsdp")
    features, width = normed[0].shape[-1], flows.shape[-1]
    half = normed[0].shape[0]
    wide = width // 3
    chunk = mixed.shape[-1]

    def body(place, normed_even, normed_odd, flows, mixed, low_even, low_odd, *refs):
        inner, outer = refs[-2:]
        outs = refs[:rings] if rotated else [refs[0].at[j] for j in range(rings)]
        long = lambda array: array.reshape(-1, array.shape[-1])
        for g in range(3):
            at = slice(g * wide, (g + 1) * wide)
            part = dot(long(normed_even[...]), long(flows[:half, :, at]), tn)
            part = part + dot(long(normed_odd[...]), long(flows[half:, :, at]), tn)
            part = part.astype(low)
            for i in range(seqs * rings):
                inner[i // rings, i % rings, :, at] = part[i * rows : (i + 1) * rows]
        part = dot(long(mixed[:half]), long(low_even[...]), tn)
        part = part + dot(long(mixed[half:]), long(low_odd[...]), tn)
        part = part.astype(low)
        for f in range(rings):
            outer[f] = part[f * rows : (f + 1) * rows]
        for j in range(rings):
            f = lax.bitwise_xor(place[0], jnp.int32(j)) if rotated else j
            for s in range(seqs):
                for g in range(3):
                    piece = inner[s, f, :, g * wide : g * wide + chunk]
                    outs[j][s, :, g * chunk : (g + 1) * chunk] = piece
                outs[j][s, :, 3 * chunk :] = outer[f, :, s * chunk : (s + 1) * chunk]

    shape = (seqs, rows, 4 * chunk)
    return plain_call(
        body,
        [shaped(shape, low)] * rings if rotated else [shaped((rings,) + shape, low)],
        scalars=1,
        scratch=[
            pltpu.VMEM((seqs, rings, rows, width), low),
            pltpu.VMEM((rings, rows, features), low),
        ],
        cost=(24 * half * normed[0].size, 8 * normed[0].size),
    )(place_of("fsdp"), *normed, flows, mixed, *lows)


def hidden_tile(hidden):
    return 256 if hidden % 256 == 0 else 128


def feed_specs(features, hidden):
    tile = hidden_tile(hidden)
    steps = hidden // tile
    return (
        pl.BlockSpec((features, tile), lambda i: (0, i)),
        pl.BlockSpec((features, tile), lambda i: (0, i + steps)),
        pl.BlockSpec((tile, features), lambda i: (i, 0)),
    )


def feed_forward(blocks, up_matrix, down, own):
    count = len(blocks)
    tokens, features = blocks[0].shape
    hidden = down.shape[0]
    tile = hidden_tile(hidden)
    steps = hidden // tile

    def body(*refs):
        gate_matrix, up_matrix, down = refs[count : count + 3]
        outs = refs[count + 3 : 2 * count + 3]
        gate_out, up_out, hidden_out, rows, total = refs[2 * count + 3 :]
        step = pl.program_id(0)

        @pl.when(step == 0)
        def _():
            for i in range(count):
                rows[i * tokens : (i + 1) * tokens] = refs[i][...]
            total[...] = jnp.zeros_like(total)

        gate = dot(rows[...], gate_matrix[...])
        up = dot(rows[...], up_matrix[...])
        gate_out[...] = gate
        up_out[...] = up
        value = (gate * jax.nn.sigmoid(gate) * up).astype(low)
        hidden_out[...] = value
        total[...] += dot(value, down[...])

        @pl.when(step == steps - 1)
        def _():
            for i in range(count):
                outs[i][...] = total[i * tokens : (i + 1) * tokens].astype(outs[i].dtype)

    columns = pl.BlockSpec((count * tokens, tile), lambda i: (0, i))
    outs = kernel_call(
        body,
        (steps,),
        [whole((tokens, features))] * count + list(feed_specs(features, hidden)),
        [whole((tokens, features))] * count + [columns] * 3,
        [
            shaped((tokens, features), jnp.float32 if own and i == 0 else low)
            for i in range(count)
        ]
        + [shaped((count * tokens, hidden), kind) for kind in (jnp.float32, jnp.float32, low)],
        scratch=[
            pltpu.VMEM((count * tokens, features), low),
            pltpu.VMEM((count * tokens, features), jnp.float32),
        ],
    )(*blocks, up_matrix, up_matrix, down)
    return outs[:count], outs[count:]


def feed_backward(blocks, gates, ups, up_matrix, down, own):
    count = len(blocks)
    tokens, features = blocks[0].shape
    hidden = down.shape[0]
    tile = hidden_tile(hidden)
    steps = hidden // tile

    def body(*refs):
        gate_part, up_part, gate_matrix, up_matrix, down = refs[count : count + 5]
        outs = refs[count + 5 : 2 * count + 5]
        gate_out, up_out, rows, total = refs[2 * count + 5 :]
        step = pl.program_id(0)

        @pl.when(step == 0)
        def _():
            for i in range(count):
                rows[i * tokens : (i + 1) * tokens] = refs[i][...]
            total[...] = jnp.zeros_like(total)

        flow = dot(rows[...], down[...], nt)
        gate = gate_part[...]
        smooth = jax.nn.sigmoid(gate)
        gate_flow = flow * up_part[...] * (smooth * (1.0 + gate * (1.0 - smooth)))
        gate_flow = gate_flow.astype(low)
        up_flow = (flow * (gate * smooth)).astype(low)
        gate_out[...] = gate_flow
        up_out[...] = up_flow
        total[...] += dot(gate_flow, gate_matrix[...], nt) + dot(up_flow, up_matrix[...], nt)

        @pl.when(step == steps - 1)
        def _():
            for i in range(count):
                outs[i][...] = total[i * tokens : (i + 1) * tokens].astype(outs[i].dtype)

    columns = pl.BlockSpec((count * tokens, tile), lambda i: (0, i))
    outs = kernel_call(
        body,
        (steps,),
        [whole((tokens, features))] * count + [columns] * 2 + list(feed_specs(features, hidden)),
        [whole((tokens, features))] * count + [columns] * 2,
        [
            shaped((tokens, features), jnp.float32 if own and i == 0 else low)
            for i in range(count)
        ]
        + [shaped((count * tokens, hidden), low)] * 2,
        scratch=[
            pltpu.VMEM((count * tokens, features), low),
            pltpu.VMEM((count * tokens, features), jnp.float32),
        ],
    )(*blocks, gates, ups, up_matrix, up_matrix, down)
    return outs[:count], outs[count:]


def feed_grads(normed, gate_flows, up_flows):
    count, groups = len(normed), len(gate_flows)
    tokens, features = normed[0].shape
    hidden = gate_flows[0].shape[1]
    sizes = [flow.shape[0] for flow in gate_flows]
    starts = [sum(sizes[:i]) for i in range(groups)]
    tile = hidden_tile(hidden)
    steps = hidden // tile

    def body(*refs):
        flows = refs[count : count + 2 * groups]
        out, rows, columns = refs[count + 2 * groups :]
        step = pl.program_id(0)

        @pl.when(step == 0)
        def _():
            for i in range(count):
                rows[i * tokens : (i + 1) * tokens] = refs[i][...]

        for half in range(2):

            @pl.when(lax.div(step, steps) == half)
            def _():
                for i in range(groups):
                    at = slice(starts[i], starts[i] + sizes[i])
                    columns[at] = flows[half * groups + i][...]

        out[...] = dot(rows[...], columns[...], tn).astype(low)

    gate_specs = [
        pl.BlockSpec((size, tile), lambda i: (0, jnp.minimum(i, steps - 1))) for size in sizes
    ]
    up_specs = [
        pl.BlockSpec((size, tile), lambda i: (0, jnp.maximum(i - steps, 0))) for size in sizes
    ]
    return kernel_call(
        body,
        (2 * steps,),
        [whole((tokens, features))] * count + gate_specs + up_specs,
        pl.BlockSpec((features, tile), lambda i: (0, i)),
        shaped((features, 2 * hidden), low),
        scratch=[
            pltpu.VMEM((count * tokens, features), low),
            pltpu.VMEM((count * tokens, tile), low),
        ],
        cost=(12 * count * tokens * features * hidden, 24 * features * hidden),
    )(*normed, *gate_flows, *up_flows)


def down_grads(hiddens, flows):
    count, groups = len(flows), len(hiddens)
    tokens, features = flows[0].shape
    hidden = hiddens[0].shape[1]
    sizes = [values.shape[0] for values in hiddens]
    starts = [sum(sizes[:i]) for i in range(groups)]
    tile = hidden_tile(hidden)

    def body(*refs):
        hiddens = refs[count : count + groups]
        out, rows, columns = refs[count + groups :]

        @pl.when(pl.program_id(0) == 0)
        def _():
            for i in range(count):
                rows[i * tokens : (i + 1) * tokens] = refs[i][...]

        for i in range(groups):
            columns[starts[i] : starts[i] + sizes[i]] = hiddens[i][...]
        out[...] = dot(columns[...], rows[...], tn).astype(low)

    return kernel_call(
        body,
        (hidden // tile,),
        [whole((tokens, features))] * count
        + [pl.BlockSpec((size, tile), lambda i: (0, i)) for size in sizes],
        pl.BlockSpec((tile, features), lambda i: (i, 0)),
        shaped((hidden, features), low),
        scratch=[
            pltpu.VMEM((count * tokens, features), low),
            pltpu.VMEM((count * tokens, tile), low),
        ],
        cost=(6 * count * tokens * features * hidden, 12 * features * hidden),
    )(*flows, *hiddens)


def join_blocks(blocks):
    rings = lax.axis_size("fsdp")
    blocks = blocks.reshape(rings, -1, blocks.shape[-1])

    def body(place, blocks, *outs):
        for j in range(rings):
            outs[j][...] = blocks[lax.bitwise_xor(place[0], jnp.int32(j))]

    return plain_call(body, [shaped(blocks.shape[1:], blocks.dtype)] * rings, scalars=1)(
        place_of("fsdp"), blocks
    )


def groups_of(blocks):
    return [blocks[:2]] + [[block] for block in blocks[2:]]


def return_sums(sums):
    return [sums[0]] + [fsdp_swap(sums[j], j) for j in range(1, len(sums))]


def adam_update(weight, first, second, gradient, rate, decay):
    first_new = beta_one * first + (1.0 - beta_one) * gradient
    second_new = beta_two * second + (1.0 - beta_two) * gradient * gradient
    first_hat = first_new / (1.0 - beta_one**STEP)
    second_hat = second_new / (1.0 - beta_two**STEP)
    weight_new = weight - rate * (first_hat / (jnp.sqrt(second_hat) + eps_adam) + decay * weight)
    return (first_new, second_new, weight_new)


def local(
    inputs,
    cotangent,
    mix_weight,
    mix_first,
    mix_second,
    feed_weight,
    feed_first,
    feed_second,
    down_weight,
    down_first,
    down_second,
    gain_weight,
    gain_first,
    gain_second,
    tap_weight,
    tap_first,
    tap_second,
):
    sequences, length, features = inputs.shape
    seqs, rings = lax.axis_size("seq"), lax.axis_size("fsdp")
    rows = mix_weight.shape[1]
    chunk = features // seqs
    wide = -(-chunk // 128) * 128
    cotangent = cotangent.reshape(-1, features)
    Order.mark = jnp.zeros(mark_shape.shape, mark_shape.dtype)

    mixes, feeds = [None] * LAYERS, [None] * LAYERS
    vector_blocks = vectors_start(gain_weight, tap_weight)
    feed_swap = swap_feed(pack_feed(feed_weight, 0))
    later_feed = swap_feed(pack_feed(feed_weight, 1))
    mix_packed = pack_mix(mix_weight, 0, vector_blocks[1:])
    mix_swap = swap_mix(mix_packed)
    down_rows = gather_rows(pack_down(down_weight, 0))
    both, vector_blocks = vectors_middle(vector_blocks, later_feed[1:])
    mix_pieces = gather_fsdp(join_mix(mix_swap, mix_packed))
    feeds[0] = (gather_rows(assemble_feed(feed_swap)), down_rows)
    later_packed = pack_mix(mix_weight, 1)
    later_swap = swap_mix(later_packed)
    vector_blocks = stack_pairs(vector_blocks)
    later_piece = join_mix(later_swap, later_packed, mix_pieces[1:2])
    later_mix = lax.all_gather(
        later_piece.reshape(-1, later_piece.shape[-1]), "fsdp", axis=0, tiled=True
    ).reshape((rings,) + later_piece.shape)
    gain_rows, tap_rows = vectors_end(both, vector_blocks)
    stream, normed = first_norm(inputs.reshape(-1, features), gain_rows[0, 0], ())
    blocks = send_seq(normed)
    later_feed = assemble_feed(later_feed)
    blocks = stack_pairs(blocks, mix_pieces[2:])
    mixes[0] = assemble_mix(mix_pieces, wide)

    kept = []
    for layer in range(LAYERS):
        last = layer + 1 == LAYERS
        gathered = blocks
        projected, even, odd = mixer_forward(blocks, *mixes[layer], tap_rows[layer])
        odd = seq_swap(odd, 1)
        (sums,) = pair_sum(even, odd)
        middle, normed_two, *later = finish(
            stream,
            sums,
            gain_rows[layer, 1],
            feeds[layer] if last else (),
            () if last else (later_feed, pack_down(down_weight, 1)),
        )
        two_blocks = gather_fsdp(normed_two)
        if not last:
            feeds[1] = tuple(gather_rows(part) for part in later)
        sums, values = [], []
        for number, group in enumerate(groups_of(two_blocks)):
            outs, saved = feed_forward(group, *feeds[layer], number == 0)
            sums += outs
            values.append(saved)
            if number == 0 and last:
                flow_low = join_blocks(flow_low)
        kept.append((stream, middle, gathered, projected, two_blocks, values))
        sums = return_sums(sums)
        if not last:
            stream, normed, flow_low = finish(
                middle, sums, gain_rows[layer + 1, 0], (), [cotangent]
            )
            flow_low = lax.all_gather(flow_low, "fsdp", axis=0, tiled=True)
            blocks = stack_pairs(send_seq(normed))
            mixes[1] = assemble_mix([later_mix], wide)

    states = (
        (mix_weight, mix_first, mix_second),
        (feed_weight, feed_first, feed_second),
        (down_weight, down_first, down_second),
    )
    new = [None] * 3
    gain_grads, tap_grads = [None] * LAYERS, [None] * LAYERS
    flow = cotangent
    for layer in reversed(range(LAYERS)):
        last = layer + 1 == LAYERS
        stream, middle, gathered, projected, two_blocks, values = kept[layer]
        back_sums, gate_flows, up_flows = [], [], []
        for number, group in enumerate(groups_of(flow_low)):
            gates, ups, _ = values[number]
            outs, (gate_flow, up_flow) = feed_backward(
                group, gates, ups, *feeds[layer], number == 0
            )
            back_sums += outs
            gate_flows.append(gate_flow)
            up_flows.append(up_flow)
        if last:
            outputs = finish(middle, sums, None).reshape(inputs.shape)
        back_sums = return_sums(back_sums)
        down_part = down_grads([value[2] for value in values], flow_low)
        middle_flow, middle_low, gain_two, *later_mix = finish_back(
            flow, back_sums, middle, gain_rows[layer, 1], [down_part] if last else [later_mix]
        )
        if last:
            (down_part,) = later_mix
            down_part = [scatter_rows(down_part)]
        else:
            later_mix = lax.psum_scatter(
                later_mix[0].reshape(-1, later_mix[0].shape[-1]),
                "fsdp",
                scatter_dimension=0,
                tiled=True,
            ).reshape(later_mix[0].shape[1:])
        blocks = send_seq(middle_low)
        feed_part = feed_grads(two_blocks, gate_flows, up_flows)
        if not last:
            later_feed = split_feed(later_feed, rows)
        even, odd, feed_part = stack_pairs(blocks, (), [feed_part])
        feed_part = scatter_rows(feed_part)
        blocks = even, odd
        even, odd, flows, mixed, tap_grads[layer] = mixer_backward(
            blocks, projected, *mixes[layer], tap_rows[layer]
        )
        (sums,) = pair_sum(even, seq_swap(odd, 1))
        mix_part = mixer_grads(gathered, flows, mixed, blocks, rows, not last)
        flow, low_flow, gain_one, *mix_part = finish_back(
            middle_flow,
            sums,
            stream,
            gain_rows[layer, 0],
            mix_part,
            () if last else later_feed[1:],
        )
        if not last:
            mix_part = return_sums(mix_part)
        gain_grads[layer] = jnp.concatenate([gain_one, gain_two])
        if last:
            flow_low = gather_fsdp(low_flow)
            (later_mix,) = mix_part
            later_feed, later_down = feed_part, down_part
    new[1] = feed_adam(later_feed, states[1], 1, new[1])
    gain_grad, tap_grad = vector_gradients(
        jnp.stack(gain_grads), jnp.stack(tap_grads), gain_weight.shape[-1]
    )
    new[2] = down_adam(later_down, states[2], 1, new[2], [gain_grad])
    even, odd = split_down(down_part, mix_part[1:])
    odd = seq_swap(odd, 1)
    mix_part = mix_reduce([mix_part, [later_mix]], ())
    (down_part,) = pair_sum(even, odd)
    feed_part = split_feed(feed_part, rows)
    new[2] = down_adam(down_part, states[2], 0, new[2])
    new[0] = mix_adam(mix_part, states[0])
    new[1] = feed_adam(feed_part, states[1], 0, new[1])
    input_grad = flow.reshape(sequences, length, features)
    gain_new = adam_update(gain_weight, gain_first, gain_second, gain_grad, rate_vector, 0.0)
    tap_new = adam_update(tap_weight, tap_first, tap_second, tap_grad, rate_vector, 0.0)
    matrices = [(part[1], part[2], part[0]) for part in new]
    return (outputs, input_grad, *sum(matrices, ()), *gain_new, *tap_new)


def solution(mesh):
    tokens = P("fsdp", "seq", None)
    rows = P(None, ("seq", "fsdp"), None)
    last = P(None, None, ("seq", "fsdp"))
    return jax.shard_map(
        local,
        mesh=mesh,
        in_specs=(tokens,) * 2 + (rows,) * 9 + (last,) * 6,
        out_specs=(tokens,) * 2 + (rows,) * 9 + (last,) * 6,
        check_vma=False,
    )
```

```python
import math

import jax
import jax.numpy as jnp
from jax import lax
from jax.experimental import pallas as pl
from jax.experimental.pallas import tpu as pltpu
from jax.sharding import PartitionSpec as P

LAYERS = 2
STEP = 10

eps_norm = 1e-05
eps_adam = 1e-08
beta_one = 0.9
beta_two = 0.95
rate_matrix = 0.05
rate_vector = 0.6
decay_matrix = 0.1

low = jnp.bfloat16


def dot(left, right, sides=((1,), (0,))):
    return lax.dot_general(left, right, (sides, ((), ())), preferred_element_type=jnp.float32)


nt = ((1,), (1,))
tn = ((0,), (0,))


def seq_order():
    count = lax.axis_size("seq")
    return list(range(0, count, 2)) + list(range(1, count, 2))


def seq_swap(array, by):
    count = lax.axis_size("seq")
    return lax.ppermute(array, "seq", [(i, i ^ by) for i in range(count)])


def send_seq(array):
    return [array] + [seq_swap(array, by) for by in range(2, lax.axis_size("seq"), 2)]


def fsdp_swap(array, by):
    count = lax.axis_size("fsdp")
    return lax.ppermute(array, "fsdp", [(i, i ^ by) for i in range(count)])


def gather_fsdp(array):
    count = lax.axis_size("fsdp")
    return [array] + [fsdp_swap(array, by) for by in range(1, count)]


def small_scatter_seq(parts):
    half = parts.shape[0] // 2
    total = parts[:half] + seq_swap(parts[half:], 1)
    for i in range(1, half):
        total = total.at[0].add(seq_swap(total[i], 2 * i))
    return total[0]


def small_scatter_fsdp(parts):
    total = parts[0]
    for by in range(1, parts.shape[0]):
        total = total + fsdp_swap(parts[by], by)
    return total


def stack_pairs(blocks, earlier=(), carried=()):
    def body(*refs):
        for i in range(len(blocks)):
            refs[-1][i] = refs[i][...]

    shape = (len(blocks),) + blocks[0].shape
    even, *rest = plain_call(
        body, [shaped(shape, blocks[0].dtype)], earlier=earlier, carried=carried
    )(*blocks)
    return even, seq_swap(even, 1), *rest


def pad_last(array, width):
    return jnp.pad(array, [(0, 0)] * (array.ndim - 1) + [(0, width - array.shape[-1])])


def place_of(axis):
    return lax.axis_index(axis).astype(jnp.int32).reshape(1)


scalar = pl.BlockSpec(memory_space=pltpu.SMEM)
held = pl.BlockSpec(memory_space=pltpu.VMEM)


def shaped(shape, kind=jnp.float32):
    return jax.ShapeDtypeStruct(shape, kind)


class Order:
    mark = None


mark_shape = jax.ShapeDtypeStruct((8, 128), jnp.float32)
anywhere = pl.BlockSpec(memory_space=pl.ANY)


def bytes_of(shape, kind):
    return math.prod(shape) * jnp.dtype(kind).itemsize


def vmem_of(operands, in_specs, out_shape, out_specs, scratch, grid):
    total = 0
    for array, spec in [*zip(operands, in_specs), *zip(out_shape, out_specs)]:
        if spec is anywhere or spec is scalar:
            continue
        if grid:
            total += 2 * bytes_of(spec.block_shape, array.dtype)
        else:
            total += bytes_of(array.shape, array.dtype)
    for array in scratch:
        total += bytes_of(array.shape, array.dtype)
    return total + total // 2 + 4 * 1024 * 1024


def ordered_call(body, operands, in_specs, out_specs, out_shape, aliases, scratch, grid, cost):
    given, made = len(operands), len(out_shape)

    def marked(*refs):
        body(*refs[:given], *refs[given + 1 : given + 1 + made], *refs[given + 2 + made :])

    outs = pl.pallas_call(
        marked,
        in_specs=list(in_specs) + [anywhere],
        out_specs=list(out_specs) + [anywhere],
        out_shape=list(out_shape) + [mark_shape],
        scratch_shapes=list(scratch),
        input_output_aliases=aliases,
        compiler_params=pltpu.CompilerParams(
            vmem_limit_bytes=56 << 20
            if cost[0] or aliases and not grid
            else min(vmem_of(operands, in_specs, out_shape, out_specs, scratch, grid), 60 << 20)
        ),
        cost_estimate=pl.CostEstimate(
            flops=cost[0], bytes_accessed=cost[1], transcendentals=0
        ),
        **grid,
    )(*operands, Order.mark)
    Order.mark = outs[-1]
    return outs[:-1]


def kernel_call(
    body, grid, in_specs, out_specs, out_shape, aliases=None, scratch=(), cost=(0, 0)
):
    single = not isinstance(out_shape, list)

    def run(*operands):
        outs = ordered_call(
            body,
            operands,
            in_specs,
            [out_specs] if single else out_specs,
            [out_shape] if single else out_shape,
            aliases or {},
            scratch,
            dict(grid=grid),
            cost,
        )
        return outs[0] if single else outs

    return run


def plain_call(
    body, out_shape, scalars=0, scratch=(), earlier=(), carried=(), cost=(0, 0)
):
    def run(*operands):
        given, made, more = len(operands), len(out_shape), len(earlier) + len(carried)

        def rest(*refs):
            outs = refs[given + more :]
            body(*refs[:given], *outs[:made], *outs[made + len(carried) :])

        first = given + len(earlier)
        return ordered_call(
            rest,
            (*operands, *earlier, *carried),
            [scalar] * scalars + [held] * (given - scalars) + [anywhere] * more,
            [held] * made + [anywhere] * len(carried),
            [*out_shape, *(jax.ShapeDtypeStruct(x.shape, x.dtype) for x in carried)],
            {first + i: made + i for i in range(len(carried))},
            scratch,
            {},
            cost,
        )

    return run


def whole(shape):
    return pl.BlockSpec(shape, lambda i: (0,) * len(shape))


def pack_mix(mix_weight, layer, earlier=()):
    seqs = lax.axis_size("seq")
    rows, columns = mix_weight.shape[1:]
    features = columns // 4
    chunk = features // seqs

    def body(place, weight, *refs):
        out = refs[-1]
        for s in range(seqs):
            slot = lax.bitwise_xor(place[0], jnp.int32(s))
            for g in range(4):
                start = g * features + s * chunk
                piece = weight[0, :, start : start + chunk].astype(low)
                out[slot if g < 3 else s, :, g * chunk : (g + 1) * chunk] = piece

    shape = (seqs, rows, 4 * chunk)
    return kernel_call(
        body,
        (1,),
        [scalar, pl.BlockSpec((1, rows, columns), lambda i: (layer, 0, 0))]
        + [anywhere] * len(earlier),
        whole(shape),
        jax.ShapeDtypeStruct(shape, low),
    )(place_of("seq"), mix_weight, *earlier)


def assemble_mix(pieces, wide):
    rings = len(pieces)
    seqs, rows, width = pieces[0].shape
    chunk = width // 4
    features = seqs * chunk

    def body(place_seq, place_fsdp, *refs):
        inner_out, outer_out = refs[rings:]
        for j in range(rings):
            f = lax.bitwise_xor(place_fsdp[0], jnp.int32(j))
            for s in range(seqs):
                owner = lax.bitwise_xor(place_seq[0], jnp.int32(s))
                for g in range(3):
                    piece = refs[j][s, :, g * chunk : (g + 1) * chunk]
                    if wide > chunk:
                        gap = jnp.zeros((rows, wide - chunk), low)
                        piece = jnp.concatenate([piece, gap], axis=1)
                    inner_out[owner, f, :, g * wide : (g + 1) * wide] = piece
                outer_out[f, :, s * chunk : (s + 1) * chunk] = refs[j][s, :, 3 * chunk :]

    inner_shape = (seqs, rings, rows, 3 * wide)
    outer_shape = (rings, rows, features)
    inner, out = plain_call(
        body, [shaped(inner_shape, low), shaped(outer_shape, low)], scalars=2
    )(place_of("seq"), place_of("fsdp"), *pieces)
    return inner.reshape(features, 3 * wide), out.reshape(rings * rows, features)


def swap_mix(packed):
    seqs = lax.axis_size("seq")
    return [packed[:1]] + [seq_swap(packed[by : by + 1], by) for by in range(1, seqs)]


def join_mix(parts, packed, earlier=()):
    seqs = len(parts)

    def body(*refs):
        out = refs[-1]
        split = out.shape[-1] // 4 * 3
        for s in range(seqs):
            out[s, :, :split] = refs[s][0, :, :split]
            out[s, :, split:] = refs[seqs][s, :, split:]

    return plain_call(body, [shaped(packed.shape, low)], earlier=earlier)(*parts, packed)[0]


def tall_of(block):
    step = 128 // min(lax.axis_size("seq"), 128)
    return -(-block // step) * step


def pack_feed(feed_weight, layer):
    seqs, rings = lax.axis_size("seq"), lax.axis_size("fsdp")
    rows, columns = feed_weight.shape[1:]
    half = columns // 2
    block = half // (seqs * rings)
    tall = tall_of(block)

    def body(place, weight, out):
        for f in range(rings):
            slot = lax.bitwise_xor(place[0], jnp.int32(f))
            for g in range(2):
                for s in range(seqs):
                    start = g * half + (s * rings + f) * block
                    piece = weight[0, :, start : start + block].astype(low)
                    if tall > block:
                        piece = jnp.concatenate(
                            [piece, jnp.zeros((rows, tall - block), low)], axis=1
                        )
                    to = (g * seqs + s) * tall
                    out[slot, :, to : to + tall] = piece

    shape = (rings, rows, 2 * seqs * tall)
    return kernel_call(
        body,
        (1,),
        [scalar, pl.BlockSpec((1, rows, columns), lambda i: (layer, 0, 0))],
        whole(shape),
        jax.ShapeDtypeStruct(shape, low),
    )(place_of("fsdp"), feed_weight)


def assemble_feed(pieces):
    rings = len(pieces)

    def body(place, *refs):
        out = refs[rings]
        for j in range(rings):
            out[lax.bitwise_xor(place[0], jnp.int32(j))] = refs[j][0]

    shape = (rings,) + pieces[0].shape[1:]
    return kernel_call(
        body,
        (1,),
        [scalar] + [whole(piece.shape) for piece in pieces],
        whole(shape),
        jax.ShapeDtypeStruct(shape, low),
    )(place_of("fsdp"), *pieces)


def swap_feed(packed):
    rings = lax.axis_size("fsdp")
    return [packed[:1]] + [fsdp_swap(packed[by : by + 1], by) for by in range(1, rings)]


def gather_rows(part):
    return lax.all_gather(part.reshape(-1, part.shape[-1]), "seq", axis=0, tiled=True)


def pack_down(down_weight, layer):
    block = down_weight.shape[1]
    return jnp.pad(down_weight[layer].astype(low), ((0, tall_of(block) - block), (0, 0)))


def adam_kernel(load, scalars, grads, state, layer, previous, scratch=(), earlier=()):
    weight = state[0]
    rows, columns = weight.shape[1:]
    tile = 16 if rows % 16 == 0 else rows
    width = 768
    steps = rows // tile
    if layer is None:
        each = steps
        where = lambda i: (lax.div(i, each), lax.rem(i, each), 0)
        specs = [pl.BlockSpec((1, tile, grad.shape[-1]), where) for grad in grads]
        steps = LAYERS * each
    else:
        where = lambda i: (layer, i, 0)
        specs = [
            pl.BlockSpec(
                grad.shape if tile == rows else (tile, grad.shape[-1]), lambda i: (i, 0)
            )
            for grad in grads
        ]
    part = pl.BlockSpec((1, tile, columns), where)
    kept = (0 if previous is None else 3) + len(earlier)
    before = len(scalars) + len(grads)

    def body(*refs):
        weight, first, second = refs[before : before + 3]
        weight_out, first_out, second_out, total = refs[before + 3 + kept : before + 7 + kept]
        load(refs[: len(scalars)], refs[len(scalars) : before], refs[before + 7 + kept :], total)
        for start in range(0, columns, width):
            at = slice(start, start + width)
            gradient = total[:, at]
            old = weight[0, :, at]
            first_new = beta_one * first[0, :, at] + (1.0 - beta_one) * gradient
            second_new = beta_two * second[0, :, at] + (1.0 - beta_two) * gradient * gradient
            first_hat = first_new / (1.0 - beta_one**STEP)
            second_hat = second_new / (1.0 - beta_two**STEP)
            step = first_hat / (jnp.sqrt(second_hat) + eps_adam) + decay_matrix * old
            first_out[0, :, at] = first_new
            second_out[0, :, at] = second_new
            weight_out[0, :, at] = old - rate_matrix * step

    return kernel_call(
        body,
        (steps,),
        [scalar] * len(scalars)
        + specs
        + [part] * 3
        + [anywhere] * kept,
        [part] * 3,
        [shaped(weight.shape)] * 3,
        aliases={before + 3 + i: i for i in range(kept - len(earlier))},
        scratch=[pltpu.VMEM((tile, columns), jnp.float32), *(make(tile) for make in scratch)],
        cost=(0, 26 * rows * columns),
    )(*scalars, *grads, *state, *(previous or ()), *earlier)


def mix_reduce(layers):
    seqs, rows, width = layers[0][0].shape
    count, rings = len(layers), len(layers[0])
    chunk = width // 4

    def body(place, *refs):
        inner_out, outer_out = refs[count * rings :]
        for layer in range(count):
            parts = refs[layer * rings : (layer + 1) * rings]
            for s in range(seqs):
                total = parts[0][s].astype(jnp.float32)
                for part in parts[1:]:
                    total = total + part[s].astype(jnp.float32)
                inner_out[lax.bitwise_xor(place[0], jnp.int32(s)), layer] = total.astype(low)
                outer_out[layer, :, s * chunk : (s + 1) * chunk] = total[:, 3 * chunk :]

    inner, last = plain_call(
        body,
        [shaped((seqs, count, rows, width), low), shaped((count, rows, seqs * chunk))],
        scalars=1,
    )(place_of("seq"), *sum((list(pieces) for pieces in layers), []))
    return [inner[0]] + [seq_swap(inner[j], j) for j in range(1, seqs)] + [last]


def mix_adam(grads, state):
    seqs = lax.axis_size("seq")
    features = state[0].shape[2] // 4
    chunk = features // seqs

    def load(scalars, grads, scratch, total):
        for s in range(seqs):
            scratch[0][lax.bitwise_xor(scalars[0][0], jnp.int32(s))] = grads[s][0]
        for s in range(seqs):
            for g in range(3):
                start = g * features + s * chunk
                piece = scratch[0][s, :, g * chunk : (g + 1) * chunk]
                total[:, start : start + chunk] = piece.astype(jnp.float32)
        total[:, 3 * features :] = grads[seqs][0]

    return adam_kernel(
        load,
        [place_of("seq")],
        grads,
        state,
        None,
        None,
        [lambda tile: pltpu.VMEM((seqs, tile, 4 * chunk), low)],
    )


def scatter_rows(grad):
    return lax.psum_scatter(grad, "seq", scatter_dimension=0, tiled=True)


def split_feed(part, rows):
    rings = lax.axis_size("fsdp")
    part = part.reshape(rings, rows, -1)

    def body(place, part, *outs):
        for j in range(rings):
            outs[j][...] = part[lax.bitwise_xor(place[0], jnp.int32(j))]

    pieces = plain_call(body, [shaped(part.shape[1:], low)] * rings, scalars=1)(
        place_of("fsdp"), part
    )
    return return_sums(pieces)


def feed_adam(grads, state, layer, previous):
    seqs, rings = lax.axis_size("seq"), lax.axis_size("fsdp")
    half = state[0].shape[2] // 2
    block = half // (seqs * rings)
    tall = tall_of(block)

    def load(scalars, grads, scratch, total):
        for j in range(rings):
            scratch[0][lax.bitwise_xor(scalars[0][0], jnp.int32(j))] = grads[j][...]
        for f in range(rings):
            for g in range(2):
                for s in range(seqs):
                    start = g * half + (s * rings + f) * block
                    at = (g * seqs + s) * tall
                    piece = scratch[0][f, :, at : at + block]
                    total[:, start : start + block] = piece.astype(jnp.float32)

    return adam_kernel(
        load,
        [place_of("fsdp")],
        grads,
        state,
        layer,
        previous,
        [lambda tile: pltpu.VMEM((rings, tile, 2 * seqs * tall), low)],
    )


def down_adam(parts, state, layer, previous):
    def load(scalars, grads, scratch, total):
        sums = grads[0][...].astype(jnp.float32)
        for grad in grads[1:]:
            sums = sums + grad[...].astype(jnp.float32)
        total[...] = sums[: total.shape[0]]

    return adam_kernel(load, [], parts, state, layer, previous)


def split_down(part, earlier):
    seqs = lax.axis_size("seq")
    part = part.reshape(seqs, -1, part.shape[-1])

    def body(place, part, even, odd):
        for i in range(seqs):
            owner = lax.bitwise_xor(place[0], jnp.int32(i))
            (even, odd)[i % 2][i // 2] = part[owner]

    return plain_call(
        body,
        [shaped((seqs // 2,) + part.shape[1:], part.dtype)] * 2,
        scalars=1,
        earlier=earlier,
    )(place_of("seq"), part)


def place_blocks(blocks, owners, place, earlier=()):
    def body(place, *refs):
        if len(blocks[0].shape) == len(refs[-1].shape):
            refs = [ref.at[i] for ref in refs[:-1] for i in range(ref.shape[0])] + [refs[-1]]
        for block, owner in zip(refs, owners(place[0])):
            refs[-1][owner] = block[...]

    shape = blocks[0].shape
    if len(blocks) == 2:
        shape = (2 * shape[0],) + shape[1:]
    else:
        shape = (len(blocks),) + shape
    return plain_call(body, [shaped(shape, blocks[0].dtype)], scalars=1, earlier=earlier)(
        place, *blocks
    )[0]


def vectors_start(gain_weight, tap_weight):
    gains = gain_weight.reshape(2 * LAYERS, -1)
    taps = tap_weight.reshape(3 * LAYERS, -1)
    return gather_fsdp(jnp.concatenate([gains, taps], axis=0).astype(low))


def vectors_middle(blocks):
    rings = lax.axis_size("fsdp")
    both = place_blocks(
        blocks,
        lambda place: [lax.bitwise_xor(place, jnp.int32(j)) for j in range(rings)],
        place_of("fsdp"),
    )
    return both, send_seq(both)


def vectors_end(both, blocks):
    spread = place_blocks(
        blocks,
        lambda place: [lax.bitwise_xor(place, jnp.int32(i)) for i in seq_order()],
        place_of("seq"),
    )
    gains = jnp.transpose(spread[:, :, : 2 * LAYERS], (2, 0, 1, 3)).astype(jnp.float32)
    taps = jnp.transpose(both[:, 2 * LAYERS :], (1, 0, 2)).astype(jnp.float32)
    return gains.reshape(LAYERS, 2, 1, -1), taps.reshape(LAYERS, 3, -1)


def vector_gradients(gain_grads, tap_grads, short):
    seqs, rings = lax.axis_size("seq"), lax.axis_size("fsdp")
    place_seq, place_fsdp = lax.axis_index("seq"), lax.axis_index("fsdp")
    gains = gain_grads.reshape(2 * LAYERS, seqs, -1)
    owner = place_seq ^ jnp.array(seq_order())
    pick = (owner[:, None] == jnp.arange(seqs)[None, :]).astype(jnp.float32)
    gains = jnp.einsum("jo,koc->jkc", pick, gains, precision=lax.Precision.HIGHEST)
    gains = small_scatter_seq(gains)
    taps = tap_grads.reshape(3 * LAYERS, -1)[:, : rings * short]
    both = jnp.concatenate([gains, taps], axis=0).reshape(5 * LAYERS, rings, short)
    owner = place_fsdp ^ jnp.arange(rings)
    pick = (owner[:, None] == jnp.arange(rings)[None, :]).astype(jnp.float32)
    both = jnp.einsum("jo,koc->jkc", pick, both, precision=lax.Precision.HIGHEST)
    both = small_scatter_fsdp(both)
    return (
        both[: 2 * LAYERS].reshape(LAYERS, 2, short),
        both[2 * LAYERS :].reshape(LAYERS, 3, short),
    )


def unit_rows(values):
    row_scale = lax.rsqrt(jnp.mean(values * values, axis=-1, keepdims=True) + eps_norm)
    return values * row_scale, row_scale


def first_norm(inputs, gain, earlier):
    def body(inputs, gain, stream_out, normed_out):
        stream = inputs[...].astype(jnp.float32)
        stream_out[...] = stream
        normed_out[...] = (unit_rows(stream)[0] * gain[...]).astype(low)

    return plain_call(
        body, [shaped(inputs.shape), shaped(inputs.shape, low)], earlier=earlier
    )(inputs, gain)


def finish(base, sums, gain, earlier=(), carried=()):
    def body(*refs):
        total = refs[0][...]
        for part in refs[1 : 1 + len(sums)]:
            total = total + part[...].astype(jnp.float32)
        if gain is None:
            refs[-1][...] = total.astype(low)
        else:
            refs[-2][...] = total
            refs[-1][...] = (unit_rows(total)[0] * refs[1 + len(sums)][...]).astype(low)

    if gain is None:
        return plain_call(body, [shaped(base.shape, low)])(base, *sums)[0]
    return plain_call(
        body,
        [shaped(base.shape), shaped(base.shape, low)],
        earlier=earlier,
        carried=carried,
    )(base, *sums, gain)


def finish_back(flow, sums, stream, gain, carried=(), earlier=()):
    def body(flow, stream, gain, *refs):
        total = refs[0][...].astype(jnp.float32)
        for part in refs[1 : len(sums)]:
            total = total + part[...].astype(jnp.float32)
        unit, row_scale = unit_rows(stream[...])
        scaled = total * gain[...]
        inner_mean = jnp.mean(scaled * unit, axis=-1, keepdims=True)
        result = flow[...].astype(jnp.float32) + row_scale * (scaled - unit * inner_mean)
        refs[-3][...] = result
        refs[-2][...] = result.astype(low)
        refs[-1][...] = jnp.sum(total * unit, axis=0, keepdims=True)

    return plain_call(
        body,
        [shaped(flow.shape), shaped(flow.shape, low), shaped((1, flow.shape[1]))],
        carried=carried,
        earlier=earlier,
    )(flow, stream, gain, *sums)


def pair_sum(even, received, earlier=(), carried=()):
    half, tokens, features = even.shape

    def body(even, received, *outs):
        for i in range(half):
            total = even[i] + received[i].astype(jnp.float32)
            outs[i][...] = total.astype(outs[i].dtype)

    outs = plain_call(
        body,
        [shaped((tokens, features))] + [shaped((tokens, features), low)] * (half - 1),
        earlier=earlier,
        carried=carried,
    )(even, received)
    return [outs[0]] + [seq_swap(outs[i], 2 * i) for i in range(1, half)], *outs[half:]


def block_neighbour(place, i, count, step):
    order = list(range(0, count, 2)) + list(range(1, count, 2))
    owner = lax.bitwise_xor(place, jnp.int32(order[i])) + step
    inside = jnp.logical_and(owner >= 0, owner < count)
    number = lax.bitwise_xor(place, jnp.where(inside, owner, place))
    return lax.div(number, 2) + lax.rem(number, 2) * (count // 2), inside


def conv_forward(place, taps, gated, i, count):
    here = gated[i]
    tokens, chunk = here.shape
    at, inside = block_neighbour(place, i, count, -1)
    before = jnp.where(inside, gated[at, tokens - 8 :, :], 0.0)
    row = lax.broadcasted_iota(jnp.int32, (tokens, chunk), 0)
    last, second = before[7:8, :], before[6:7, :]
    one = jnp.where(row == 0, last, pltpu.roll(here, 1, 0))
    two = jnp.where(row == 0, second, jnp.where(row == 1, last, pltpu.roll(here, 2, 0)))
    return taps[0:1, :] * two + taps[1:2, :] * one + taps[2:3, :] * here, one, two


def mixer_forward(blocks, inner, outer, taps):
    half, tokens, features = blocks[0].shape
    count = 2 * half
    chunk = outer.shape[0]
    wide = inner.shape[1] // 3

    def body(place, even_in, odd_in, inner, outer, taps, *refs):
        projected, even, odd, gated, mixed = refs
        for k, rows in enumerate((even_in, odd_in)):
            rows = rows[...].reshape(half * tokens, features)
            for g in range(3):
                columns = slice(g * wide, (g + 1) * wide)
                part = dot(rows, inner[:, columns]).reshape(half, tokens, wide)
                projected[k * half : (k + 1) * half, :, columns] = part

        for i in range(count):
            product = projected[i, :, :wide] * projected[i, :, 2 * wide :]
            gated[i] = product[:, :chunk].astype(low).astype(jnp.float32)
        taps = taps[...]
        for i in range(count):
            conv_out = conv_forward(place[0], taps, gated, i, count)[0]
            mixed[i] = (projected[i, :, wide : wide + chunk] * conv_out).astype(low)
        rows = mixed[:half].reshape(half * tokens, chunk)
        even[...] = dot(rows, outer[...]).reshape(half, tokens, features)
        rows = mixed[half:].reshape(half * tokens, chunk)
        odd[...] = dot(rows, outer[...]).reshape(half, tokens, features).astype(low)

    return plain_call(
        body,
        [
            shaped((count, tokens, 3 * wide)),
            shaped((half, tokens, features)),
            shaped((half, tokens, features), low),
        ],
        scalars=1,
        scratch=[
            pltpu.VMEM((count, tokens, chunk), jnp.float32),
            pltpu.VMEM((count, tokens, chunk), low),
        ],
    )(place_of("seq"), *blocks, inner, outer, taps)


def mixer_backward(blocks, projected, inner, outer, taps):
    half, tokens, features = blocks[0].shape
    count = 2 * half
    chunk = outer.shape[0]
    wide = inner.shape[1] // 3

    def body(place, even_in, odd_in, projected, inner, outer, taps, *refs):
        even, odd, flows, mixed, tap_out, gated, flow = refs
        for i in range(count):
            product = projected[i, :, :wide] * projected[i, :, 2 * wide :]
            gated[i] = product[:, :chunk].astype(low).astype(jnp.float32)
        taps = taps[...]
        tap_sums = [jnp.zeros((1, chunk), jnp.float32)] * 3
        for k in range(2):
            rows = (even_in, odd_in)[k][...].reshape(half * tokens, features)
            back = dot(rows, outer[...], nt).reshape(half, tokens, chunk)
            for i in range(k * half, (k + 1) * half):
                conv_out, one, two = conv_forward(place[0], taps, gated, i, count)
                gate = projected[i, :, wide : wide + chunk]
                mixed[i] = (gate * conv_out).astype(low)
                mixed_flow = back[i - k * half]
                conv_flow = mixed_flow * gate
                flow[i] = conv_flow
                for j, shifted in enumerate((two, one, gated[i])):
                    term = jnp.sum(conv_flow * shifted, axis=0, keepdims=True)
                    tap_sums[j] = tap_sums[j] + term
                flows[i, :, wide : wide + chunk] = (mixed_flow * conv_out).astype(low)
        for j in range(3):
            tap_out[j : j + 1, :] = tap_sums[j]
        row = lax.broadcasted_iota(jnp.int32, (tokens, chunk), 0)
        for i in range(count):
            here = flow[i]
            at, inside = block_neighbour(place[0], i, count, 1)
            beyond = jnp.where(inside, flow[at, :8, :], 0.0)
            first, second = beyond[0:1, :], beyond[1:2, :]
            one = jnp.where(row == tokens - 1, first, pltpu.roll(here, tokens - 1, 0))
            two = jnp.where(
                row == tokens - 1,
                second,
                jnp.where(row == tokens - 2, first, pltpu.roll(here, tokens - 2, 0)),
            )
            gated_flow = taps[2:3, :] * here + taps[1:2, :] * one + taps[0:1, :] * two
            x_part = projected[i, :, 2 * wide : 2 * wide + chunk]
            b_part = projected[i, :, :chunk]
            flows[i, :, :chunk] = (gated_flow * x_part).astype(low)
            flows[i, :, 2 * wide : 2 * wide + chunk] = (gated_flow * b_part).astype(low)
            if wide > chunk:
                for g in range(3):
                    gap = jnp.zeros((tokens, wide - chunk), low)
                    flows[i, :, g * wide + chunk : (g + 1) * wide] = gap
        rows = flows[:half].reshape(half * tokens, 3 * wide)
        even[...] = dot(rows, inner[...], nt).reshape(half, tokens, features)
        rows = flows[half:].reshape(half * tokens, 3 * wide)
        odd[...] = dot(rows, inner[...], nt).reshape(half, tokens, features).astype(low)

    return plain_call(
        body,
        [
            shaped((half, tokens, features)),
            shaped((half, tokens, features), low),
            shaped((count, tokens, 3 * wide), low),
            shaped((count, tokens, chunk), low),
            shaped((3, chunk)),
        ],
        scalars=1,
        scratch=[pltpu.VMEM((count, tokens, chunk), jnp.float32)] * 2,
    )(place_of("seq"), *blocks, projected, inner, outer, taps)


def mixer_grads(normed, flows, mixed, lows, rows):
    seqs, rings = lax.axis_size("seq"), lax.axis_size("fsdp")
    features, width = normed[0].shape[-1], flows.shape[-1]
    half = normed[0].shape[0]
    wide = width // 3
    chunk = mixed.shape[-1]

    def body(place, normed_even, normed_odd, flows, mixed, low_even, low_odd, *refs):
        outs, inner, outer = refs[:rings], refs[rings], refs[rings + 1]
        long = lambda array: array.reshape(-1, array.shape[-1])
        for g in range(3):
            at = slice(g * wide, (g + 1) * wide)
            part = dot(long(normed_even[...]), long(flows[:half, :, at]), tn)
            part = part + dot(long(normed_odd[...]), long(flows[half:, :, at]), tn)
            part = part.astype(low)
            for i in range(seqs * rings):
                inner[i // rings, i % rings, :, at] = part[i * rows : (i + 1) * rows]
        part = dot(long(mixed[:half]), long(low_even[...]), tn)
        part = part + dot(long(mixed[half:]), long(low_odd[...]), tn)
        part = part.astype(low)
        for f in range(rings):
            outer[f] = part[f * rows : (f + 1) * rows]
        for j in range(rings):
            f = lax.bitwise_xor(place[0], jnp.int32(j))
            for s in range(seqs):
                for g in range(3):
                    piece = inner[s, f, :, g * wide : g * wide + chunk]
                    outs[j][s, :, g * chunk : (g + 1) * chunk] = piece
                outs[j][s, :, 3 * chunk :] = outer[f, :, s * chunk : (s + 1) * chunk]

    return plain_call(
        body,
        [shaped((seqs, rows, 4 * chunk), low)] * rings,
        scalars=1,
        scratch=[
            pltpu.VMEM((seqs, rings, rows, width), low),
            pltpu.VMEM((rings, rows, features), low),
        ],
        cost=(24 * half * normed[0].size, 8 * normed[0].size),
    )(place_of("fsdp"), *normed, flows, mixed, *lows)


def hidden_tile(hidden):
    return 256 if hidden % 256 == 0 else 128


def feed_specs(features, hidden):
    tile = hidden_tile(hidden)
    steps = hidden // tile
    return (
        pl.BlockSpec((features, tile), lambda i: (0, i)),
        pl.BlockSpec((features, tile), lambda i: (0, i + steps)),
        pl.BlockSpec((tile, features), lambda i: (i, 0)),
    )


def feed_forward(blocks, up_matrix, down, own):
    count = len(blocks)
    tokens, features = blocks[0].shape
    hidden = down.shape[0]
    tile = hidden_tile(hidden)
    steps = hidden // tile

    def body(*refs):
        gate_matrix, up_matrix, down = refs[count : count + 3]
        outs = refs[count + 3 : 2 * count + 3]
        gate_out, up_out, hidden_out, rows, total = refs[2 * count + 3 :]
        step = pl.program_id(0)

        @pl.when(step == 0)
        def _():
            for i in range(count):
                rows[i * tokens : (i + 1) * tokens] = refs[i][...]
            total[...] = jnp.zeros_like(total)

        gate = dot(rows[...], gate_matrix[...])
        up = dot(rows[...], up_matrix[...])
        gate_out[...] = gate
        up_out[...] = up
        value = (gate * jax.nn.sigmoid(gate) * up).astype(low)
        hidden_out[...] = value
        total[...] += dot(value, down[...])

        @pl.when(step == steps - 1)
        def _():
            for i in range(count):
                outs[i][...] = total[i * tokens : (i + 1) * tokens].astype(outs[i].dtype)

    columns = pl.BlockSpec((count * tokens, tile), lambda i: (0, i))
    outs = kernel_call(
        body,
        (steps,),
        [whole((tokens, features))] * count + list(feed_specs(features, hidden)),
        [whole((tokens, features))] * count + [columns] * 3,
        [
            shaped((tokens, features), jnp.float32 if own and i == 0 else low)
            for i in range(count)
        ]
        + [shaped((count * tokens, hidden), kind) for kind in (jnp.float32, jnp.float32, low)],
        scratch=[
            pltpu.VMEM((count * tokens, features), low),
            pltpu.VMEM((count * tokens, features), jnp.float32),
        ],
    )(*blocks, up_matrix, up_matrix, down)
    return outs[:count], outs[count:]


def feed_backward(blocks, gates, ups, up_matrix, down, own):
    count = len(blocks)
    tokens, features = blocks[0].shape
    hidden = down.shape[0]
    tile = hidden_tile(hidden)
    steps = hidden // tile

    def body(*refs):
        gate_part, up_part, gate_matrix, up_matrix, down = refs[count : count + 5]
        outs = refs[count + 5 : 2 * count + 5]
        gate_out, up_out, rows, total = refs[2 * count + 5 :]
        step = pl.program_id(0)

        @pl.when(step == 0)
        def _():
            for i in range(count):
                rows[i * tokens : (i + 1) * tokens] = refs[i][...]
            total[...] = jnp.zeros_like(total)

        flow = dot(rows[...], down[...], nt)
        gate = gate_part[...]
        smooth = jax.nn.sigmoid(gate)
        gate_flow = flow * up_part[...] * (smooth * (1.0 + gate * (1.0 - smooth)))
        gate_flow = gate_flow.astype(low)
        up_flow = (flow * (gate * smooth)).astype(low)
        gate_out[...] = gate_flow
        up_out[...] = up_flow
        total[...] += dot(gate_flow, gate_matrix[...], nt) + dot(up_flow, up_matrix[...], nt)

        @pl.when(step == steps - 1)
        def _():
            for i in range(count):
                outs[i][...] = total[i * tokens : (i + 1) * tokens].astype(outs[i].dtype)

    columns = pl.BlockSpec((count * tokens, tile), lambda i: (0, i))
    outs = kernel_call(
        body,
        (steps,),
        [whole((tokens, features))] * count + [columns] * 2 + list(feed_specs(features, hidden)),
        [whole((tokens, features))] * count + [columns] * 2,
        [
            shaped((tokens, features), jnp.float32 if own and i == 0 else low)
            for i in range(count)
        ]
        + [shaped((count * tokens, hidden), low)] * 2,
        scratch=[
            pltpu.VMEM((count * tokens, features), low),
            pltpu.VMEM((count * tokens, features), jnp.float32),
        ],
    )(*blocks, gates, ups, up_matrix, up_matrix, down)
    return outs[:count], outs[count:]


def feed_grads(normed, gate_flows, up_flows):
    count, groups = len(normed), len(gate_flows)
    tokens, features = normed[0].shape
    hidden = gate_flows[0].shape[1]
    sizes = [flow.shape[0] for flow in gate_flows]
    starts = [sum(sizes[:i]) for i in range(groups)]
    tile = hidden_tile(hidden)
    steps = hidden // tile

    def body(*refs):
        flows = refs[count : count + 2 * groups]
        out, rows, columns = refs[count + 2 * groups :]
        step = pl.program_id(0)

        @pl.when(step == 0)
        def _():
            for i in range(count):
                rows[i * tokens : (i + 1) * tokens] = refs[i][...]

        for half in range(2):

            @pl.when(lax.div(step, steps) == half)
            def _():
                for i in range(groups):
                    at = slice(starts[i], starts[i] + sizes[i])
                    columns[at] = flows[half * groups + i][...]

        out[...] = dot(rows[...], columns[...], tn).astype(low)

    gate_specs = [
        pl.BlockSpec((size, tile), lambda i: (0, jnp.minimum(i, steps - 1))) for size in sizes
    ]
    up_specs = [
        pl.BlockSpec((size, tile), lambda i: (0, jnp.maximum(i - steps, 0))) for size in sizes
    ]
    return kernel_call(
        body,
        (2 * steps,),
        [whole((tokens, features))] * count + gate_specs + up_specs,
        pl.BlockSpec((features, tile), lambda i: (0, i)),
        shaped((features, 2 * hidden), low),
        scratch=[
            pltpu.VMEM((count * tokens, features), low),
            pltpu.VMEM((count * tokens, tile), low),
        ],
        cost=(12 * count * tokens * features * hidden, 24 * features * hidden),
    )(*normed, *gate_flows, *up_flows)


def down_grads(hiddens, flows):
    count, groups = len(flows), len(hiddens)
    tokens, features = flows[0].shape
    hidden = hiddens[0].shape[1]
    sizes = [values.shape[0] for values in hiddens]
    starts = [sum(sizes[:i]) for i in range(groups)]
    tile = hidden_tile(hidden)

    def body(*refs):
        hiddens = refs[count : count + groups]
        out, rows, columns = refs[count + groups :]

        @pl.when(pl.program_id(0) == 0)
        def _():
            for i in range(count):
                rows[i * tokens : (i + 1) * tokens] = refs[i][...]

        for i in range(groups):
            columns[starts[i] : starts[i] + sizes[i]] = hiddens[i][...]
        out[...] = dot(columns[...], rows[...], tn).astype(low)

    return kernel_call(
        body,
        (hidden // tile,),
        [whole((tokens, features))] * count
        + [pl.BlockSpec((size, tile), lambda i: (0, i)) for size in sizes],
        pl.BlockSpec((tile, features), lambda i: (i, 0)),
        shaped((hidden, features), low),
        scratch=[
            pltpu.VMEM((count * tokens, features), low),
            pltpu.VMEM((count * tokens, tile), low),
        ],
        cost=(6 * count * tokens * features * hidden, 12 * features * hidden),
    )(*flows, *hiddens)


def join_blocks(blocks):
    def body(*refs):
        for i in range(len(blocks)):
            refs[len(blocks) + i][...] = refs[i][...]

    return plain_call(body, [shaped(block.shape, block.dtype) for block in blocks])(*blocks)


def groups_of(blocks):
    return [blocks[:2]] + [[block] for block in blocks[2:]]


def return_sums(sums):
    return [sums[0]] + [fsdp_swap(sums[j], j) for j in range(1, len(sums))]


def adam_update(weight, first, second, gradient, rate, decay):
    first_new = beta_one * first + (1.0 - beta_one) * gradient
    second_new = beta_two * second + (1.0 - beta_two) * gradient * gradient
    first_hat = first_new / (1.0 - beta_one**STEP)
    second_hat = second_new / (1.0 - beta_two**STEP)
    weight_new = weight - rate * (first_hat / (jnp.sqrt(second_hat) + eps_adam) + decay * weight)
    return (first_new, second_new, weight_new)


def local(
    inputs,
    cotangent,
    mix_weight,
    mix_first,
    mix_second,
    feed_weight,
    feed_first,
    feed_second,
    down_weight,
    down_first,
    down_second,
    gain_weight,
    gain_first,
    gain_second,
    tap_weight,
    tap_first,
    tap_second,
):
    sequences, length, features = inputs.shape
    seqs, rings = lax.axis_size("seq"), lax.axis_size("fsdp")
    rows = mix_weight.shape[1]
    chunk = features // seqs
    wide = -(-chunk // 128) * 128
    cotangent = cotangent.reshape(-1, features)
    Order.mark = jnp.zeros(mark_shape.shape, mark_shape.dtype)

    mixes, feeds = [None] * LAYERS, [None] * LAYERS
    vector_blocks = vectors_start(gain_weight, tap_weight)
    feed_swap = swap_feed(pack_feed(feed_weight, 0))
    mix_packed = pack_mix(mix_weight, 0, vector_blocks[1:])
    mix_swap = swap_mix(mix_packed)
    down_rows = gather_rows(pack_down(down_weight, 0))
    both, vector_blocks = vectors_middle(vector_blocks)
    mix_pieces = gather_fsdp(join_mix(mix_swap, mix_packed))
    feed_part = assemble_feed(feed_swap)
    later_packed = pack_mix(mix_weight, 1)
    later_swap = swap_mix(later_packed)
    vector_blocks = stack_pairs(vector_blocks)
    later_piece = join_mix(later_swap, later_packed, mix_pieces[1:2])
    gain_rows, tap_rows = vectors_end(both, vector_blocks)
    stream, normed = first_norm(inputs.reshape(-1, features), gain_rows[0, 0], ())
    blocks = send_seq(normed)
    later_feed = pack_feed(feed_weight, 1)
    *blocks, feed_part = stack_pairs(blocks, mix_pieces[2:], [feed_part])
    feeds[0] = (gather_rows(feed_part), down_rows)
    mixes[0] = assemble_mix(mix_pieces, wide)
    later_mix = [None, None, fsdp_swap(later_piece, 2)] if rings > 2 else [None, None]

    kept = []
    for layer in range(LAYERS):
        last = layer + 1 == LAYERS
        gathered = blocks
        projected, even, odd = mixer_forward(blocks, *mixes[layer], tap_rows[layer])
        odd = seq_swap(odd, 1)
        if last:
            sums, flow_low = pair_sum(even, odd, (), [cotangent])
            flow_low = gather_fsdp(flow_low)
            middle, normed_two = finish(stream, sums, gain_rows[layer, 1])
        else:
            (sums,) = pair_sum(even, odd)
            middle, normed_two, later_piece, down_packed, later_feed = finish(
                stream,
                sums,
                gain_rows[layer, 1],
                later_mix[2:],
                (later_piece, pack_down(down_weight, 1), later_feed),
            )
        two_blocks = gather_fsdp(normed_two)
        if not last:
            later_mix[0] = later_piece
            later_mix[1] = fsdp_swap(later_piece, 1)
            later_down = gather_rows(down_packed)
            later_feed = swap_feed(later_feed)
        sums, values = [], []
        for number, group in enumerate(groups_of(two_blocks)):
            outs, saved = feed_forward(group, *feeds[layer], number == 0)
            sums += outs
            values.append(saved)
        if last:
            flow_low = join_blocks(flow_low)
        kept.append((stream, middle, gathered, projected, two_blocks, values))
        sums = return_sums(sums)
        if not last:
            stream, normed, later_piece, later_feed = finish(
                middle,
                sums,
                gain_rows[layer + 1, 0],
                later_mix[1:2],
                [later_piece, assemble_feed(later_feed)],
            )
            feeds[1] = gather_rows(later_feed), later_down
            blocks = send_seq(normed)
            later_mix += [fsdp_swap(later_piece, by) for by in range(3, rings)]
            blocks = stack_pairs(blocks)
            mixes[1] = assemble_mix(later_mix, wide)

    states = (
        (mix_weight, mix_first, mix_second),
        (feed_weight, feed_first, feed_second),
        (down_weight, down_first, down_second),
    )
    new = [None] * 3
    gain_grads, tap_grads = [None] * LAYERS, [None] * LAYERS
    flow = cotangent
    later_mix = ()
    for layer in reversed(range(LAYERS)):
        last = layer + 1 == LAYERS
        stream, middle, gathered, projected, two_blocks, values = kept[layer]
        back_sums, gate_flows, up_flows = [], [], []
        for number, group in enumerate(groups_of(flow_low)):
            gates, ups, _ = values[number]
            outs, (gate_flow, up_flow) = feed_backward(
                group, gates, ups, *feeds[layer], number == 0
            )
            back_sums += outs
            gate_flows.append(gate_flow)
            up_flows.append(up_flow)
        if last:
            outputs = finish(middle, sums, None).reshape(inputs.shape)
        back_sums = return_sums(back_sums)
        down_part = down_grads([value[2] for value in values], flow_low)
        middle_flow, middle_low, gain_two, down_part, *later_mix = finish_back(
            flow, back_sums, middle, gain_rows[layer, 1], [down_part, *later_mix]
        )
        later_mix = return_sums(later_mix) if later_mix else later_mix
        if last:
            down_part = [scatter_rows(down_part)]
        blocks = send_seq(middle_low)
        feed_part = feed_grads(two_blocks, gate_flows, up_flows)
        if not last:
            later_feed = split_feed(later_feed, rows)
        even, odd, feed_part = stack_pairs(
            blocks, () if last else later_mix[2:3], [feed_part]
        )
        feed_part = scatter_rows(feed_part)
        blocks = even, odd
        even, odd, flows, mixed, tap_grads[layer] = mixer_backward(
            blocks, projected, *mixes[layer], tap_rows[layer]
        )
        (sums,) = pair_sum(even, seq_swap(odd, 1), () if last else later_feed[1:])
        mix_part = mixer_grads(gathered, flows, mixed, blocks, rows)
        flow, low_flow, gain_one, *mix_part = finish_back(
            middle_flow,
            sums,
            stream,
            gain_rows[layer, 0],
            mix_part,
            () if last else (later_mix[1], *later_mix[3:]),
        )
        if not last:
            mix_part = return_sums(mix_part)
        gain_grads[layer] = jnp.concatenate([gain_one, gain_two])
        if last:
            flow_low = gather_fsdp(low_flow)
            later_mix, later_feed, later_down = mix_part, feed_part, down_part
    new[1] = feed_adam(later_feed, states[1], 1, new[1])
    even, odd = split_down(down_part, mix_part[1:])
    odd = seq_swap(odd, 1)
    new[2] = down_adam(later_down, states[2], 1, new[2])
    (down_part,) = pair_sum(even, odd)
    gain_grad, tap_grad = vector_gradients(
        jnp.stack(gain_grads), jnp.stack(tap_grads), gain_weight.shape[-1]
    )
    mix_part = mix_reduce([mix_part, later_mix])
    feed_part = split_feed(feed_part, rows)
    new[2] = down_adam(down_part, states[2], 0, new[2])
    new[0] = mix_adam(mix_part, states[0])
    new[1] = feed_adam(feed_part, states[1], 0, new[1])
    input_grad = flow.reshape(sequences, length, features)
    gain_new = adam_update(gain_weight, gain_first, gain_second, gain_grad, rate_vector, 0.0)
    tap_new = adam_update(tap_weight, tap_first, tap_second, tap_grad, rate_vector, 0.0)
    matrices = [(part[1], part[2], part[0]) for part in new]
    return (outputs, input_grad, *sum(matrices, ()), *gain_new, *tap_new)


def solution(mesh):
    tokens = P("fsdp", "seq", None)
    rows = P(None, ("seq", "fsdp"), None)
    last = P(None, None, ("seq", "fsdp"))
    return jax.shard_map(
        local,
        mesh=mesh,
        in_specs=(tokens,) * 2 + (rows,) * 9 + (last,) * 6,
        out_specs=(tokens,) * 2 + (rows,) * 9 + (last,) * 6,
        check_vma=False,
    )
```
